32 devices in a mesh: dp: 8 (over z, x), tensor: 4 (over y, core).
Axes of the slice: x: 2, y: 2, z: 4, core: 2. Of those that a mesh axis runs over, the one named last changes fastest.
Arguments:
- tokens: bfloat16 [7584, 768], P('dp'), may hold values from -6 to 6
- token_mask: int32 [7584], P('dp'), may hold values from 0 to 1, as said below
- expert_type: int32 [7584], P('dp'), may hold values from 0 to 1, as said below
- cotangent: bfloat16 [7584, 768], P('dp'), may hold values from -6 to 6
- ln1_gain: float32 [768], replicated, may hold values from 0.5 to 1.5
- ln1_bias: float32 [768], replicated, may hold values from -0.6 to 0.6
- w_qkv: bfloat16 [768, 3, 768], P(None, None, 'tensor'), may hold values from -0.21875 to 0.21875
- qv_bias: float32 [2, 768], P(None, 'tensor'), may hold values from -0.6 to 0.6
- w_out: bfloat16 [768, 768], P('tensor'), may hold values from -1.75 to 1.75
- out_bias: float32 [768], replicated, may hold values from -0.6 to 0.6
- ln2_gain: float32 [768], replicated, may hold values from 0.5 to 1.5
- ln2_bias: float32 [768], replicated, may hold values from -0.6 to 0.6
- w_up: bfloat16 [2, 768, 3072], P(None, None, 'tensor'), may hold values from -0.21875 to 0.21875
- up_bias: float32 [2, 3072], P(None, 'tensor'), may hold values from -0.6 to 0.6
- w_down: bfloat16 [2, 3072, 768], P(None, 'tensor'), may hold values from -0.109375 to 0.109375
- down_bias: float32 [2, 768], replicated, may hold values from -0.6 to 0.6
Outputs:
- output: bfloat16 [7584, 768], P('dp')
- grad_tokens: bfloat16 [7584, 768], P('dp')
- grad_ln1_gain: float32 [768], replicated
- grad_ln1_bias: float32 [768], replicated
- grad_qkv: float32 [768, 3, 768], P(None, None, 'tensor')
- grad_qv_bias: float32 [2, 768], P(None, 'tensor')
- grad_out: float32 [768, 768], P('tensor')
- grad_out_bias: float32 [768], replicated
- grad_ln2_gain: float32 [768], replicated
- grad_ln2_bias: float32 [768], replicated
- grad_up: float32 [2, 768, 3072], P(None, None, 'tensor')
- grad_up_bias: float32 [2, 3072], P(None, 'tensor')
- grad_down: float32 [2, 3072, 768], P(None, 'tensor')
- grad_down_bias: float32 [2, 768], replicated
- counts: int32 [2], replicated
The draws below stay inside these ranges and needn't reach their ends.
Inputs may be any that keep to these rules, and one draw needn't show every extreme that they name: `token_mask`: in every item of 237 rows the first 197 rows are 1; the last 40 rows hold a leading run of 1 of 8 to 40 rows where the item's expert_type is 1, and are all 0 where it is 0; the last item has a run of 40. `expert_type`: the same on all 237 rows of an item; the first item is 0 and the last is 1.
All inputs are finite; a program needn't handle non-finite values.
Results may differ from the reference program's by a relative error of at most 0.013.
Values may be sent and summed in bfloat16 or wider, within the bound.
No kernel may reach another device: no remote copies, remote signals or barrier semaphores. Data moves between devices by JAX's collectives and lax.ppermute only.
A program may use at most 128 MiB of HBM per device.

```python
import jax
import jax.numpy as jnp
from jax import lax

D = 768
HEADS = 12
HEAD = 64
FF = 3072
PATCHES = 197
CAP = 40
CAP_MIN = 8
SEQ = 237
ITEMS = 32
ROWS = 7584


def item_layout(key):
    index = jnp.arange(ITEMS)
    first_key, second_key = jax.random.split(key)
    ticket = jax.random.randint(first_key, (ITEMS,), 0, 2 * ITEMS)
    paired = (ticket < ITEMS // 2 + index).astype(jnp.int32)
    paired = paired.at[0].set(0).at[ITEMS - 1].set(1)
    ceiling = CAP_MIN + (CAP - CAP_MIN) * (index + 1) // ITEMS
    length = jax.random.randint(second_key, (ITEMS,), CAP_MIN, ceiling + 1)
    length = length.at[ITEMS - 1].set(CAP)
    return (paired, length)


def draw_token_mask(key, part):
    paired, length = item_layout(key)
    position = jnp.arange(SEQ)[None, :]
    caption = position - PATCHES
    live = (position < PATCHES) | (paired[:, None] == 1) & (caption < length[:, None])
    return live.astype(jnp.int32).reshape(ITEMS * SEQ)


def draw_expert_type(key, part):
    paired, length = item_layout(key)
    return jnp.broadcast_to(paired[:, None], (ITEMS, SEQ)).reshape(ITEMS * SEQ).astype(jnp.int32)


def shard_levels(stream_key, dims, cuts, least, top_value):
    def one(axis_at, shards_of):
        draws = jax.random.uniform(jax.random.fold_in(jax.random.fold_in(stream_key, 6), axis_at), (shards_of,), jnp.float32, least / len(cuts), top_value / len(cuts))
        return jnp.repeat(jnp.exp(draws), dims[axis_at] // shards_of).reshape((-1,) + (1,) * (len(dims) - axis_at - 1))

    level = one(*cuts[0])
    for cut in cuts[1:]:
        level = level * one(*cut)
    return level


def gaussian(stream_key, shape, deviation, limit, cuts=(), kind=jnp.bfloat16):
    level = shard_levels(stream_key, shape, cuts, -0.22, 0.18) if cuts else 1.0
    array = jax.random.normal(stream_key, shape, jnp.float32) * deviation * level
    return jnp.minimum(jnp.maximum(array, -limit), limit).astype(kind)


def setup_inputs(seed: int = 0) -> dict:
    arg_keys = jax.random.split(jax.random.key(seed), 17)
    return {
        "tokens": gaussian(arg_keys[0], (ROWS, D), 1.0, 6.0, ((0, 8),)),
        "token_mask": draw_token_mask(jax.random.fold_in(arg_keys[16], 71), 0),
        "expert_type": draw_expert_type(jax.random.fold_in(arg_keys[16], 71), 0),
        "cotangent": gaussian(arg_keys[3], (ROWS, D), 1.0, 6.0, ((0, 8),)),
        "ln1_gain": jnp.clip(1.0 + 0.1 * jax.random.normal(arg_keys[4], (D,), jnp.float32), 0.5, 1.5),
        "ln1_bias": gaussian(arg_keys[5], (D,), 0.1, 0.6, (), jnp.float32),
        "w_qkv": gaussian(arg_keys[6], (D, 3, D), D ** -0.5, 0.21875, ((2, 4),)),
        "qv_bias": gaussian(arg_keys[7], (2, D), 0.1, 0.6, ((1, 4),), jnp.float32),
        "w_out": gaussian(arg_keys[8], (D, D), (D // 64) ** -0.5, 1.75, ((0, 4),)),
        "out_bias": gaussian(arg_keys[9], (D,), 0.1, 0.6, (), jnp.float32),
        "ln2_gain": jnp.clip(1.0 + 0.1 * jax.random.normal(arg_keys[10], (D,), jnp.float32), 0.5, 1.5),
        "ln2_bias": gaussian(arg_keys[11], (D,), 0.1, 0.6, (), jnp.float32),
        "w_up": gaussian(arg_keys[12], (2, D, FF), D ** -0.5, 0.21875, ((2, 4),)),
        "up_bias": gaussian(arg_keys[13], (2, FF), 0.1, 0.6, ((1, 4),), jnp.float32),
        "w_down": gaussian(arg_keys[14], (2, FF, D), FF ** -0.5, 0.109375, ((1, 4),)),
        "down_bias": gaussian(arg_keys[15], (2, D), 0.1, 0.6, (), jnp.float32),
    }


epsilon = 1e-05
highest = lax.Precision.HIGHEST

@jax.custom_vjp
def low(v):
    return lax.optimization_barrier(v.astype(jnp.bfloat16)).astype(jnp.float32)

@jax.custom_vjp
def low_back(v):
    return v

def low_keep(v):
    return (low(v), None)

def low_pass(kept, grad):
    return (grad,)

def back_keep(v):
    return (v, None)

def back_low(kept, grad):
    return (low(grad),)
low.defvjp(low_keep, low_pass)
low_back.defvjp(back_keep, back_low)

def normalize(field):
    mean_row = lax.optimization_barrier(jnp.mean(field, -1, keepdims=True))
    centered = field - mean_row
    return centered * lax.rsqrt(lax.optimization_barrier(jnp.mean(centered * centered, -1, keepdims=True)) + epsilon)

def attend(pieces):
    queries, key_rows, value_rows, key_mask = pieces
    scores = jnp.einsum('qhe,khe->hqk', queries, key_rows, precision=highest) * 0.125
    scores = low_back(jnp.where(key_mask[None, None, :], scores, -1e+30))
    attention = jax.nn.softmax(scores, axis=-1)
    return jnp.einsum('hqk,khe->qhe', low(attention), value_rows, precision=highest)

def forward(stream, ln1_gain, ln1_bias, w_qkv, qv_bias, w_out, out_bias, ln2_gain, ln2_bias, w_up, up_bias, w_down, down_bias, key_mask, expert_rows):
    normed = low(normalize(stream) * ln1_gain + ln1_bias)
    bias_three = jnp.stack([qv_bias[0], jnp.zeros_like(qv_bias[0]), qv_bias[1]])
    projected = jnp.einsum('rd,dje->rje', normed, w_qkv, precision=highest) + bias_three
    projected = low(low_back(projected)).reshape(ITEMS, SEQ, 3, HEADS, HEAD)
    context = lax.map(jax.checkpoint(attend), (projected[:, :, 0], projected[:, :, 1], projected[:, :, 2], key_mask))
    context = low(low_back(context.reshape(ITEMS * SEQ, D)))
    attn_branch = low_back(jnp.dot(context, w_out, precision=highest))
    middle = stream + attn_branch + out_bias
    normed_two = low(normalize(middle) * ln2_gain + ln2_bias)
    expert_sum = jnp.zeros_like(middle)
    for expert in range(2):
        hidden = low_back(jnp.dot(normed_two, w_up[expert], precision=highest) + up_bias[expert])
        activated = low(jax.nn.gelu(hidden, approximate=False))
        expert_sum = expert_sum + expert_rows[:, expert:expert + 1] * jnp.dot(activated, w_down[expert], precision=highest)
    return middle + low_back(expert_sum) + jnp.dot(expert_rows, down_bias, precision=highest)

def reference(tokens, token_mask, expert_type, cotangent, ln1_gain, ln1_bias, w_qkv, qv_bias, w_out, out_bias, ln2_gain, ln2_bias, w_up, up_bias, w_down, down_bias):
    language = expert_type == 1
    vision_count = jnp.sum(jnp.where(language, 0, token_mask))
    language_count = jnp.sum(jnp.where(language, token_mask, 0))
    counts = jnp.stack([vision_count, language_count]).astype(jnp.int32)
    count_float = counts.astype(jnp.float32)
    mask_float = token_mask.astype(jnp.float32)
    row_weight = mask_float * (count_float[0] + count_float[1]) / (2.0 * jnp.where(language, count_float[1], count_float[0]))
    expert_rows = (expert_type[:, None] == jnp.arange(2)[None, :]).astype(jnp.float32)
    key_mask = (token_mask > 0).reshape(ITEMS, SEQ)
    params = tuple((a.astype(jnp.float32) for a in (tokens, ln1_gain, ln1_bias, w_qkv, qv_bias, w_out, out_bias, ln2_gain, ln2_bias, w_up, up_bias, w_down, down_bias)))

    def closed(*values):
        return forward(*values, key_mask, expert_rows)
    output, pull = jax.vjp(closed, *params)
    grads = pull(cotangent.astype(jnp.float32) * row_weight[:, None])
    return (output.astype(jnp.bfloat16), grads[0].astype(jnp.bfloat16), grads[1], grads[2], grads[3], grads[4], grads[5], grads[6], grads[7], grads[8], grads[9], grads[10], grads[11], grads[12], counts)
```

```python
import functools

import jax
import jax.numpy as jnp
from jax import lax
from jax.experimental import pallas as pl
from jax.experimental.pallas import tpu as pltpu
from jax.sharding import PartitionSpec as P

HEAD = 64
PATCHES = 197
CAP = 40
SEQ = PATCHES + CAP
PAD = 240
ATT = 256

epsilon = 1e-05
f32 = jnp.float32
bf16 = jnp.bfloat16

NT = (((1,), (1,)), ((), ()))
NN = (((1,), (0,)), ((), ()))
TN = (((0,), (0,)), ((), ()))


def dot(a, b, dims=NN):
    return lax.dot_general(a, b, dims, preferred_element_type=f32)


def iota(shape, dim):
    return lax.broadcasted_iota(jnp.int32, shape, dim)


def unit_rows(x):
    mean = jnp.mean(x, -1, keepdims=True)
    centered = x - mean
    scale = lax.rsqrt(jnp.mean(centered * centered, -1, keepdims=True) + epsilon)
    return centered * scale, scale


def norm_back(grad, unit, scale, gain):
    t = grad * gain
    return scale * (
        t - jnp.mean(t, -1, keepdims=True) - unit * jnp.mean(t * unit, -1, keepdims=True)
    )


VMEM = pltpu.VMEM
SMEM = pltpu.SMEM


def vspec():
    return pl.BlockSpec(memory_space=VMEM)


def sspec():
    return pl.BlockSpec(memory_space=SMEM)


def aspec():
    return pl.BlockSpec(memory_space=pl.ANY)


def call(kernel, ins, specs, outs, scratch=(), limit=40, flops=0, name=None):
    size = sum(a.size * a.dtype.itemsize for a in ins)
    size += sum(o.size * o.dtype.itemsize for o in outs)
    return pl.pallas_call(
        kernel,
        out_shape=list(outs),
        in_specs=list(specs),
        out_specs=[vspec() for _ in outs],
        scratch_shapes=list(scratch),
        compiler_params=pltpu.CompilerParams(vmem_limit_bytes=limit * 1024 * 1024),
        cost_estimate=pl.CostEstimate(
            flops=int(flops), bytes_accessed=int(size), transcendentals=0
        ),
        name=name,
    )(*ins)


def arr(shape, dtype):
    return jax.ShapeDtypeStruct(shape, dtype)


def stage_rows(ref, buf, chunk):
    low = 2 * chunk * SEQ
    high = low + 2 * SEQ
    base = low // 16 * 16
    top = min(ref.shape[0], -(-high // 16) * 16)
    buf[0 : top - base] = ref[...][base:top].astype(f32)
    return [low - base, low - base + SEQ]


def item_rows(buf, offset, count):
    rows = buf[pl.ds(offset, count), :]
    return jnp.where(iota(rows.shape, 0) < SEQ, rows, 0.0)


STAGE = 2 * SEQ + 32


def attention_forward(chunk, items, heads, meta, tokens, w_t, b_three, gain, bias, ctx, proj, normed, buf):
    width = heads * HEAD
    offsets = stage_rows(tokens, buf, chunk)
    for j in range(2):
        live = meta[1 + 2 * chunk + j]
        x = item_rows(buf, offsets[j], ATT)
        unit, _ = unit_rows(x)
        n_row = (unit * gain[...] + bias[...]).astype(bf16)
        normed[j] = n_row[:PAD]
        p_row = (dot(n_row, w_t[...], NT) + b_three[...]).astype(bf16)
        proj[j] = p_row[:PAD]
        key_live = iota((ATT, ATT), 1) < live
        for h in range(heads):
            q = p_row[:, h * HEAD : (h + 1) * HEAD]
            k = p_row[:, width + h * HEAD : width + (h + 1) * HEAD]
            v = p_row[:, 2 * width + h * HEAD : 2 * width + (h + 1) * HEAD]
            s = jnp.where(key_live, dot(q, k, NT) * 0.125, -1e30)
            e = jnp.exp(s - jnp.max(s, -1, keepdims=True))
            att = (e * (1.0 / jnp.sum(e, -1, keepdims=True))).astype(bf16)
            c = dot(att, v).astype(bf16)
            at = j * width + h * HEAD
            ctx[:, at : at + HEAD] = c[:PAD]


def run_attention_forward(chunk, items, heads, meta, tokens, w_t, b_three, gain, bias):
    width = heads * HEAD
    d = tokens.shape[1]
    return call(
        functools.partial(attention_forward, chunk, items, heads),
        (meta, tokens, w_t, b_three, gain, bias),
        [sspec()] + [vspec()] * 5,
        [arr((PAD, 2 * width), bf16), arr((2, PAD, 3 * width), bf16), arr((2, PAD, d), bf16)],
        [VMEM((STAGE, d), f32)],
        flops=2 * 2 * ATT * (d * 3 * width + 4 * ATT * width),
        name="attention_forward_%d" % chunk,
    )


def gelu_parts(h):
    cdf = 0.5 * (1.0 + lax.erf(h * 0.7071067811865476))
    density = jnp.exp(-0.5 * h * h) * 0.3989422804014327
    return h * cdf, cdf + h * density


def experts(
    chunk, items, heads, meta, weight, tokens, cot, c0, c1, c2, c3, o0, o1, o2, o3, out_bias, gain, bias,
    up_bias, w_up_any, w_down_any,
    middle, own_grad, normed, active, ghid, gout, down_own, down_other, part_own, part_other, small,
    buf, cbuf, ctx, w_out, w_up, w_down, sems,
):
    width = heads * HEAD
    copy_up = pltpu.make_async_copy(w_up_any, w_up, sems.at[0])
    copy_down = pltpu.make_async_copy(w_down_any, w_down, sems.at[1])
    copy_up.start()
    copy_down.start()
    t = meta[0]
    core = lax.rem(t, 2)
    first = core == 0
    for step, (c, o) in enumerate(((c0, o0), (c1, o1), (c2, o2), (c3, o3))):
        if step == 0:
            slot = t
        elif step == 1:
            slot = t + 1 - 2 * core
        elif step == 2:
            slot = lax.rem(t + 2, 4)
        else:
            slot = lax.rem(t + 3 - 2 * core, 4)
        ctx[slot] = c[...]
        w_out[slot] = o[...]
    offsets = stage_rows(tokens, buf, chunk)
    cot_offsets = stage_rows(cot, cbuf, chunk)
    mids, grads, n_rows = [], [], []
    for j in range(2):
        x = item_rows(buf, offsets[j], PAD)
        total = jnp.zeros((PAD, x.shape[1]), f32)
        for s in range(4):
            total = total + dot(ctx[s][:, j * width : (j + 1) * width], w_out[s])
        mid = x + total + out_bias[...]
        mids.append(mid)
        unit, _ = unit_rows(mid)
        n_row = (unit * gain[...] + bias[...]).astype(bf16)
        normed[j] = n_row
        n_rows.append(n_row)
        raw = item_rows(cbuf, cot_offsets[j], PAD)
        live = iota(raw.shape, 0) < meta[1 + 2 * chunk + j]
        grad = jnp.where(live, raw, 0.0) * weight[2 * chunk + j]
        grads.append(grad)
        gout[j] = grad.astype(bf16)
    middle[...] = jnp.where(first, mids[0], mids[1])
    own_grad[...] = jnp.where(first, grads[0], grads[1])
    small[...] = jnp.zeros_like(small)
    copy_up.wait()
    copy_down.wait()
    parts, downs = [], []
    for j in range(2):
        e = meta[1 + items + 2 * chunk + j]
        wu = w_up[e]
        wd = w_down[e]
        h = dot(n_rows[j], wu) + up_bias[e]
        value, slope = gelu_parts(h)
        act = value.astype(bf16)
        active[j] = act
        gh = (dot(gout[j], wd, NT) * slope).astype(bf16)
        ghid[j] = gh
        part = dot(gh, wu, NT)
        parts.append(part)
        downs.append(dot(act, wd))
        small[pl.ds(e, 1), :] += jnp.sum(gh.astype(f32), 0, keepdims=True)
        small[pl.ds(e + 2, 1), :] += jnp.sum(grads[j], 0, keepdims=True)
    part_own[...] = jnp.where(first, parts[0], parts[1]).astype(bf16)
    part_other[...] = jnp.where(first, parts[1], parts[0]).astype(bf16)
    down_own[...] = jnp.where(first, downs[0], downs[1]).astype(bf16)
    down_other[...] = jnp.where(first, downs[1], downs[0]).astype(bf16)


def run_experts(chunk, items, heads, meta, weight, tokens, cot, ctxs, outs, out_bias, gain, bias, up_bias, w_up, w_down):
    width = heads * HEAD
    d = tokens.shape[1]
    ff = w_up.shape[2]
    row = arr((PAD, d), bf16)
    return call(
        functools.partial(experts, chunk, items, heads),
        (meta, weight, tokens, cot, *ctxs, *outs, out_bias, gain, bias, up_bias, w_up, w_down),
        [sspec()] * 2 + [vspec()] * 14 + [aspec()] * 2,
        [
            arr((PAD, d), f32),
            arr((PAD, d), f32),
            arr((2, PAD, d), bf16),
            arr((2, PAD, ff), bf16),
            arr((2, PAD, ff), bf16),
            arr((2, PAD, d), bf16),
            row,
            row,
            row,
            row,
            arr((8, d), f32),
        ],
        [
            VMEM((STAGE, d), f32),
            VMEM((STAGE, d), f32),
            VMEM((4, PAD, 2 * width), bf16),
            VMEM((4, width, d), bf16),
            VMEM(w_up.shape, bf16),
            VMEM(w_down.shape, bf16),
            pltpu.SemaphoreType.DMA((2,)),
        ],
        flops=2 * 2 * PAD * d * (4 * width + 4 * ff),
        limit=48,
        name="experts_%d" % chunk,
    )


def expert_grads(items, meta, *refs):
    lefts, rights = refs[: items // 2], refs[items // 2 : items]
    out, total = refs[items], refs[items + 1]
    total[...] = jnp.zeros_like(total)
    for i in range(items):
        e = meta[1 + items + i]
        total[e] += dot(lefts[i // 2][i % 2], rights[i // 2][i % 2], TN)
    out[...] = total[...].astype(bf16)


def run_expert_grads(items, meta, lefts, rights, name):
    shape = (2, lefts[0].shape[2], rights[0].shape[2])
    return call(
        functools.partial(expert_grads, items),
        (meta, *lefts, *rights),
        [sspec()] + [vspec()] * items,
        [arr(shape, bf16)],
        [VMEM(shape, f32)],
        flops=2 * items * PAD * shape[1] * shape[2],
        name=name,
    )[0]


def norm_two_back(middle, own_grad, pair, far, gain, grad_mid, branch, small):
    unit, scale = unit_rows(middle[...])
    grad = pair[...].astype(f32) + far[...].astype(f32)
    out = own_grad[...] + norm_back(grad, unit, scale, gain[...])
    grad_mid[...] = out
    branch[...] = out.astype(bf16)
    small[...] = jnp.zeros_like(small)
    small[0:1, :] = jnp.sum(grad * unit, 0, keepdims=True)
    small[1:2, :] = jnp.sum(grad, 0, keepdims=True)
    small[2:3, :] = jnp.sum(out, 0, keepdims=True)


def run_norm_two_back(chunk, middle, own_grad, pair, far, gain):
    shape = middle.shape
    return call(
        norm_two_back,
        (middle, own_grad, pair, far, gain),
        [vspec()] * 5,
        [arr(shape, f32), arr(shape, bf16), arr((8, shape[1]), f32)],
        flops=20 * middle.size,
        name="norm_two_back_%d" % chunk,
    )


def attention_backward(chunk, items, heads, meta, own, other, w_out, proj, w_t, gproj, part_own, part_other, small):
    width = heads * HEAD
    first = lax.rem(meta[0], 2) == 0
    parts = []
    small[...] = jnp.zeros_like(small)
    for j in range(2):
        live = meta[1 + 2 * chunk + j]
        a, b = (own, other) if j == 0 else (other, own)
        branch = jnp.where(first, a[...], b[...])
        gctx = dot(branch, w_out[...], NT).astype(bf16)
        p_row = proj[j]
        key_live = iota((PAD, PAD), 1) < live
        gq, gk, gv = [], [], []
        for h in range(heads):
            q = p_row[:, h * HEAD : (h + 1) * HEAD]
            k = p_row[:, width + h * HEAD : width + (h + 1) * HEAD]
            v = p_row[:, 2 * width + h * HEAD : 2 * width + (h + 1) * HEAD]
            gc = gctx[:, h * HEAD : (h + 1) * HEAD]
            s = jnp.where(key_live, dot(q, k, NT) * 0.125, -1e30)
            e = jnp.exp(s - jnp.max(s, -1, keepdims=True))
            att = e * (1.0 / jnp.sum(e, -1, keepdims=True))
            ga = dot(gc, v, NT)
            gs = (att * (ga - jnp.sum(ga * att, -1, keepdims=True))).astype(bf16)
            gv.append(dot(att.astype(bf16), gc, TN))
            gq.append(dot(gs, k) * 0.125)
            gk.append(dot(gs, q, TN) * 0.125)
        gp = jnp.concatenate(gq + gk + gv, axis=1).astype(bf16)
        gproj[j] = gp
        small[0:1, :] += jnp.sum(gp.astype(f32), 0, keepdims=True)
        parts.append(dot(gp, w_t[...]))
    part_own[...] = jnp.where(first, parts[0], parts[1]).astype(bf16)
    part_other[...] = jnp.where(first, parts[1], parts[0]).astype(bf16)


def run_attention_backward(chunk, items, heads, meta, own, other, w_out, proj, w_t):
    width = heads * HEAD
    d = own.shape[1]
    return call(
        functools.partial(attention_backward, chunk, items, heads),
        (meta, own, other, w_out, proj, w_t),
        [sspec()] + [vspec()] * 5,
        [arr((2, PAD, 3 * width), bf16), arr((PAD, d), bf16), arr((PAD, d), bf16), arr((8, 3 * width), f32)],
        flops=2 * 2 * PAD * (d * 4 * width + 5 * PAD * width),
        name="attention_backward_%d" % chunk,
    )


def attention_grads(items, heads, meta, *refs):
    width = heads * HEAD
    chunks = items // 2
    gproj, normed, ctx = refs[:chunks], refs[chunks : 2 * chunks], refs[2 * chunks : 3 * chunks]
    own, other = refs[3 * chunks : 4 * chunks], refs[4 * chunks : 5 * chunks]
    out = refs[5 * chunks]
    first = lax.rem(meta[0], 2) == 0
    rows = 3 * width
    total = jnp.zeros((rows, out.shape[1]), f32)
    total_out = jnp.zeros((width, out.shape[1]), f32)
    for k in range(chunks):
        for j in range(2):
            total = total + dot(gproj[k][j], normed[k][j], TN)
            a, b = (own[k], other[k]) if j == 0 else (other[k], own[k])
            branch = jnp.where(first, a[...], b[...])
            total_out = total_out + dot(ctx[k][:, j * width : (j + 1) * width], branch, TN)
    out[0:rows, :] = total.astype(bf16)
    out[rows:, :] = total_out.astype(bf16)


def run_attention_grads(items, heads, meta, gproj, normed, ctx, own, other):
    width = heads * HEAD
    d = own[0].shape[1]
    return call(
        functools.partial(attention_grads, items, heads),
        (meta, *gproj, *normed, *ctx, *own, *other),
        [sspec()] + [vspec()] * (5 * items // 2),
        [arr((4 * width, d), bf16)],
        flops=2 * items * PAD * d * 4 * width,
        name="attention_grads",
    )[0]


def norm_one_back(chunk, meta, tokens, grad_mid, pair, far, gain, grad_own, small, buf):
    first = lax.rem(meta[0], 2) == 0
    offsets = stage_rows(tokens, buf, chunk)
    x = jnp.where(first, item_rows(buf, offsets[0], PAD), item_rows(buf, offsets[1], PAD))
    unit, scale = unit_rows(x)
    grad = pair[...].astype(f32) + far[...].astype(f32)
    grad_own[...] = (grad_mid[...] + norm_back(grad, unit, scale, gain[...])).astype(bf16)
    small[...] = jnp.zeros_like(small)
    small[0:1, :] = jnp.sum(grad * unit, 0, keepdims=True)
    small[1:2, :] = jnp.sum(grad, 0, keepdims=True)


def run_norm_one_back(chunk, meta, tokens, grad_mid, pair, far, gain):
    shape = grad_mid.shape
    return call(
        functools.partial(norm_one_back, chunk),
        (meta, tokens, grad_mid, pair, far, gain),
        [sspec()] + [vspec()] * 5,
        [arr(shape, bf16), arr((8, shape[1]), f32)],
        [VMEM((STAGE, shape[1]), f32)],
        flops=20 * grad_mid.size,
        name="norm_one_back_%d" % chunk,
    )


def output_rows(chunk, items, meta, middle, pair, far, down_bias, out):
    e0 = meta[1 + items + 2 * chunk]
    e1 = meta[1 + items + 2 * chunk + 1]
    e = jnp.where(lax.rem(meta[0], 2) == 0, e0, e1)
    out[...] = (middle[...] + pair[...].astype(f32) + far[...].astype(f32) + down_bias[e]).astype(bf16)


def run_output_rows(chunk, items, meta, middle, pair, far, down_bias):
    return call(
        functools.partial(output_rows, chunk, items),
        (meta, middle, pair, far, down_bias),
        [sspec()] + [vspec()] * 4,
        [arr(middle.shape, bf16)],
        flops=4 * middle.size,
        name="output_rows_%d" % chunk,
    )[0]


def assemble(items, meta, *refs):
    chunks = items // 2
    own, other, out, buf = refs[:chunks], refs[chunks : 2 * chunks], refs[2 * chunks], refs[2 * chunks + 1]
    first = lax.rem(meta[0], 2) == 0
    for k in range(chunks):
        for j in range(2):
            a, b = (own[k], other[k]) if j == 0 else (other[k], own[k])
            rows = jnp.where(first, a[...], b[...]).astype(f32)
            buf[pl.ds((2 * k + j) * SEQ, PAD), :] = rows
    out[...] = buf[0 : items * SEQ, :].astype(bf16)


def run_assemble(items, meta, own, other, name):
    d = own[0].shape[1]
    return call(
        functools.partial(assemble, items),
        (meta, *own, *other),
        [sspec()] + [vspec()] * items,
        [arr((items * SEQ, d), bf16)],
        [VMEM((items * SEQ + 16, d), f32)],
        name=name,
    )[0]


def swap(value, axis, size, bit):
    return lax.ppermute(value, axis, [(i, i ^ bit) for i in range(size)])


def sum_over(value, axis, size):
    bit = 1
    while bit < size:
        value = value + swap(value, axis, size, bit)
        bit = 2 * bit
    return value


def sum_over_items(piece, dp):
    flat = piece.reshape(-1, piece.shape[-1])
    share = lax.psum_scatter(flat, "dp", scatter_dimension=0, tiled=True)
    return lax.all_gather(share, "dp", axis=0, tiled=True).reshape(piece.shape).astype(f32)


def local(
    dp, tp,
    tokens, token_mask, expert_type, cotangent, ln1_gain, ln1_bias, w_qkv, qv_bias, w_out, out_bias,
    ln2_gain, ln2_bias, w_up, up_bias, w_down, down_bias,
):
    rows, d = tokens.shape
    items = rows // SEQ
    width = w_qkv.shape[2]
    heads = width // HEAD
    t = lax.axis_index("tensor").astype(jnp.int32)
    core_swap = lambda v: swap(v, "tensor", tp, 1)
    far_swap = lambda v: swap(v, "tensor", tp, 2)

    lives = jnp.sum(token_mask.reshape(items, SEQ), 1)
    kinds = expert_type.reshape(items, SEQ)[:, 0]
    meta = jnp.concatenate([t[None], lives, kinds, jnp.zeros((15 - 2 * items,), jnp.int32)])
    ones = jnp.sum(jnp.where(kinds == 1, lives, 0))
    local_counts = jnp.stack([jnp.sum(lives) - ones, ones]).astype(f32)

    w_t = w_qkv.transpose(1, 2, 0).reshape(3 * width, d)
    b_three = jnp.concatenate([qv_bias[0], jnp.zeros_like(qv_bias[0]), qv_bias[1]])[None]
    row = lambda v: v.reshape(1, -1)
    up_bias3 = up_bias[:, None, :]
    down_bias3 = down_bias[:, None, :]

    o0 = w_out
    o2 = far_swap(o0)
    o1 = core_swap(o0)
    o3 = core_swap(o2)
    outs = (o0, o1, o2, o3)

    chunks = range(items // 2)
    ctx, proj, normed_one, ctxs = [], [], [], []
    for k in chunks:
        c0, p, n = run_attention_forward(k, items, heads, meta, tokens, w_t, b_three, row(ln1_gain), row(ln1_bias))
        ctx.append(c0)
        proj.append(p)
        normed_one.append(n)
        c2 = far_swap(c0)
        c1 = core_swap(c0)
        c3 = core_swap(c2)
        ctxs.append((c0, c1, c2, c3))

    totals = sum_over(local_counts, "dp", dp)
    weight = (totals[0] + totals[1]) / (2.0 * jnp.where(kinds == 1, totals[1], totals[0]))

    exp = [
        run_experts(
            k, items, heads, meta, weight, tokens, cotangent, ctxs[k], outs, row(out_bias), row(ln2_gain),
            row(ln2_bias), up_bias3, w_up, w_down,
        )
        for k in chunks
    ]
    middle, own_grad, normed_two, active, ghid, gout, down_own, down_other, part_own, part_other, small_e = zip(*exp)

    grad_down_part = run_expert_grads(items, meta, active, gout, "down_grads")
    grad_up_part = run_expert_grads(items, meta, normed_two, ghid, "up_grads")

    def pair_sum(own, other):
        return (own.astype(f32) + core_swap(other).astype(f32)).astype(bf16)

    grad_mid, branch_own, branch_other, small_n = [], [], [], []
    for k in chunks:
        pair = pair_sum(part_own[k], part_other[k])
        g, b, s = run_norm_two_back(k, middle[k], own_grad[k], pair, far_swap(pair), row(ln2_gain))
        grad_mid.append(g)
        branch_own.append(b)
        branch_other.append(core_swap(b))
        small_n.append(s)

    gproj, small_a, one_own, one_other = [], [], [], []
    for k in chunks:
        g, po, pt, s = run_attention_backward(k, items, heads, meta, branch_own[k], branch_other[k], w_out, proj[k], w_t)
        gproj.append(g)
        one_own.append(po)
        one_other.append(pt)
        small_a.append(s)
    grad_attn_part = run_attention_grads(items, heads, meta, gproj, normed_one, ctx, branch_own, branch_other)

    grad_own, small_o = [], []
    for k in chunks:
        pair = pair_sum(one_own[k], one_other[k])
        g, s = run_norm_one_back(k, meta, tokens, grad_mid[k], pair, far_swap(pair), row(ln1_gain))
        grad_own.append(g)
        small_o.append(s)
    grad_tokens = run_assemble(items, meta, grad_own, [core_swap(g) for g in grad_own], "grad_tokens")

    out_own = []
    for k in chunks:
        pair = pair_sum(down_own[k], down_other[k])
        out_own.append(run_output_rows(k, items, meta, middle[k], pair, far_swap(pair), down_bias3))
    output = run_assemble(items, meta, out_own, [core_swap(o) for o in out_own], "output")

    grad_down = sum_over_items(grad_down_part, dp)
    grad_up = sum_over_items(grad_up_part, dp)
    grad_attn = sum_over_items(grad_attn_part, dp)

    norms = jnp.concatenate([sum(small_n)[:3], sum(small_o)[:2], jnp.zeros((3, d), f32)])
    norms = norms + core_swap(norms)
    projected = jnp.pad(sum(small_a)[:1], ((0, 0), (0, d - 3 * width)))
    small = jnp.concatenate([norms, sum(small_e)[:4], projected, jnp.zeros((3, d), f32)])
    small = sum_over(small, "dp", dp)

    grad_qkv = grad_attn[: 3 * width].reshape(3, width, d).transpose(2, 0, 1)
    grad_out = grad_attn[3 * width :]
    grad_qv_bias = jnp.stack([small[12, :width], small[12, 2 * width : 3 * width]])
    return (
        output,
        grad_tokens,
        small[3],
        small[4],
        grad_qkv,
        grad_qv_bias,
        grad_out,
        small[2],
        small[0],
        small[1],
        grad_up,
        small[8:10],
        grad_down,
        small[10:12],
        totals.astype(jnp.int32),
    )


def solution(mesh):
    in_specs = (
        P("dp", None),
        P("dp"),
        P("dp"),
        P("dp", None),
        P(),
        P(),
        P(None, None, "tensor"),
        P(None, "tensor"),
        P("tensor", None),
        P(),
        P(),
        P(),
        P(None, None, "tensor"),
        P(None, "tensor"),
        P(None, "tensor", None),
        P(),
    )
    out_specs = (
        P("dp", None),
        P("dp", None),
        P(),
        P(),
        P(None, None, "tensor"),
        P(None, "tensor"),
        P("tensor", None),
        P(),
        P(),
        P(),
        P(None, None, "tensor"),
        P(None, "tensor"),
        P(None, "tensor", None),
        P(),
        P(),
    )
    return jax.shard_map(
        functools.partial(local, mesh.shape["dp"], mesh.shape["tensor"]),
        mesh=mesh,
        in_specs=in_specs,
        out_specs=out_specs,
        check_vma=False,
    )
```

```python
import functools

import jax
import jax.numpy as jnp
from jax import lax
from jax.experimental import pallas as pl
from jax.experimental.pallas import tpu as pltpu
from jax.sharding import PartitionSpec as P

HEAD = 64
PATCHES = 197
CAP = 40
SEQ = PATCHES + CAP
PAD = 240
ATT = 256
STAGE = 2 * SEQ + 32

epsilon = 1e-05
f32 = jnp.float32
bf16 = jnp.bfloat16

NT = (((1,), (1,)), ((), ()))
NN = (((1,), (0,)), ((), ()))
TN = (((0,), (0,)), ((), ()))

VMEM = pltpu.VMEM
SMEM = pltpu.SMEM


def dot(a, b, dims=NN):
    return lax.dot_general(a, b, dims, preferred_element_type=f32)


def iota(shape, dim):
    return lax.broadcasted_iota(jnp.int32, shape, dim)


def unit_rows(x):
    mean = jnp.mean(x, -1, keepdims=True)
    centered = x - mean
    scale = lax.rsqrt(jnp.mean(centered * centered, -1, keepdims=True) + epsilon)
    return centered * scale, scale


def norm_back(grad, unit, scale, gain):
    t = grad * gain
    return scale * (
        t - jnp.mean(t, -1, keepdims=True) - unit * jnp.mean(t * unit, -1, keepdims=True)
    )


def line(ref):
    return ref[...].reshape(1, -1)


def vspec():
    return pl.BlockSpec(memory_space=VMEM)


def sspec():
    return pl.BlockSpec(memory_space=SMEM)


def aspec():
    return pl.BlockSpec(memory_space=pl.ANY)


class Order:
    def __init__(self):
        self.last = None

    def __call__(self, kernel, ins, specs, outs, scratch=(), limit=16, flops=0, name=None):
        size = sum(a.size * a.dtype.itemsize for a in ins)
        size += sum(o.size * o.dtype.itemsize for o in outs)
        taken = len(ins)
        behind = () if self.last is None or any(a is self.last for a in ins) else (self.last,)

        def body(*refs):
            kernel(*refs[:taken], *refs[taken + len(behind) :])

        results = pl.pallas_call(
            body,
            out_shape=list(outs),
            in_specs=list(specs) + [aspec() for _ in behind],
            out_specs=[vspec() for _ in outs],
            scratch_shapes=list(scratch),
            compiler_params=pltpu.CompilerParams(vmem_limit_bytes=limit * 1024 * 1024),
            cost_estimate=pl.CostEstimate(
                flops=int(flops), bytes_accessed=int(size), transcendentals=0
            ),
            name=name,
        )(*ins, *behind)
        self.last = results[0]
        return results


def arr(shape, dtype):
    return jax.ShapeDtypeStruct(shape, dtype)


def position():
    return lax.axis_index("tensor")


def is_first():
    return lax.rem(position(), 2) == 0


def places():
    place = lax.axis_index("dp")
    low = lax.rem(place, 2)
    high = lax.rem(lax.div(place, 2), 2)
    first = is_first()
    return jnp.where(first, low, high), jnp.where(first, high, low)


def live_rows(mask, item):
    count = PATCHES
    for slot in range(CAP):
        count = count + mask[item * SEQ + PATCHES + slot]
    return count


def expert_of(kind, item):
    return kind[item * SEQ]


def stage_rows(ref, buf, chunk):
    low = 2 * chunk * SEQ
    high = low + 2 * SEQ
    base = low // 16 * 16
    top = min(ref.shape[0], -(-high // 16) * 16)
    buf[0 : top - base] = ref[...][base:top].astype(f32)
    return [low - base, low - base + SEQ]


def item_rows(buf, offset, count, live=SEQ):
    rows = buf[pl.ds(offset, count), :]
    return jnp.where(iota(rows.shape, 0) < live, rows, 0.0)


def count_rows(items, mask, kind, out):
    total = 0
    second = 0
    for i in range(items):
        n = live_rows(mask, i)
        total = total + n
        second = second + n * expert_of(kind, i)
    row = iota(out.shape, 0)
    out[...] = jnp.where(row == 0, total - second, second).astype(f32)


def run_count_rows(call, items, mask, kind):
    return call(
        functools.partial(count_rows, items), (mask, kind), [sspec()] * 2, [arr((8, 128), f32)], limit=4, name="count"
    )[0]


def row_weight(counts):
    both = counts[0:1, 0:1] + counts[1:2, 0:1]
    return both / (2.0 * counts[0:1, 0:1]), both / (2.0 * counts[1:2, 0:1])


def attention_forward(chunk, heads, mask, tokens, w_t, qv_bias, gain, bias, ctx, proj, normed, buf):
    width = heads * HEAD
    offsets = stage_rows(tokens, buf, chunk)
    b_three = jnp.concatenate([qv_bias[0:1, :], jnp.zeros((1, width), f32), qv_bias[1:2, :]], axis=1)
    for j in range(2):
        live = live_rows(mask, 2 * chunk + j)
        x = item_rows(buf, offsets[j], ATT)
        unit, _ = unit_rows(x)
        n_row = (unit * line(gain) + line(bias)).astype(bf16)
        normed[j] = n_row[:PAD]
        p_row = (dot(n_row, w_t[...], NT) + b_three).astype(bf16)
        proj[j] = p_row[:PAD]
        key_live = iota((ATT, ATT), 1) < live
        for h in range(heads):
            q = p_row[:, h * HEAD : (h + 1) * HEAD]
            k = p_row[:, width + h * HEAD : width + (h + 1) * HEAD]
            v = p_row[:, 2 * width + h * HEAD : 2 * width + (h + 1) * HEAD]
            s = jnp.where(key_live, dot(q, k, NT) * 0.125, -1e30)
            e = jnp.exp(s - jnp.max(s, -1, keepdims=True))
            att = (e * (1.0 / jnp.sum(e, -1, keepdims=True))).astype(bf16)
            c = dot(att, v).astype(bf16)
            at = j * width + h * HEAD
            ctx[:, at : at + HEAD] = c[:PAD]


def run_attention_forward(call, chunk, heads, mask, tokens, w_t, qv_bias, gain, bias):
    width = heads * HEAD
    d = tokens.shape[1]
    return call(
        functools.partial(attention_forward, chunk, heads),
        (mask, tokens, w_t, qv_bias, gain, bias),
        [sspec()] + [vspec()] * 5,
        [arr((PAD, 2 * width), bf16), arr((2, PAD, 3 * width), bf16), arr((2, PAD, d), bf16)],
        [VMEM((STAGE, d), f32)],
        flops=2 * 2 * ATT * (d * 3 * width + 4 * ATT * width),
        name="attention_forward_%d" % chunk,
    )


def gelu_parts(h):
    cdf = 0.5 * (1.0 + lax.erf(h * 0.7071067811865476))
    density = jnp.exp(-0.5 * h * h) * 0.3989422804014327
    return h * cdf, cdf + h * density


def experts(
    chunk, heads, mask, kind, tokens, cot, c0, c1, c2, c3, o0, o1, o2, o3, out_bias, gain, bias,
    up_bias, w_up, w_down,
    middle, masked, normed, active, ghid, down_own, down_other, part_own, part_other, small,
    buf, cbuf, ctx, w_out,
):
    width = heads * HEAD
    d = tokens.shape[1]
    t = position()
    core = lax.rem(t, 2)
    first = core == 0
    slots = (t, t + 1 - 2 * core, lax.rem(t + 2, 4), lax.rem(t + 3 - 2 * core, 4))
    for slot, c, o in zip(slots, (c0, c1, c2, c3), (o0, o1, o2, o3)):
        ctx[slot] = c[...]
        w_out[slot] = o[...]
    offsets = stage_rows(tokens, buf, chunk)
    cot_offsets = stage_rows(cot, cbuf, chunk)
    mids, cots, n_rows = [], [], []
    for j in range(2):
        x = item_rows(buf, offsets[j], PAD)
        total = jnp.zeros((PAD, d), f32)
        for s in range(4):
            total = total + dot(ctx[s][:, j * width : (j + 1) * width], w_out[s])
        mid = x + total + line(out_bias)
        mids.append(mid)
        unit, _ = unit_rows(mid)
        n_row = (unit * line(gain) + line(bias)).astype(bf16)
        normed[j] = n_row
        n_rows.append(n_row)
        c_row = item_rows(cbuf, cot_offsets[j], PAD, live_rows(mask, 2 * chunk + j)).astype(bf16)
        masked[j] = c_row
        cots.append(c_row)
    middle[...] = jnp.where(first, mids[0], mids[1])
    small[...] = jnp.zeros_like(small)
    parts, downs = [], []
    for j in range(2):
        e = expert_of(kind, 2 * chunk + j)
        wu = w_up[e]
        wd = w_down[e]
        h = dot(n_rows[j], wu) + up_bias[pl.ds(e, 1), :]
        value, slope = gelu_parts(h)
        act = value.astype(bf16)
        active[j] = act
        gh = (dot(cots[j], wd, NT) * slope).astype(bf16)
        ghid[j] = gh
        parts.append(dot(gh, wu, NT))
        downs.append(dot(act, wd))
        small[pl.ds(e, 1), :] += jnp.sum(gh.astype(f32), 0, keepdims=True)
        small[pl.ds(e + 2, 1), :] += jnp.sum(cots[j].astype(f32), 0, keepdims=True)
    part_own[...] = jnp.where(first, parts[0], parts[1]).astype(bf16)
    part_other[...] = jnp.where(first, parts[1], parts[0]).astype(bf16)
    down_own[...] = jnp.where(first, downs[0], downs[1]).astype(bf16)
    down_other[...] = jnp.where(first, downs[1], downs[0]).astype(bf16)


def run_experts(
    call, chunk, heads, mask, kind, tokens, cot, ctxs, outs, out_bias, gain, bias, up_bias, w_up, w_down
):
    width = heads * HEAD
    d = tokens.shape[1]
    ff = w_up.shape[2]
    row = arr((PAD, d), bf16)
    return call(
        functools.partial(experts, chunk, heads),
        (mask, kind, tokens, cot, *ctxs, *outs, out_bias, gain, bias, up_bias, w_up, w_down),
        [sspec()] * 2 + [vspec()] * 16,
        [
            arr((PAD, d), f32),
            arr((2, PAD, d), bf16),
            arr((2, PAD, d), bf16),
            arr((2, PAD, ff), bf16),
            arr((2, PAD, ff), bf16),
            row,
            row,
            row,
            row,
            arr((8, d), f32),
        ],
        [
            VMEM((STAGE, d), f32),
            VMEM((STAGE, d), f32),
            VMEM((4, PAD, 2 * width), bf16),
            VMEM((4, width, d), bf16),
        ],
        flops=2 * 2 * PAD * d * (4 * width + 4 * ff),
        limit=24,
        name="experts_%d" % chunk,
    )


def expert_grads(items, kind, counts, *refs):
    chunks = items // 2
    lefts, rights = refs[:chunks], refs[chunks : 2 * chunks]
    send, keep, total = refs[2 * chunks :]
    for i in range(items):
        e = expert_of(kind, i)
        term = dot(lefts[i // 2][i % 2], rights[i // 2][i % 2], TN)
        if i == 0:
            total[e] = term
            total[1 - e] = jnp.zeros_like(term)
        else:
            total[e] += term
    first, second = row_weight(counts)
    one, _ = places()
    keep[...] = (total[one] * jnp.where(one == 0, first, second)).astype(bf16)
    send[...] = (total[1 - one] * jnp.where(one == 0, second, first)).astype(bf16)


def run_expert_grads(call, items, kind, counts, lefts, rights, name):
    shape = (lefts[0].shape[2], rights[0].shape[2])
    return call(
        functools.partial(expert_grads, items),
        (kind, counts, *lefts, *rights),
        [sspec()] + [vspec()] * (1 + items),
        [arr(shape, bf16)] * 2,
        [VMEM((2, *shape), f32)],
        flops=2 * items * PAD * shape[0] * shape[1],
        name=name,
    )


def own_weight(chunk, kind, counts):
    e = jnp.where(is_first(), expert_of(kind, 2 * chunk), expert_of(kind, 2 * chunk + 1))
    first, second = row_weight(counts)
    return jnp.where(e == 0, first, second)


def norm_two_back(chunk, kind, counts, middle, masked, pair, far, gain, grad_mid, branch, small):
    weight = own_weight(chunk, kind, counts)
    unit, scale = unit_rows(middle[...])
    grad = (pair[...].astype(f32) + far[...].astype(f32)) * weight
    own_cot = jnp.where(is_first(), masked[0], masked[1]).astype(f32)
    out = own_cot * weight + norm_back(grad, unit, scale, line(gain))
    grad_mid[...] = out
    branch[...] = out.astype(bf16)
    small[...] = jnp.zeros_like(small)
    small[0:1, :] = jnp.sum(grad * unit, 0, keepdims=True)
    small[1:2, :] = jnp.sum(grad, 0, keepdims=True)
    small[2:3, :] = jnp.sum(out, 0, keepdims=True)


def run_norm_two_back(call, chunk, kind, counts, middle, masked, pair, far, gain):
    shape = middle.shape
    return call(
        functools.partial(norm_two_back, chunk),
        (kind, counts, middle, masked, pair, far, gain),
        [sspec()] + [vspec()] * 6,
        [arr(shape, f32), arr(shape, bf16), arr((8, shape[1]), f32)],
        flops=20 * middle.size,
        name="norm_two_back_%d" % chunk,
    )


def attention_backward(chunk, heads, mask, own, other, w_out, proj, w_t, gproj, part_own, part_other, small):
    width = heads * HEAD
    first = is_first()
    parts = []
    small[...] = jnp.zeros_like(small)
    for j in range(2):
        live = live_rows(mask, 2 * chunk + j)
        a, b = (own, other) if j == 0 else (other, own)
        branch = jnp.where(first, a[...], b[...])
        gctx = dot(branch, w_out[...], NT).astype(bf16)
        p_row = proj[j]
        key_live = iota((PAD, PAD), 1) < live
        gq, gk, gv = [], [], []
        for h in range(heads):
            q = p_row[:, h * HEAD : (h + 1) * HEAD]
            k = p_row[:, width + h * HEAD : width + (h + 1) * HEAD]
            v = p_row[:, 2 * width + h * HEAD : 2 * width + (h + 1) * HEAD]
            gc = gctx[:, h * HEAD : (h + 1) * HEAD]
            s = jnp.where(key_live, dot(q, k, NT) * 0.125, -1e30)
            e = jnp.exp(s - jnp.max(s, -1, keepdims=True))
            att = e * (1.0 / jnp.sum(e, -1, keepdims=True))
            ga = dot(gc, v, NT)
            gs = (att * (ga - jnp.sum(ga * att, -1, keepdims=True))).astype(bf16)
            gv.append(dot(att.astype(bf16), gc, TN))
            gq.append(dot(gs, k) * 0.125)
            gk.append(dot(gs, q, TN) * 0.125)
        gp = jnp.concatenate(gq + gk + gv, axis=1).astype(bf16)
        gproj[j] = gp
        small[0:1, :] += jnp.sum(gp.astype(f32), 0, keepdims=True)
        parts.append(dot(gp, w_t[...]))
    part_own[...] = jnp.where(first, parts[0], parts[1]).astype(bf16)
    part_other[...] = jnp.where(first, parts[1], parts[0]).astype(bf16)


def run_attention_backward(call, chunk, heads, mask, own, other, w_out, proj, w_t):
    width = heads * HEAD
    d = own.shape[1]
    return call(
        functools.partial(attention_backward, chunk, heads),
        (mask, own, other, w_out, proj, w_t),
        [sspec()] + [vspec()] * 5,
        [arr((2, PAD, 3 * width), bf16), arr((PAD, d), bf16), arr((PAD, d), bf16), arr((8, 3 * width), f32)],
        flops=2 * 2 * PAD * (d * 4 * width + 5 * PAD * width),
        name="attention_backward_%d" % chunk,
    )


def attention_grads(items, heads, *refs):
    width = heads * HEAD
    chunks = items // 2
    gproj, normed, ctx = refs[:chunks], refs[chunks : 2 * chunks], refs[2 * chunks : 3 * chunks]
    own, other = refs[3 * chunks : 4 * chunks], refs[4 * chunks : 5 * chunks]
    send, keep, both = refs[5 * chunks :]
    first = is_first()
    rows = 3 * width
    total = jnp.zeros((rows, keep.shape[1]), f32)
    total_out = jnp.zeros((width, keep.shape[1]), f32)
    for k in range(chunks):
        for j in range(2):
            total = total + dot(gproj[k][j], normed[k][j], TN)
            a, b = (own[k], other[k]) if j == 0 else (other[k], own[k])
            branch = jnp.where(first, a[...], b[...])
            total_out = total_out + dot(ctx[k][:, j * width : (j + 1) * width], branch, TN)
    half = 2 * width
    both[0] = total[:half].astype(bf16)
    both[1, 0 : rows - half] = total[half:].astype(bf16)
    both[1, rows - half :] = total_out.astype(bf16)
    one, _ = places()
    keep[...] = both[one]
    send[...] = both[1 - one]


def run_attention_grads(call, items, heads, gproj, normed, ctx, own, other):
    width = heads * HEAD
    d = own[0].shape[1]
    return call(
        functools.partial(attention_grads, items, heads),
        (*gproj, *normed, *ctx, *own, *other),
        [vspec()] * (5 * items // 2),
        [arr((2 * width, d), bf16)] * 2,
        [VMEM((2, 2 * width, d), bf16)],
        flops=2 * items * PAD * d * 4 * width,
        name="attention_grads",
    )


def norm_one_back(chunk, tokens, grad_mid, pair, far, gain, grad_own, small, buf):
    offsets = stage_rows(tokens, buf, chunk)
    x = jnp.where(is_first(), item_rows(buf, offsets[0], PAD), item_rows(buf, offsets[1], PAD))
    unit, scale = unit_rows(x)
    grad = pair[...].astype(f32) + far[...].astype(f32)
    grad_own[...] = (grad_mid[...] + norm_back(grad, unit, scale, line(gain))).astype(bf16)
    small[...] = jnp.zeros_like(small)
    small[0:1, :] = jnp.sum(grad * unit, 0, keepdims=True)
    small[1:2, :] = jnp.sum(grad, 0, keepdims=True)


def run_norm_one_back(call, chunk, tokens, grad_mid, pair, far, gain):
    shape = grad_mid.shape
    return call(
        functools.partial(norm_one_back, chunk),
        (tokens, grad_mid, pair, far, gain),
        [vspec()] * 5,
        [arr(shape, bf16), arr((8, shape[1]), f32)],
        [VMEM((STAGE, shape[1]), f32)],
        flops=20 * grad_mid.size,
        name="norm_one_back_%d" % chunk,
    )


def output_rows(chunk, kind, middle, pair, far, down_bias, out):
    e = jnp.where(is_first(), expert_of(kind, 2 * chunk), expert_of(kind, 2 * chunk + 1))
    bias = down_bias[pl.ds(e, 1), :]
    out[...] = (middle[...] + (pair[...].astype(f32) + far[...].astype(f32)) + bias).astype(bf16)


def run_output_rows(call, chunk, kind, middle, pair, far, down_bias):
    return call(
        functools.partial(output_rows, chunk),
        (kind, middle, pair, far, down_bias),
        [sspec()] + [vspec()] * 4,
        [arr(middle.shape, bf16)],
        flops=4 * middle.size,
        name="output_rows_%d" % chunk,
    )[0]


def assemble(items, *refs):
    chunks = items // 2
    own, other, out, buf = refs[:chunks], refs[chunks : 2 * chunks], refs[2 * chunks], refs[2 * chunks + 1]
    first = is_first()
    for k in range(chunks):
        for j in range(2):
            a, b = (own[k], other[k]) if j == 0 else (other[k], own[k])
            rows = jnp.where(first, a[...], b[...]).astype(f32)
            buf[pl.ds((2 * k + j) * SEQ, PAD), :] = rows
    out[...] = buf[0 : items * SEQ, :].astype(bf16)


def run_assemble(call, items, own, other, name):
    d = own[0].shape[1]
    return call(
        functools.partial(assemble, items),
        (*own, *other),
        [vspec()] * items,
        [arr((items * SEQ, d), bf16)],
        [VMEM((items * SEQ + 16, d), f32)],
        name=name,
    )[0]


def swap(value, axis, size, bit):
    return lax.ppermute(value, axis, [(i, i ^ bit) for i in range(size)])


def add_kernel(a, b, out):
    out[...] = (a[...].astype(f32) + b[...].astype(f32)).astype(out.dtype)


def run_add(call, a, b, name):
    return call(add_kernel, (a, b), [vspec()] * 2, [arr(a.shape, a.dtype)], name=name)[0]


def fold_kernel(keep, got, send_next, keep_next):
    _, two = places()
    keep_next[...] = (keep[two].astype(f32) + got[two].astype(f32)).astype(bf16)
    send_next[...] = (keep[1 - two].astype(f32) + got[1 - two].astype(f32)).astype(bf16)


def join_kernel(stage, own, other, out):
    bit = places()[stage]
    out[bit] = own[...].astype(out.dtype)
    out[1 - bit] = other[...].astype(out.dtype)


def run_join(call, stage, own, other, dtype, name):
    out = call(
        functools.partial(join_kernel, stage), (own, other), [vspec()] * 2, [arr((2, *own.shape), dtype)], name=name
    )[0]
    return out.reshape(2 * own.shape[0], *own.shape[1:])


class Sum:
    def __init__(self, call, dp, tp, name, send, keep):
        self.call, self.dp, self.tp, self.name, self.keep = call, dp, tp, name, keep
        if dp == 8:
            self.got = self.cross(send, (1, 2))
            return
        one, _ = places()
        flat = jnp.where(one == 0, jnp.concatenate([keep, send]), jnp.concatenate([send, keep]))
        share = lax.psum_scatter(flat, "dp", scatter_dimension=0, tiled=True)
        self.whole = lax.all_gather(share, "dp", axis=0, tiled=True).astype(f32)

    def cross(self, value, bits):
        dp, tp = self.dp, self.tp
        route = [(i * tp + t, (i ^ bits[t % 2]) * tp + t) for i in range(dp) for t in range(tp)]
        return lax.ppermute(value, ("dp", "tensor"), route)

    def quarter(self):
        if self.dp != 8:
            return
        rows, d = self.keep.shape
        halves = (2, rows // 2, d)
        send, self.keep = self.call(
            fold_kernel,
            (self.keep.reshape(halves), self.got.reshape(halves)),
            [vspec()] * 2,
            [arr(halves[1:], bf16)] * 2,
            name=self.name + "_half",
        )
        self.got = self.cross(send, (2, 1))

    def middle(self):
        if self.dp != 8:
            return
        self.keep = run_add(self.call, self.keep, self.got, self.name + "_quarter")
        self.got = self.cross(self.keep, (4, 4))

    def back_half(self):
        if self.dp != 8:
            return
        self.keep = run_add(self.call, self.keep, self.got, self.name + "_sum")
        self.got = self.cross(self.keep, (2, 1))

    def back_whole(self):
        if self.dp != 8:
            return
        self.keep = run_join(self.call, 1, self.keep, self.got, bf16, self.name + "_join")
        self.got = self.cross(self.keep, (1, 2))

    def finish(self):
        if self.dp == 8:
            self.whole = run_join(self.call, 0, self.keep, self.got, f32, self.name + "_whole")
        return self.whole


def collect(heads, chunks, *refs):
    width = heads * HEAD
    two, one, exp, attn = (refs[i * chunks : (i + 1) * chunks] for i in range(4))
    norms, rest = refs[4 * chunks :]
    norms[...] = jnp.zeros_like(norms)
    rest[...] = jnp.zeros_like(rest)
    norms[0:3, :] = sum(r[0:3, :] for r in two)
    norms[3:5, :] = sum(r[0:2, :] for r in one)
    rest[0:4, :] = sum(r[0:4, :] for r in exp)
    rest[4:5, 0 : 3 * width] = sum(r[0:1, :] for r in attn)


def stack_kernel(norms, got, rest, out):
    out[0:8, :] = norms[...] + got[...]
    out[8:16, :] = rest[...]


def local(
    dp, tp,
    tokens, token_mask, expert_type, cotangent, ln1_gain, ln1_bias, w_qkv, qv_bias, w_out, out_bias,
    ln2_gain, ln2_bias, w_up, up_bias, w_down, down_bias,
):
    rows, d = tokens.shape
    items = rows // SEQ
    width = w_qkv.shape[2]
    heads = width // HEAD
    core_swap = lambda v: swap(v, "tensor", tp, 1)
    far_swap = lambda v: swap(v, "tensor", tp, 2)
    chunks = items // 2
    call = Order()
    w_t = w_qkv.transpose(1, 2, 0).reshape(3 * width, d)

    def pair_sum(own, other, name):
        pair = run_add(call, own, core_swap(other), name)
        return pair, far_swap(pair)

    o2 = far_swap(w_out)
    outs = (w_out, core_swap(w_out), o2, core_swap(o2))
    totals = run_count_rows(call, items, token_mask, expert_type)
    bit = 1
    ctx, proj, normed_one, ctxs = [], [], [], []
    for k in range(chunks):
        got = swap(totals, "dp", dp, bit) if bit < dp else None
        c0, p, n = run_attention_forward(call, k, heads, token_mask, tokens, w_t, qv_bias, ln1_gain, ln1_bias)
        ctx.append(c0)
        proj.append(p)
        normed_one.append(n)
        c2 = far_swap(c0)
        ctxs.append((c0, core_swap(c0), c2, core_swap(c2)))
        if bit < dp:
            totals = run_add(call, totals, got, "count_%d" % bit)
            bit = 2 * bit
    got = swap(totals, "dp", dp, bit) if bit < dp else None

    middle, masked, normed_two, active, ghid, small_e = [], [], [], [], [], []
    down, part, pairs = [], [], []
    for k in range(chunks):
        m, c, n, a, g, do, dt, po, pt, s = run_experts(
            call, k, heads, token_mask, expert_type, tokens, cotangent, ctxs[k], outs, out_bias, ln2_gain, ln2_bias,
            up_bias, w_up, w_down,
        )
        for group, value in zip(
            (middle, masked, normed_two, active, ghid, down, part, small_e), (m, c, n, a, g, (do, dt), (po, pt), s)
        ):
            group.append(value)
        if k < chunks - 1:
            pairs.append(pair_sum(po, pt, "part_%d" % k))
        if k == 0:
            while bit < dp:
                totals = run_add(call, totals, got, "count_%d" % bit)
                bit = 2 * bit
                got = swap(totals, "dp", dp, bit) if bit < dp else None

    send, keep = run_expert_grads(call, items, expert_type, totals, active, masked, "down_grads")
    sum_down = Sum(call, dp, tp, "down", send, keep)

    grad_mid, branch_own, branch_other, small_n = [None] * chunks, [None] * chunks, [None] * chunks, [None] * chunks
    gproj, small_a, ones = [None] * chunks, [None] * chunks, [None] * chunks

    def norm_two(k):
        grad_mid[k], branch_own[k], small_n[k] = run_norm_two_back(
            call, k, expert_type, totals, middle[k], masked[k], *pairs[k], ln2_gain
        )
        branch_other[k] = core_swap(branch_own[k])

    def attention(k):
        gproj[k], po, pt, small_a[k] = run_attention_backward(
            call, k, heads, token_mask, branch_own[k], branch_other[k], w_out, proj[k], w_t
        )
        ones[k] = (po, pt)

    for k in range(chunks - 1):
        norm_two(k)
    pairs.append(pair_sum(*part[-1], "part_%d" % (chunks - 1)))
    for k in range(chunks - 1):
        attention(k)
    norm_two(chunks - 1)
    sum_down.quarter()
    send, keep = run_expert_grads(call, items, expert_type, totals, normed_two, ghid, "up_grads")
    sum_up = Sum(call, dp, tp, "up", send, keep)
    attention(chunks - 1)
    sum_down.middle()
    send, keep = run_attention_grads(call, items, heads, gproj, normed_one, ctx, branch_own, branch_other)
    pairs_one = [pair_sum(*ones[k], "one_%d" % k) for k in range(chunks)]
    sum_up.quarter()
    sum_attn = Sum(call, dp, tp, "attn", send, keep)
    pairs_down = [pair_sum(*down[k], "out_%d" % k) for k in range(chunks)]
    sum_up.middle()
    sum_attn.quarter()

    grad_own, small_o = [], []
    for k in range(chunks):
        g, s = run_norm_one_back(call, k, tokens, grad_mid[k], *pairs_one[k], ln1_gain)
        grad_own.append(g)
        small_o.append(s)
    grad_other = [core_swap(g) for g in grad_own]
    norms, rest = call(
        functools.partial(collect, heads, chunks),
        (*small_n, *small_o, *small_e, *small_a),
        [vspec()] * (4 * chunks),
        [arr((8, d), f32)] * 2,
        name="collect",
    )
    got_norms = core_swap(norms)
    sum_down.back_half()
    small = call(stack_kernel, (norms, got_norms, rest), [vspec()] * 3, [arr((16, d), f32)], name="stack")[0]
    bit = 1
    got = swap(small, "dp", dp, bit) if bit < dp else None
    sum_attn.middle()
    grad_tokens = run_assemble(call, items, grad_own, grad_other, "grad_tokens")
    sum_down.back_whole()
    out_own = [run_output_rows(call, k, expert_type, middle[k], *pairs_down[k], down_bias) for k in range(chunks)]
    out_other = [core_swap(o) for o in out_own]
    while bit < dp:
        small = run_add(call, small, got, "small_%d" % bit)
        bit = 2 * bit
        got = swap(small, "dp", dp, bit) if bit < dp else None
    output = run_assemble(call, items, out_own, out_other, "output")
    sum_up.back_half()
    grad_down = sum_down.finish()
    sum_up.back_whole()
    sum_attn.back_half()
    sum_attn.back_whole()
    grad_up = sum_up.finish()
    grad_attn = sum_attn.finish()

    both = totals[:2, 0]
    weights = ((both[0] + both[1]) / (2.0 * both))[:, None]
    grad_qkv = grad_attn[: 3 * width].reshape(3, width, d).transpose(2, 0, 1)
    grad_out = grad_attn[3 * width :]
    grad_qv_bias = jnp.stack([small[12, :width], small[12, 2 * width : 3 * width]])
    return (
        output,
        grad_tokens,
        small[3],
        small[4],
        grad_qkv,
        grad_qv_bias,
        grad_out,
        small[2],
        small[0],
        small[1],
        grad_up.reshape(w_up.shape),
        small[8:10] * weights,
        grad_down.reshape(w_down.shape),
        small[10:12] * weights,
        both.astype(jnp.int32),
    )


def solution(mesh):
    in_specs = (
        P("dp", None),
        P("dp"),
        P("dp"),
        P("dp", None),
        P(),
        P(),
        P(None, None, "tensor"),
        P(None, "tensor"),
        P("tensor", None),
        P(),
        P(),
        P(),
        P(None, None, "tensor"),
        P(None, "tensor"),
        P(None, "tensor", None),
        P(),
    )
    out_specs = (
        P("dp", None),
        P("dp", None),
        P(),
        P(),
        P(None, None, "tensor"),
        P(None, "tensor"),
        P("tensor", None),
        P(),
        P(),
        P(),
        P(None, None, "tensor"),
        P(None, "tensor"),
        P(None, "tensor", None),
        P(),
        P(),
    )
    return jax.shard_map(
        functools.partial(local, mesh.shape["dp"], mesh.shape["tensor"]),
        mesh=mesh,
        in_specs=in_specs,
        out_specs=out_specs,
        check_vma=False,
    )
```

```python
import functools

import jax
import jax.numpy as jnp
from jax import lax
from jax.experimental import pallas as pl
from jax.experimental.pallas import tpu as pltpu
from jax.sharding import PartitionSpec as P

HEAD = 64
PATCHES = 197
CAP = 40
SEQ = PATCHES + CAP
PAD = 240
ATT = 256
STAGE = 2 * SEQ + 32

epsilon = 1e-05
f32 = jnp.float32
bf16 = jnp.bfloat16

NT = (((1,), (1,)), ((), ()))
NN = (((1,), (0,)), ((), ()))
TN = (((0,), (0,)), ((), ()))

VMEM = pltpu.VMEM
SMEM = pltpu.SMEM
DMA = pltpu.SemaphoreType.DMA


def dot(a, b, dims=NN):
    return lax.dot_general(a, b, dims, preferred_element_type=f32)


def iota(shape, dim):
    return lax.broadcasted_iota(jnp.int32, shape, dim)


def unit_rows(x):
    mean = jnp.mean(x, -1, keepdims=True)
    centered = x - mean
    scale = lax.rsqrt(jnp.mean(centered * centered, -1, keepdims=True) + epsilon)
    return centered * scale, scale


def norm_back(grad, unit, scale, gain):
    t = grad * gain
    return scale * (
        t - jnp.mean(t, -1, keepdims=True) - unit * jnp.mean(t * unit, -1, keepdims=True)
    )


def vspec():
    return pl.BlockSpec(memory_space=VMEM)


def hspec():
    return pl.BlockSpec(memory_space=pltpu.HBM)


def aspec():
    return pl.BlockSpec(memory_space=pl.ANY)


class Order:
    def __init__(self):
        self.last = None

    def __call__(self, kernel, ins, outs, scratch=(), limit=16, specs=None, out_specs=None, name=None):
        taken = len(ins)
        behind = () if self.last is None or any(a is self.last for a in ins) else (self.last,)

        def body(*refs):
            kernel(*refs[:taken], *refs[taken + len(behind) :])

        results = pl.pallas_call(
            body,
            out_shape=list(outs),
            in_specs=list(specs or [vspec() for _ in ins]) + [aspec() for _ in behind],
            out_specs=list(out_specs or [vspec() for _ in outs]),
            scratch_shapes=list(scratch),
            compiler_params=pltpu.CompilerParams(vmem_limit_bytes=limit * 1024 * 1024),
            cost_estimate=pl.CostEstimate(flops=1, bytes_accessed=1, transcendentals=0),
            name=name,
        )(*ins, *behind)
        self.last = results[0]
        return results


def arr(shape, dtype):
    return jax.ShapeDtypeStruct(shape, dtype)


def position():
    return lax.axis_index("tensor")


def is_first():
    return lax.rem(position(), 2) == 0


def places():
    place = lax.axis_index("dp")
    low = lax.rem(place, 2)
    high = lax.rem(lax.div(place, 2), 2)
    first = is_first()
    return jnp.where(first, low, high), jnp.where(first, high, low)


def stage_rows(rows, buf, chunk):
    low = 2 * chunk * SEQ
    high = low + 2 * SEQ
    base = low // 16 * 16
    top = min(rows.shape[0], -(-high // 16) * 16)
    buf[0 : top - base] = rows[base:top].astype(f32)
    return [low - base, low - base + SEQ]


def item_rows(buf, offset, count, live=SEQ):
    rows = buf[pl.ds(offset, count), :]
    return jnp.where(iota(rows.shape, 0) < live, rows, 0.0)


def live_of(info, item):
    return info[item : item + 1, 0:1].astype(jnp.int32)


def expert_vector(info, items, item):
    return info[items + item : items + item + 1, 0:1]


def expert_of(info, items, item):
    return jnp.max(info[items + item : items + item + 1, :]).astype(jnp.int32)


def row_weight(counts):
    both = counts[0:1, 0:1] + counts[1:2, 0:1]
    return both / (2.0 * counts[0:1, 0:1]), both / (2.0 * counts[1:2, 0:1])


def attention_items(chunk, heads, info, rows, w_t, qv_bias, gain, bias, ctx, proj, normed, kept, buf):
    width = heads * HEAD
    offsets = stage_rows(rows, buf, chunk)
    b_three = jnp.concatenate([qv_bias[0:1, :], jnp.zeros((1, width), f32), qv_bias[1:2, :]], axis=1)
    for j in range(2):
        live = live_of(info, 2 * chunk + j)
        x = item_rows(buf, offsets[j], ATT)
        kept[j] = x[:PAD].astype(bf16)
        unit, _ = unit_rows(x)
        n_row = (unit * gain + bias).astype(bf16)
        normed[j] = n_row[:PAD]
        p_row = (dot(n_row, w_t[...], NT) + b_three).astype(bf16)
        proj[j] = p_row[:PAD]
        key_live = iota((ATT, ATT), 1) < live
        for h in range(heads):
            q = p_row[:, h * HEAD : (h + 1) * HEAD]
            k = p_row[:, width + h * HEAD : width + (h + 1) * HEAD]
            v = p_row[:, 2 * width + h * HEAD : 2 * width + (h + 1) * HEAD]
            s = jnp.where(key_live, dot(q, k, NT) * 0.125, -1e30)
            e = jnp.exp(s - jnp.max(s, -1, keepdims=True))
            att = (e * (1.0 / jnp.sum(e, -1, keepdims=True))).astype(bf16)
            c = dot(att, v).astype(bf16)
            at = j * width + h * HEAD
            ctx[:, at : at + HEAD] = c[:PAD]


def front(
    items, heads, mask_h, kind_h, tokens_h, w_h, qv_h, *refs
):
    vectors_h, refs = refs[:5], refs[5:]
    ctx, proj, normed, kept, info, counts, vecs = refs[:7]
    mask, kind, tokens, w_t, qv_bias, lines, buf, sems = refs[7:]
    pairs = [(mask_h, mask), (kind_h, kind), (tokens_h, tokens), (w_h, w_t), (qv_h, qv_bias)]
    pairs += [(v, lines.at[i]) for i, v in enumerate(vectors_h)]
    copies = [pltpu.make_async_copy(a, b, sems.at[i]) for i, (a, b) in enumerate(pairs)]
    for c in copies:
        c.start()
    copies[0].wait()
    copies[1].wait()
    total = 0
    second = 0
    row = iota(info.shape, 0)
    value = jnp.zeros(info.shape, f32)
    for i in range(items):
        n = PATCHES
        for slot in range(CAP):
            n = n + mask[i * SEQ + PATCHES + slot]
        e = kind[i * SEQ]
        total = total + n
        second = second + n * e
        value = jnp.where(row == i, n.astype(f32), value)
        value = jnp.where(row == items + i, e.astype(f32), value)
    info[...] = value
    row = iota(counts.shape, 0)
    counts[...] = jnp.where(row == 0, (total - second).astype(f32), second.astype(f32))
    for c in copies[2:]:
        c.wait()
    for i in range(5):
        vecs[i : i + 1, :] = lines[i : i + 1, :]
    attention_items(
        0, heads, info, tokens[...], w_t, qv_bias, lines[0:1, :], lines[1:2, :], ctx, proj, normed, kept, buf
    )


def run_front(call, items, heads, mask, kind, tokens, w_t, qv_bias, vectors):
    width = heads * HEAD
    rows, d = tokens.shape
    ins = (mask, kind, tokens, w_t, qv_bias, *vectors)
    return call(
        functools.partial(front, items, heads),
        ins,
        [
            arr((PAD, 2 * width), bf16),
            arr((2, PAD, 3 * width), bf16),
            arr((2, PAD, d), bf16),
            arr((2, PAD, d), bf16),
            arr((2 * items, 128), f32),
            arr((8, 128), f32),
            arr((8, d), f32),
        ],
        [
            SMEM(mask.shape, jnp.int32),
            SMEM(kind.shape, jnp.int32),
            VMEM(tokens.shape, bf16),
            VMEM(w_t.shape, bf16),
            VMEM(qv_bias.shape, f32),
            VMEM((8, d), f32),
            VMEM((STAGE, d), f32),
            DMA((len(ins),)),
        ],
        specs=[hspec() for _ in ins],
        limit=60,
        name="front",
    )


def attention_forward(chunk, heads, info, vecs, tokens, w_t, qv_bias, ctx, proj, normed, kept, buf):
    attention_items(
        chunk, heads, info, tokens[...], w_t, qv_bias, vecs[0:1, :], vecs[1:2, :], ctx, proj, normed, kept, buf
    )


def run_attention_forward(call, chunk, heads, info, vecs, tokens, w_t, qv_bias):
    width = heads * HEAD
    d = tokens.shape[1]
    return call(
        functools.partial(attention_forward, chunk, heads),
        (info, vecs, tokens, w_t, qv_bias),
        [arr((PAD, 2 * width), bf16), arr((2, PAD, 3 * width), bf16), arr((2, PAD, d), bf16), arr((2, PAD, d), bf16)],
        [VMEM((STAGE, d), f32)],
        name="attention_forward_%d" % chunk,
    )


def mask_rows(items, info, cot, masked, small, buf):
    d = cot.shape[1]
    buf[0 : items * SEQ] = cot[...].astype(f32)
    zero = jnp.zeros((1, d), f32)
    sums = [zero, zero]
    for i in range(items):
        rows = item_rows(buf, i * SEQ, PAD, live_of(info, i))
        masked[i] = rows.astype(bf16)
        line = jnp.sum(rows, 0, keepdims=True)
        e = expert_vector(info, items, i)
        for x in range(2):
            sums[x] = sums[x] + jnp.where(e == x, line, 0.0)
    small[...] = jnp.zeros_like(small)
    small[0:1, :] = sums[0]
    small[1:2, :] = sums[1]


def run_mask_rows(call, items, info, cot):
    d = cot.shape[1]
    return call(
        functools.partial(mask_rows, items),
        (info, cot),
        [arr((items, PAD, d), bf16), arr((8, d), f32)],
        [VMEM((items * SEQ + 16, d), f32)],
        name="mask_rows",
    )


def gather_slots():
    t = position()
    core = lax.rem(t, 2)
    return (t, t + 1 - 2 * core, lax.rem(t + 2, 4), lax.rem(t + 3 - 2 * core, 4))


def slot_kernel(a, b, c, d, out):
    for slot, ref in zip(gather_slots(), (a, b, c, d)):
        out[slot] = ref[...]


def run_slots(call, parts, name):
    return call(slot_kernel, parts, [arr((4, *parts[0].shape), parts[0].dtype)], name=name)[0]


def gelu_parts(h):
    cdf = 0.5 * (1.0 + lax.erf(h * 0.7071067811865476))
    density = jnp.exp(-0.5 * h * h) * 0.3989422804014327
    return h * cdf, cdf + h * density


def experts(chunk, items, heads, info, vecs, kept, masked, c0, c1, c2, c3, w_out, up_bias, w_up, w_down, *refs):
    width = heads * HEAD
    d = kept.shape[2]
    middle, normed, active, ghid, small = refs[:5]
    sides = refs[5:9]
    ctx = refs[9]
    first = is_first()
    for slot, c in zip(gather_slots(), (c0, c1, c2, c3)):
        ctx[slot] = c[...]
    mids, n_rows = [], []
    for j in range(2):
        total = jnp.zeros((PAD, d), f32)
        for s in range(4):
            total = total + dot(ctx[s][:, j * width : (j + 1) * width], w_out[s])
        mid = kept[j].astype(f32) + total + vecs[2:3, :]
        mids.append(mid)
        unit, _ = unit_rows(mid)
        n_row = (unit * vecs[3:4, :] + vecs[4:5, :]).astype(bf16)
        normed[j] = n_row
        n_rows.append(n_row)
    middle[...] = jnp.where(first, mids[0], mids[1])
    parts, downs = [], []
    zero = jnp.zeros((1, w_up.shape[2]), f32)
    sums = [zero, zero]
    for j in range(2):
        e = expert_of(info, items, 2 * chunk + j)
        wu = w_up[e]
        wd = w_down[e]
        h = dot(n_rows[j], wu) + up_bias[pl.ds(e, 1), :]
        value, slope = gelu_parts(h)
        act = value.astype(bf16)
        active[j] = act
        gh = (dot(masked[2 * chunk + j], wd, NT) * slope).astype(bf16)
        ghid[j] = gh
        parts.append(dot(gh, wu, NT))
        downs.append(dot(act, wd))
        line = jnp.sum(gh.astype(f32), 0, keepdims=True)
        flag = expert_vector(info, items, 2 * chunk + j)
        for x in range(2):
            sums[x] = sums[x] + jnp.where(flag == x, line, 0.0)
    small[...] = jnp.zeros_like(small)
    small[0:1, :] = sums[0]
    small[1:2, :] = sums[1]
    values = (
        jnp.where(first, parts[0], parts[1]),
        jnp.where(first, parts[1], parts[0]),
        jnp.where(first, downs[0], downs[1]),
        jnp.where(first, downs[1], downs[0]),
    )
    for side, value in zip(sides, values):
        side[...] = value.astype(bf16)


def run_experts(call, chunk, items, heads, info, vecs, kept, masked, ctxs, w_out, up_bias, w_up, w_down):
    width = heads * HEAD
    d = kept.shape[2]
    ff = w_up.shape[2]
    side = arr((PAD, d), bf16)
    return call(
        functools.partial(experts, chunk, items, heads),
        (info, vecs, kept, masked, *ctxs, w_out, up_bias, w_up, w_down),
        [
            arr((PAD, d), f32),
            arr((2, PAD, d), bf16),
            arr((2, PAD, ff), bf16),
            arr((2, PAD, ff), bf16),
            arr((8, d), f32),
        ]
        + [side] * 4,
        [VMEM((4, PAD, 2 * width), bf16)],
        limit=20,
        name="experts_%d" % chunk,
    )


def expert_grads(items, merged, info, *refs):
    chunks = items // 2
    lefts, refs = refs[:chunks], refs[chunks:]
    rights = refs[: 1 if merged else chunks]
    send, keep, total = refs[len(rights) :]
    for i in range(items):
        e = expert_of(info, items, i)
        right = rights[0][i] if merged else rights[i // 2][i % 2]
        term = dot(lefts[i // 2][i % 2], right, TN)
        if i == 0:
            total[e] = term
            total[1 - e] = jnp.zeros_like(term)
        else:
            total[e] += term
    one, _ = places()
    keep[...] = total[one].astype(bf16)
    send[...] = total[1 - one].astype(bf16)


def run_expert_grads(call, items, info, lefts, rights, name):
    merged = len(rights) == 1
    shape = (lefts[0].shape[2], rights[0].shape[2])
    return call(
        functools.partial(expert_grads, items, merged),
        (info, *lefts, *rights),
        [arr(shape, bf16)] * 2,
        [VMEM((2, *shape), f32)],
        name=name,
    )


def own_expert(info, items, chunk):
    return jnp.where(is_first(), expert_vector(info, items, 2 * chunk), expert_vector(info, items, 2 * chunk + 1))


def norm_two_back(items, info, counts, vecs, masked, pair, far, *refs):
    chunks = items // 2
    middles, branch, (grad_mid, small) = refs[:chunks], refs[chunks : 2 * chunks], refs[2 * chunks :]
    d = pair.shape[2]
    first, second = row_weight(counts)
    zero = jnp.zeros((1, d), f32)
    sums = [zero] * 3
    for k in range(chunks):
        weight = jnp.where(own_expert(info, items, k) == 0, first, second)
        own_cot = jnp.where(is_first(), masked[2 * k], masked[2 * k + 1]).astype(f32)
        unit, scale = unit_rows(middles[k][...])
        grad = (pair[k].astype(f32) + far[k].astype(f32)) * weight
        out = own_cot * weight + norm_back(grad, unit, scale, vecs[3:4, :])
        grad_mid[k] = out
        branch[k][...] = out.astype(bf16)
        for i, value in enumerate((grad * unit, grad, out)):
            sums[i] = sums[i] + jnp.sum(value, 0, keepdims=True)
    small[...] = jnp.zeros_like(small)
    for i in range(3):
        small[i : i + 1, :] = sums[i]


def run_norm_two_back(call, items, info, counts, vecs, masked, pair, far, middles):
    return call(
        functools.partial(norm_two_back, items),
        (info, counts, vecs, masked, pair, far, *middles),
        [arr(pair.shape[1:], bf16)] * len(middles) + [arr(pair.shape, f32), arr((8, pair.shape[2]), f32)],
        name="norm_two_back",
    )


def attention_backward(
    chunk, heads, info, own, other, w_out, proj, w_t, kept, gproj, small, small_one, part_own, part_other
):
    width = heads * HEAD
    first = is_first()
    parts = []
    d = w_t.shape[1]
    sums = [jnp.zeros((1, d), f32)] * 2
    total = jnp.zeros((1, 3 * width), f32)
    for j in range(2):
        live = live_of(info, 2 * chunk + j)
        a, b = (own, other) if j == 0 else (other, own)
        branch = jnp.where(first, a[...], b[...])
        gctx = dot(branch, w_out[...], NT).astype(bf16)
        p_row = proj[j]
        key_live = iota((PAD, PAD), 1) < live
        gq, gk, gv = [], [], []
        for h in range(heads):
            q = p_row[:, h * HEAD : (h + 1) * HEAD]
            k = p_row[:, width + h * HEAD : width + (h + 1) * HEAD]
            v = p_row[:, 2 * width + h * HEAD : 2 * width + (h + 1) * HEAD]
            gc = gctx[:, h * HEAD : (h + 1) * HEAD]
            s = jnp.where(key_live, dot(q, k, NT) * 0.125, -1e30)
            e = jnp.exp(s - jnp.max(s, -1, keepdims=True))
            att = e * (1.0 / jnp.sum(e, -1, keepdims=True))
            ga = dot(gc, v, NT)
            gs = (att * (ga - jnp.sum(ga * att, -1, keepdims=True))).astype(bf16)
            gv.append(dot(att.astype(bf16), gc, TN))
            gq.append(dot(gs, k) * 0.125)
            gk.append(dot(gs, q, TN) * 0.125)
        gp = jnp.concatenate(gq + gk + gv, axis=1).astype(bf16)
        gproj[j] = gp
        total = total + jnp.sum(gp.astype(f32), 0, keepdims=True)
        part = dot(gp, w_t[...])
        parts.append(part)
        unit, _ = unit_rows(kept[j].astype(f32))
        sums[0] = sums[0] + jnp.sum(part * unit, 0, keepdims=True)
        sums[1] = sums[1] + jnp.sum(part, 0, keepdims=True)
    small[...] = jnp.zeros_like(small)
    small[0:1, :] = total
    small_one[...] = jnp.zeros_like(small_one)
    for i in range(2):
        small_one[i : i + 1, :] = sums[i]
    part_own[...] = jnp.where(first, parts[0], parts[1]).astype(bf16)
    part_other[...] = jnp.where(first, parts[1], parts[0]).astype(bf16)


def run_attention_backward(call, chunk, heads, info, own, other, w_out, proj, w_t, kept):
    width = heads * HEAD
    d = own.shape[1]
    side = arr((PAD, d), bf16)
    return call(
        functools.partial(attention_backward, chunk, heads),
        (info, own, other, w_out, proj, w_t, kept),
        [arr((2, PAD, 3 * width), bf16), arr((8, 3 * width), f32), arr((8, d), f32), side, side],
        name="attention_backward_%d" % chunk,
    )


def attention_grads(items, heads, *refs):
    width = heads * HEAD
    chunks = items // 2
    own, other, gproj, normed, ctx = (refs[i * chunks : (i + 1) * chunks] for i in range(5))
    send, keep, both = refs[5 * chunks :]
    first = is_first()
    rows = 3 * width
    total = jnp.zeros((rows, keep.shape[1]), f32)
    total_out = jnp.zeros((width, keep.shape[1]), f32)
    for k in range(chunks):
        for j in range(2):
            total = total + dot(gproj[k][j], normed[k][j], TN)
            a, b = (own, other) if j == 0 else (other, own)
            branch = jnp.where(first, a[k][...], b[k][...])
            total_out = total_out + dot(ctx[k][:, j * width : (j + 1) * width], branch, TN)
    half = 2 * width
    both[0] = total[:half].astype(bf16)
    both[1, 0 : rows - half] = total[half:].astype(bf16)
    both[1, rows - half :] = total_out.astype(bf16)
    one, _ = places()
    keep[...] = both[one]
    send[...] = both[1 - one]


def run_attention_grads(call, items, heads, own, other, gproj, normed, ctx):
    width = heads * HEAD
    d = own[0].shape[1]
    return call(
        functools.partial(attention_grads, items, heads),
        (*own, *other, *gproj, *normed, *ctx),
        [arr((2 * width, d), bf16)] * 2,
        [VMEM((2, 2 * width, d), bf16)],
        name="attention_grads",
    )


def norm_one_back(items, vecs, grad_mid, pair, far, *refs):
    chunks = items // 2
    kept, grad_own = refs[:chunks], refs[chunks]
    for k in range(chunks):
        x = jnp.where(is_first(), kept[k][0], kept[k][1]).astype(f32)
        unit, scale = unit_rows(x)
        grad = pair[k].astype(f32) + far[k].astype(f32)
        grad_own[k] = (grad_mid[k] + norm_back(grad, unit, scale, vecs[0:1, :])).astype(bf16)


def run_norm_one_back(call, items, vecs, grad_mid, pair, far, kept):
    return call(
        functools.partial(norm_one_back, items),
        (vecs, grad_mid, pair, far, *kept),
        [arr(pair.shape, bf16)],
        name="norm_one_back",
    )[0]


def output_rows(items, info, down_bias, pair, far, *refs):
    chunks = items // 2
    middles, out = refs[:chunks], refs[chunks]
    for k in range(chunks):
        bias = jnp.where(own_expert(info, items, k) == 0, down_bias[0:1, :], down_bias[1:2, :])
        out[k] = (middles[k][...] + (pair[k].astype(f32) + far[k].astype(f32)) + bias).astype(bf16)


def run_output_rows(call, items, info, down_bias, pair, far, middles):
    return call(
        functools.partial(output_rows, items),
        (info, down_bias, pair, far, *middles),
        [arr(pair.shape, bf16)],
        name="output_rows",
    )[0]


def assemble(items, own, other, out, buf, low, sem):
    first = is_first()
    for k in range(items // 2):
        for j in range(2):
            a, b = (own, other) if j == 0 else (other, own)
            buf[pl.ds((2 * k + j) * SEQ, PAD), :] = jnp.where(first, a[k], b[k]).astype(f32)
    low[...] = buf[0 : items * SEQ, :].astype(bf16)
    copy = pltpu.make_async_copy(low, out, sem)
    copy.start()
    copy.wait()


def run_assemble(call, items, own, other, name):
    d = own.shape[2]
    return call(
        functools.partial(assemble, items),
        (own, other),
        [arr((items * SEQ, d), bf16)],
        [VMEM((items * SEQ + 16, d), f32), VMEM((items * SEQ, d), bf16), DMA],
        out_specs=[hspec()],
        name=name,
    )[0]


def swap(value, axis, size, bit):
    return lax.ppermute(value, axis, [(i, i ^ bit) for i in range(size)])


def add_kernel(a, b, out):
    out[...] = (a[...].astype(f32) + b[...].astype(f32)).astype(out.dtype)


def run_add(call, a, b, name):
    return call(add_kernel, (a, b), [arr(a.shape, a.dtype)], name=name)[0]


def pair_kernel(chunks, *refs):
    own, got, out = refs[:chunks], refs[chunks : 2 * chunks], refs[2 * chunks]
    for k in range(chunks):
        out[k] = (own[k][...].astype(f32) + got[k][...].astype(f32)).astype(bf16)


def run_pair(call, own, got, name):
    return call(
        functools.partial(pair_kernel, len(own)), (*own, *got), [arr((len(own), *own[0].shape), bf16)], name=name
    )[0]


def ride(refs):
    if refs:
        held, came, out = refs
        out[...] = held[...] + came[...]


def add_ride_kernel(a, b, *refs):
    refs = list(refs)
    out = refs.pop(2 if len(refs) == 4 else 0)
    out[...] = (a[...].astype(f32) + b[...].astype(f32)).astype(out.dtype)
    ride(refs)


def fold_kernel(keep, got, *refs):
    refs = list(refs)
    at = 2 if len(refs) == 5 else 0
    send_next, keep_next = refs.pop(at), refs.pop(at)
    ride(refs)
    _, two = places()
    keep_next[...] = (keep[two].astype(f32) + got[two].astype(f32)).astype(bf16)
    send_next[...] = (keep[1 - two].astype(f32) + got[1 - two].astype(f32)).astype(bf16)


def join_kernel(own, other, out):
    _, bit = places()
    out[bit] = own[...]
    out[1 - bit] = other[...]


PIECES = 4


def whole_kernel(scaled, *refs):
    counts = refs[0] if scaled else None
    own, other, out, buf, sems = refs[1:] if scaled else refs
    bit, _ = places()
    rows = own.shape[0] // PIECES
    copies = []
    for side, ref in enumerate((own, other)):
        half = bit if side == 0 else 1 - bit
        weight = 1.0
        if scaled:
            first, second = row_weight(counts)
            weight = jnp.where(half == 0, first, second)
        for i in range(PIECES):
            at = pl.ds(i * rows, rows)
            buf[side, at] = ref[at].astype(f32) * weight
            copy = pltpu.make_async_copy(buf.at[side, at], out.at[half, at], sems.at[side, i])
            copy.start()
            copies.append(copy)
    for copy in copies:
        copy.wait()


def run_whole(call, counts, own, other, name, limit):
    scaled = counts is not None
    shape = (2, *own.shape)
    return call(
        functools.partial(whole_kernel, scaled),
        ((counts,) if scaled else ()) + (own, other),
        [arr(shape, f32)],
        [VMEM(shape, f32), DMA((2, PIECES))],
        out_specs=[hspec()],
        limit=limit,
        name=name,
    )[0]


def attention_whole_kernel(rows, own, other, grad_qkv, grad_out, low, buf, sems):
    bit, _ = places()
    half = own.shape[0]
    low[bit] = own[...]
    low[1 - bit] = other[...]
    copies = []
    spans = [(grad_qkv, 0, 0, half), (grad_qkv, 1, half, rows - half), (grad_out, 1, 0, 2 * half - rows)]
    start = [0, 0, rows - half]
    for i, (out, side, to, count) in enumerate(spans):
        at = pl.ds(start[i], count)
        buf[side, at] = low[side, at].astype(f32)
        copy = pltpu.make_async_copy(buf.at[side, at], out.at[pl.ds(to, count)], sems.at[i])
        copy.start()
        copies.append(copy)
    for copy in copies:
        copy.wait()


def run_attention_whole(call, rows, own, other, name):
    half, d = own.shape
    return call(
        functools.partial(attention_whole_kernel, rows),
        (own, other),
        [arr((rows, d), f32), arr((2 * half - rows, d), f32)],
        [VMEM((2, half, d), bf16), VMEM((2, half, d), f32), DMA((3,))],
        out_specs=[hspec(), hspec()],
        limit=60,
        name=name,
    )


class Sum:
    def __init__(self, call, dp, tp, name, send, keep, rider=None):
        self.call, self.dp, self.tp, self.name, self.keep, self.rider = call, dp, tp, name, keep, rider
        if dp == 8:
            self.go((1, 2), send)
            return
        low = (lax.axis_index("dp") % 2).astype(jnp.int32)
        high = (lax.axis_index("dp") // 2 % 2).astype(jnp.int32)
        one = jnp.where(lax.axis_index("tensor") % 2 == 0, low, high)
        flat = jnp.where(one == 0, jnp.concatenate([keep, send]), jnp.concatenate([send, keep]))
        share = lax.psum_scatter(flat, "dp", scatter_dimension=0, tiled=True)
        whole = lax.all_gather(share, "dp", axis=0, tiled=True).reshape(2, *keep.shape)
        self.keep = jnp.where(one == 0, whole[0], whole[1])
        self.got = jnp.where(one == 0, whole[1], whole[0])
        if rider is not None:
            self.rider = lax.psum(rider, "dp")

    def cross(self, value, bits):
        dp, tp = self.dp, self.tp
        route = [(i * tp + t, (i ^ bits[t % 2]) * tp + t) for i in range(dp) for t in range(tp)]
        return lax.ppermute(value, ("dp", "tensor"), route)

    def go(self, bits, value, riding=True):
        riding = riding and self.rider is not None
        self.came = (self.rider, self.cross(self.rider, bits)) if riding else ()
        self.got = self.cross(value, bits)

    def step(self, kernel, ins, outs, name):
        ride_out = [arr(self.rider.shape, f32)] if self.came else []
        out = self.call(kernel, (*ins, *self.came), [*outs, *ride_out], name=self.name + name)
        if self.came:
            self.rider = out[-1]
        return out

    def quarter(self):
        if self.dp != 8:
            return
        rows, d = self.keep.shape
        halves = (2, rows // 2, d)
        send, self.keep, *_ = self.step(
            fold_kernel,
            (self.keep.reshape(halves), self.got.reshape(halves)),
            [arr(halves[1:], bf16)] * 2,
            "_half",
        )
        self.go((2, 1), send)

    def middle(self):
        if self.dp != 8:
            return
        self.keep = self.step(add_ride_kernel, (self.keep, self.got), [arr(self.keep.shape, bf16)], "_quarter")[0]
        self.go((4, 4), self.keep)

    def back_half(self):
        if self.dp != 8:
            return
        self.keep = self.step(add_ride_kernel, (self.keep, self.got), [arr(self.keep.shape, bf16)], "_sum")[0]
        self.go((2, 1), self.keep, False)

    def back_whole(self):
        if self.dp != 8:
            return
        rows, d = self.keep.shape
        out = self.call(join_kernel, (self.keep, self.got), [arr((2, rows, d), bf16)], name=self.name + "_join")[0]
        self.keep = out.reshape(2 * rows, d)
        self.go((1, 2), self.keep, False)


def collect(heads, chunks, two, cots, *refs):
    width = heads * HEAD
    exp, attn, one, (out,) = refs[:chunks], refs[chunks : 2 * chunks], refs[2 * chunks : 3 * chunks], refs[3 * chunks :]
    out[...] = jnp.zeros_like(out)
    out[0:3, :] = two[0:3, :] * 0.5
    out[3:5, :] = sum(r[0:2, :] for r in one)
    out[8:10, :] = sum(r[0:2, :] for r in exp)
    out[10:12, :] = cots[0:2, :]
    out[12:13, 0 : 3 * width] = sum(r[0:1, :] for r in attn)


def small_outputs(heads, counts, small, norms, got, *outs):
    width = heads * HEAD
    d = small.shape[1]
    for i in range(5):
        outs[i][...] = (norms[i : i + 1, :] + got[i : i + 1, :]).reshape(d)
    for i, weight in enumerate(row_weight(counts)):
        outs[5][i : i + 1, :] = small[8 + i : 9 + i, :] * weight
        outs[6][i : i + 1, :] = small[10 + i : 11 + i, :] * weight
    row = small[12:13, :]
    outs[7][0:1, :] = row[:, 0:width]
    outs[7][1:2, :] = row[:, 2 * width : 3 * width]


def run_small_outputs(call, heads, counts, small, norms, got):
    d = small.shape[1]
    return call(
        functools.partial(small_outputs, heads),
        (counts, small, norms, got),
        [arr((d,), f32)] * 5 + [arr((2, d), f32)] * 2 + [arr((2, heads * HEAD), f32)],
        name="small_outputs",
    )


def core_rows_kernel(small, got, out):
    out[...] = small[0:8, :] + got[0:8, :]


def local(
    dp, tp,
    tokens, token_mask, expert_type, cotangent, ln1_gain, ln1_bias, w_qkv, qv_bias, w_out, out_bias,
    ln2_gain, ln2_bias, w_up, up_bias, w_down, down_bias,
):
    rows, d = tokens.shape
    items = rows // SEQ
    width = w_qkv.shape[2]
    heads = width // HEAD
    core_swap = lambda v: swap(v, "tensor", tp, 1)
    far_swap = lambda v: swap(v, "tensor", tp, 2)
    chunks = items // 2
    call = Order()
    w_t = w_qkv.transpose(1, 2, 0).reshape(3 * width, d)

    o2 = far_swap(w_out)
    o1 = core_swap(w_out)
    c0, p, n, x, info, totals, vecs = run_front(
        call, items, heads, token_mask, expert_type, tokens, w_t, qv_bias,
        (ln1_gain, ln1_bias, out_bias, ln2_gain, ln2_bias),
    )
    ctx, proj, normed_one, kept, ctxs = [c0], [p], [n], [x], []
    got = swap(totals, "dp", dp, 1)
    for k in range(1, chunks + 1):
        c2 = far_swap(ctx[-1])
        ctxs.append((ctx[-1], core_swap(ctx[-1]), c2, core_swap(c2)))
        if k < chunks:
            c0, p, n, x = run_attention_forward(call, k, heads, info, vecs, tokens, w_t, qv_bias)
            for group, value in zip((ctx, proj, normed_one, kept), (c0, p, n, x)):
                group.append(value)
    bit = 1

    def count_step(bit, totals, got):
        if bit >= dp:
            return bit, totals, None
        totals = run_add(call, totals, got, "count_%d" % bit)
        bit = 2 * bit
        return bit, totals, swap(totals, "dp", dp, bit) if bit < dp else None

    bit, totals, got = count_step(bit, totals, got)
    masked, small_c = run_mask_rows(call, items, info, cotangent)
    bit, totals, got = count_step(bit, totals, got)
    w_all = run_slots(call, (w_out, o1, o2, core_swap(o2)), "w_out_all")

    middle, normed_two, active, ghid, small_e = [], [], [], [], []
    part_own, part_got, down_own, down_got = [], [], [], []
    for k in range(chunks):
        m, n, a, g, s, po, pt, do, dt = run_experts(
            call, k, items, heads, info, vecs, kept[k], masked, ctxs[k], w_all, up_bias, w_up, w_down
        )
        for group, value in zip(
            (middle, normed_two, active, ghid, small_e, part_own, part_got, down_own, down_got),
            (m, n, a, g, s, po, core_swap(pt), do, core_swap(dt)),
        ):
            group.append(value)
        if k == 0:
            while bit < dp:
                bit, totals, got = count_step(bit, totals, got)

    send, keep = run_expert_grads(call, items, info, active, [masked], "down_grads")
    sum_down = Sum(call, dp, tp, "down", send, keep)
    part = run_pair(call, part_own, part_got, "part")
    part_far = far_swap(part)
    down = run_pair(call, down_own, down_got, "expert_rows")
    down_far = far_swap(down)
    sum_down.quarter()
    send, keep = run_expert_grads(call, items, info, normed_two, ghid, "up_grads")
    sum_up = Sum(call, dp, tp, "up", send, keep)
    sum_down.middle()
    *branch_own, grad_mid, small_n = run_norm_two_back(
        call, items, info, totals, vecs, masked, part, part_far, middle
    )
    branch_other = [core_swap(b) for b in branch_own]
    gproj, small_a, small_o, one_own, one_got = [], [], [], [], []
    for k in range(chunks):
        g, sa, so, po, pt = run_attention_backward(
            call, k, heads, info, branch_own[k], branch_other[k], w_out, proj[k], w_t, kept[k]
        )
        for group, value in zip((gproj, small_a, small_o, one_own, one_got), (g, sa, so, po, core_swap(pt))):
            group.append(value)
    small = call(
        functools.partial(collect, heads, chunks),
        (small_n, small_c, *small_e, *small_a, *small_o),
        [arr((16, d), f32)],
        name="collect",
    )[0]
    send, keep = run_attention_grads(call, items, heads, branch_own, branch_other, gproj, normed_one, ctx)
    sum_attn = Sum(call, dp, tp, "attn", send, keep, small)
    sum_up.quarter()
    sum_down.back_half()
    one = run_pair(call, one_own, one_got, "one")
    one_far = far_swap(one)
    sum_up.middle()
    sum_attn.quarter()
    out_own = run_output_rows(call, items, info, down_bias, down, down_far, middle)
    out_other = core_swap(out_own)
    sum_down.back_whole()
    output = run_assemble(call, items, out_own, out_other, "output")
    grad_own = run_norm_one_back(call, items, vecs, grad_mid, one, one_far, kept)
    grad_other = core_swap(grad_own)
    sum_up.back_half()
    sum_attn.middle()
    grad_tokens = run_assemble(call, items, grad_own, grad_other, "grad_tokens")
    grad_down = run_whole(call, totals, sum_down.keep, sum_down.got, "down_whole", 20)
    sum_up.back_whole()
    sum_attn.back_half()
    small = sum_attn.rider
    norms = call(core_rows_kernel, (small, core_swap(small)), [arr((8, d), f32)], name="norm_rows")[0]
    norms_got = far_swap(norms)
    sum_attn.back_whole()
    smalls = run_small_outputs(call, heads, totals, small, norms, norms_got)
    grad_up = run_whole(call, totals, sum_up.keep, sum_up.got, "up_whole", 60)
    grad_qkv, grad_out = run_attention_whole(call, 3 * width, sum_attn.keep, sum_attn.got, "attn_whole")
    return (
        output,
        grad_tokens,
        smalls[3],
        smalls[4],
        grad_qkv.reshape(3, width, d).transpose(2, 0, 1),
        smalls[7],
        grad_out,
        smalls[2],
        smalls[0],
        smalls[1],
        grad_up.reshape(w_up.shape),
        smalls[5],
        grad_down.reshape(w_down.shape),
        smalls[6],
        totals[:2, 0].astype(jnp.int32),
    )


def solution(mesh):
    in_specs = (
        P("dp", None),
        P("dp"),
        P("dp"),
        P("dp", None),
        P(),
        P(),
        P(None, None, "tensor"),
        P(None, "tensor"),
        P("tensor", None),
        P(),
        P(),
        P(),
        P(None, None, "tensor"),
        P(None, "tensor"),
        P(None, "tensor", None),
        P(),
    )
    out_specs = (
        P("dp", None),
        P("dp", None),
        P(),
        P(),
        P(None, None, "tensor"),
        P(None, "tensor"),
        P("tensor", None),
        P(),
        P(),
        P(),
        P(None, None, "tensor"),
        P(None, "tensor"),
        P(None, "tensor", None),
        P(),
        P(),
    )
    return jax.shard_map(
        functools.partial(local, mesh.shape["dp"], mesh.shape["tensor"]),
        mesh=mesh,
        in_specs=in_specs,
        out_specs=out_specs,
        check_vma=False,
    )
```

```python
import functools

import jax
import jax.numpy as jnp
from jax import lax
from jax.experimental import pallas as pl
from jax.experimental.pallas import tpu as pltpu
from jax.sharding import PartitionSpec as P

HEAD = 64
PATCHES = 197
CAP = 40
SEQ = PATCHES + CAP
PAD = 240
ATT = 256
STAGE = 2 * SEQ + 32

epsilon = 1e-05
f32 = jnp.float32
bf16 = jnp.bfloat16

NT = (((1,), (1,)), ((), ()))
NN = (((1,), (0,)), ((), ()))
TN = (((0,), (0,)), ((), ()))

VMEM = pltpu.VMEM
SMEM = pltpu.SMEM
DMA = pltpu.SemaphoreType.DMA


def dot(a, b, dims=NN):
    return lax.dot_general(a, b, dims, preferred_element_type=f32)


def iota(shape, dim):
    return lax.broadcasted_iota(jnp.int32, shape, dim)


def unit_rows(x):
    mean = jnp.mean(x, -1, keepdims=True)
    centered = x - mean
    scale = lax.rsqrt(jnp.mean(centered * centered, -1, keepdims=True) + epsilon)
    return centered * scale, scale


def norm_back(grad, unit, scale, gain):
    t = grad * gain
    return scale * (
        t - jnp.mean(t, -1, keepdims=True) - unit * jnp.mean(t * unit, -1, keepdims=True)
    )


def vspec():
    return pl.BlockSpec(memory_space=VMEM)


def hspec():
    return pl.BlockSpec(memory_space=pltpu.HBM)


def aspec():
    return pl.BlockSpec(memory_space=pl.ANY)


class Order:
    def __init__(self):
        self.last = None

    def __call__(self, kernel, ins, outs, scratch=(), limit=16, specs=None, out_specs=None, name=None):
        taken = len(ins)
        behind = () if self.last is None or any(a is self.last for a in ins) else (self.last,)

        def body(*refs):
            kernel(*refs[:taken], *refs[taken + len(behind) :])

        results = pl.pallas_call(
            body,
            out_shape=list(outs),
            in_specs=list(specs or [vspec() for _ in ins]) + [aspec() for _ in behind],
            out_specs=list(out_specs or [vspec() for _ in outs]),
            scratch_shapes=list(scratch),
            compiler_params=pltpu.CompilerParams(vmem_limit_bytes=limit * 1024 * 1024),
            cost_estimate=pl.CostEstimate(flops=1, bytes_accessed=1, transcendentals=0),
            name=name,
        )(*ins, *behind)
        self.last = results[0]
        return results


def arr(shape, dtype):
    return jax.ShapeDtypeStruct(shape, dtype)


def position():
    return lax.axis_index("tensor")


def is_first():
    return lax.rem(position(), 2) == 0


def places():
    place = lax.axis_index("dp")
    low = lax.rem(place, 2)
    high = lax.rem(lax.div(place, 2), 2)
    first = is_first()
    return jnp.where(first, low, high), jnp.where(first, high, low)


def stage_rows(rows, buf, chunk):
    low = 2 * chunk * SEQ
    high = low + 2 * SEQ
    base = low // 16 * 16
    top = min(rows.shape[0], -(-high // 16) * 16)
    buf[0 : top - base] = rows[base:top].astype(f32)
    return [low - base, low - base + SEQ]


def item_rows(buf, offset, count, live=SEQ):
    rows = buf[pl.ds(offset, count), :]
    return jnp.where(iota(rows.shape, 0) < live, rows, 0.0)


def live_of(info, item):
    return info[item : item + 1, 0:1].astype(jnp.int32)


def expert_vector(info, items, item):
    return info[items + item : items + item + 1, 0:1]


def expert_of(info, items, item):
    return jnp.max(info[items + item : items + item + 1, :]).astype(jnp.int32)


def row_weight(counts):
    both = counts[0:1, 0:1] + counts[1:2, 0:1]
    return both / (2.0 * counts[0:1, 0:1]), both / (2.0 * counts[1:2, 0:1])


def attention_items(chunk, heads, info, rows, w_t, qv_bias, gain, bias, ctx, proj, normed, kept, buf):
    width = heads * HEAD
    offsets = stage_rows(rows, buf, chunk)
    b_three = jnp.concatenate([qv_bias[0:1, :], jnp.zeros((1, width), f32), qv_bias[1:2, :]], axis=1)
    for j in range(2):
        live = live_of(info, 2 * chunk + j)
        x = item_rows(buf, offsets[j], ATT)
        kept[j] = x[:PAD].astype(bf16)
        unit, _ = unit_rows(x)
        n_row = (unit * gain + bias).astype(bf16)
        normed[j] = n_row[:PAD]
        p_row = (dot(n_row, w_t[...], NT) + b_three).astype(bf16)
        proj[j] = p_row[:PAD]
        key_live = iota((ATT, ATT), 1) < live
        for h in range(heads):
            q = p_row[:, h * HEAD : (h + 1) * HEAD]
            k = p_row[:, width + h * HEAD : width + (h + 1) * HEAD]
            v = p_row[:, 2 * width + h * HEAD : 2 * width + (h + 1) * HEAD]
            s = jnp.where(key_live, dot(q, k, NT) * 0.125, -1e30)
            e = jnp.exp(s - jnp.max(s, -1, keepdims=True))
            att = (e * (1.0 / jnp.sum(e, -1, keepdims=True))).astype(bf16)
            c = dot(att, v).astype(bf16)
            at = j * width + h * HEAD
            ctx[:, at : at + HEAD] = c[:PAD]


def front(
    items, heads, mask_h, kind_h, tokens_h, w_h, qv_h, *refs
):
    vectors_h, refs = refs[:5], refs[5:]
    ctx, proj, normed, kept, info, counts, vecs = refs[:7]
    mask, kind, tokens, w_t, qv_bias, lines, buf, sems = refs[7:]
    pairs = [(mask_h, mask), (kind_h, kind), (tokens_h, tokens), (w_h, w_t), (qv_h, qv_bias)]
    pairs += [(v, lines.at[i]) for i, v in enumerate(vectors_h)]
    copies = [pltpu.make_async_copy(a, b, sems.at[i]) for i, (a, b) in enumerate(pairs)]
    for c in copies:
        c.start()
    copies[0].wait()
    copies[1].wait()
    total = 0
    second = 0
    row = iota(info.shape, 0)
    value = jnp.zeros(info.shape, f32)
    for i in range(items):
        n = PATCHES
        for slot in range(CAP):
            n = n + mask[i * SEQ + PATCHES + slot]
        e = kind[i * SEQ]
        total = total + n
        second = second + n * e
        value = jnp.where(row == i, n.astype(f32), value)
        value = jnp.where(row == items + i, e.astype(f32), value)
    info[...] = value
    row = iota(counts.shape, 0)
    counts[...] = jnp.where(row == 0, (total - second).astype(f32), second.astype(f32))
    for c in copies[2:]:
        c.wait()
    for i in range(5):
        vecs[i : i + 1, :] = lines[i : i + 1, :]
    attention_items(
        0, heads, info, tokens[...], w_t, qv_bias, lines[0:1, :], lines[1:2, :], ctx, proj, normed, kept, buf
    )


def run_front(call, items, heads, mask, kind, tokens, w_t, qv_bias, vectors):
    width = heads * HEAD
    rows, d = tokens.shape
    ins = (mask, kind, tokens, w_t, qv_bias, *vectors)
    return call(
        functools.partial(front, items, heads),
        ins,
        [
            arr((PAD, 2 * width), bf16),
            arr((2, PAD, 3 * width), bf16),
            arr((2, PAD, d), bf16),
            arr((2, PAD, d), bf16),
            arr((2 * items, 128), f32),
            arr((8, 128), f32),
            arr((8, d), f32),
        ],
        [
            SMEM(mask.shape, jnp.int32),
            SMEM(kind.shape, jnp.int32),
            VMEM(tokens.shape, bf16),
            VMEM(w_t.shape, bf16),
            VMEM(qv_bias.shape, f32),
            VMEM((8, d), f32),
            VMEM((STAGE, d), f32),
            DMA((len(ins),)),
        ],
        specs=[hspec() for _ in ins],
        limit=60,
        name="front",
    )


def attention_forward(chunk, heads, *refs):
    hbm, outs, local, sems = refs[:5], refs[5:9], refs[9:14], refs[15]
    copies = [pltpu.make_async_copy(a, b, sems.at[i]) for i, (a, b) in enumerate(zip(hbm, local))]
    for c in copies:
        c.start()
    for c in copies:
        c.wait()
    info, vecs, tokens, w_t, qv_bias = local
    attention_items(
        chunk, heads, info, tokens[...], w_t, qv_bias, vecs[0:1, :], vecs[1:2, :], *outs, refs[14]
    )


def run_attention_forward(call, chunk, heads, info, vecs, tokens, w_t, qv_bias):
    width = heads * HEAD
    d = tokens.shape[1]
    ins = (info, vecs, tokens, w_t, qv_bias)
    return call(
        functools.partial(attention_forward, chunk, heads),
        ins,
        [arr((PAD, 2 * width), bf16), arr((2, PAD, 3 * width), bf16), arr((2, PAD, d), bf16), arr((2, PAD, d), bf16)],
        [VMEM(a.shape, a.dtype) for a in ins] + [VMEM((STAGE, d), f32), DMA((len(ins),))],
        specs=[hspec() for _ in ins],
        limit=60,
        name="attention_forward_%d" % chunk,
    )


def mask_rows(items, info, cot, masked, small, buf):
    d = cot.shape[1]
    buf[0 : items * SEQ] = cot[...].astype(f32)
    zero = jnp.zeros((1, d), f32)
    sums = [zero, zero]
    for i in range(items):
        rows = item_rows(buf, i * SEQ, PAD, live_of(info, i))
        masked[i] = rows.astype(bf16)
        line = jnp.sum(rows, 0, keepdims=True)
        e = expert_vector(info, items, i)
        for x in range(2):
            sums[x] = sums[x] + jnp.where(e == x, line, 0.0)
    small[...] = jnp.zeros_like(small)
    small[0:1, :] = sums[0]
    small[1:2, :] = sums[1]


def run_mask_rows(call, items, info, cot):
    d = cot.shape[1]
    return call(
        functools.partial(mask_rows, items),
        (info, cot),
        [arr((items, PAD, d), bf16), arr((8, d), f32)],
        [VMEM((items * SEQ + 16, d), f32)],
        name="mask_rows",
    )


def gather_slots():
    t = position()
    core = lax.rem(t, 2)
    return (t, t + 1 - 2 * core, lax.rem(t + 2, 4), lax.rem(t + 3 - 2 * core, 4))


def pack_kernel(own, far, out):
    out[0] = own[...]
    out[1] = far[...]


def run_pack(call, own, far, name):
    return call(pack_kernel, (own, far), [arr((2, *own.shape), own.dtype)], name=name)[0]


def put_slots(out, both, got):
    t, near, far, across = gather_slots()
    out[t] = both[0]
    out[far] = both[1]
    out[near] = got[0]
    out[across] = got[1]


def slot_kernel(both, got, out):
    put_slots(out, both, got)


def run_slots(call, both, got, name):
    return call(slot_kernel, (both, got), [arr((4, *both.shape[1:]), both.dtype)], name=name)[0]


def gelu_parts(h):
    cdf = 0.5 * (1.0 + lax.erf(h * 0.7071067811865476))
    density = jnp.exp(-0.5 * h * h) * 0.3989422804014327
    return h * cdf, cdf + h * density


def experts(chunk, items, heads, last, info, vecs, kept, masked, both, got, w_out, up_bias, w_up, w_down, *refs):
    width = heads * HEAD
    d = kept.shape[2]
    before, refs = (refs[: 4 * chunk], refs[4 * chunk :]) if last else ((), refs)
    middle, normed, active, ghid, small = refs[:5]
    sides = refs[5:9]
    ctx = refs[9]
    first = is_first()
    put_slots(ctx, both, got)
    mids, n_rows = [], []
    for j in range(2):
        total = jnp.zeros((PAD, d), f32)
        for s in range(4):
            total = total + dot(ctx[s][:, j * width : (j + 1) * width], w_out[s])
        mid = kept[j].astype(f32) + total + vecs[2:3, :]
        mids.append(mid)
        unit, _ = unit_rows(mid)
        n_row = (unit * vecs[3:4, :] + vecs[4:5, :]).astype(bf16)
        normed[j] = n_row
        n_rows.append(n_row)
    middle[...] = jnp.where(first, mids[0], mids[1])
    parts, downs = [], []
    zero = jnp.zeros((1, w_up.shape[2]), f32)
    sums = [zero, zero]
    for j in range(2):
        e = expert_of(info, items, 2 * chunk + j)
        wu = w_up[e]
        wd = w_down[e]
        h = dot(n_rows[j], wu) + up_bias[pl.ds(e, 1), :]
        value, slope = gelu_parts(h)
        act = value.astype(bf16)
        active[j] = act
        gh = (dot(masked[2 * chunk + j], wd, NT) * slope).astype(bf16)
        ghid[j] = gh
        parts.append(dot(gh, wu, NT))
        downs.append(dot(act, wd))
        line = jnp.sum(gh.astype(f32), 0, keepdims=True)
        flag = expert_vector(info, items, 2 * chunk + j)
        for x in range(2):
            sums[x] = sums[x] + jnp.where(flag == x, line, 0.0)
    small[...] = jnp.zeros_like(small)
    small[0:1, :] = sums[0]
    small[1:2, :] = sums[1]
    values = (
        jnp.where(first, parts[0], parts[1]),
        jnp.where(first, parts[1], parts[0]),
        jnp.where(first, downs[0], downs[1]),
        jnp.where(first, downs[1], downs[0]),
    )
    for i, (side, value) in enumerate(zip(sides, values)):
        if last:
            for k in range(chunk):
                side[k] = before[4 * k + i][...]
            side[chunk] = value.astype(bf16)
        else:
            side[...] = value.astype(bf16)


def run_experts(call, chunk, items, heads, info, vecs, kept, masked, ctxs, w_out, up_bias, w_up, w_down, before):
    width = heads * HEAD
    d = kept.shape[2]
    ff = w_up.shape[2]
    last = chunk == items // 2 - 1
    side = arr((chunk + 1, PAD, d), bf16) if last else arr((PAD, d), bf16)
    return call(
        functools.partial(experts, chunk, items, heads, last),
        (info, vecs, kept, masked, *ctxs, w_out, up_bias, w_up, w_down, *(before if last else ())),
        [
            arr((PAD, d), f32),
            arr((2, PAD, d), bf16),
            arr((2, PAD, ff), bf16),
            arr((2, PAD, ff), bf16),
            arr((8, d), f32),
        ]
        + [side] * 4,
        [VMEM((4, PAD, 2 * width), bf16)],
        limit=20,
        name="experts_%d" % chunk,
    )


def expert_grads(items, merged, info, *refs):
    chunks = items // 2
    lefts, refs = refs[:chunks], refs[chunks:]
    rights = refs[: 1 if merged else chunks]
    send, keep, total = refs[len(rights) :]
    for i in range(items):
        e = expert_of(info, items, i)
        right = rights[0][i] if merged else rights[i // 2][i % 2]
        term = dot(lefts[i // 2][i % 2], right, TN)
        if i == 0:
            total[e] = term
            total[1 - e] = jnp.zeros_like(term)
        else:
            total[e] += term
    one, _ = places()
    keep[...] = total[one].astype(bf16)
    send[...] = total[1 - one].astype(bf16)


def run_expert_grads(call, items, info, lefts, rights, name):
    merged = len(rights) == 1
    shape = (lefts[0].shape[2], rights[0].shape[2])
    return call(
        functools.partial(expert_grads, items, merged),
        (info, *lefts, *rights),
        [arr(shape, bf16)] * 2,
        [VMEM((2, *shape), f32)],
        name=name,
    )


def own_expert(info, items, chunk):
    return jnp.where(is_first(), expert_vector(info, items, 2 * chunk), expert_vector(info, items, 2 * chunk + 1))


def item_weight(info, items, item, counts):
    first, second = row_weight(counts)
    return jnp.where(expert_vector(info, items, item) == 0, first, second)


def own_weight(info, items, chunk, counts):
    first, second = row_weight(counts)
    return jnp.where(own_expert(info, items, chunk) == 0, first, second)


def norm_two_back(chunks, vecs, masked, pair, far, *refs):
    middles, branch, (grad_mid, small) = refs[:chunks], refs[chunks : 2 * chunks], refs[2 * chunks :]
    small[...] = jnp.zeros_like(small)
    for k in range(chunks):
        own_cot = jnp.where(is_first(), masked[2 * k], masked[2 * k + 1]).astype(f32)
        unit, scale = unit_rows(middles[k][...])
        grad = pair[k].astype(f32) + far[k].astype(f32)
        out = own_cot + norm_back(grad, unit, scale, vecs[3:4, :])
        grad_mid[k] = out
        branch[k][...] = out.astype(bf16)
        for i, value in enumerate((grad * unit, grad, out)):
            small[3 * k + i : 3 * k + i + 1, :] = jnp.sum(value, 0, keepdims=True)


def run_norm_two_back(call, vecs, masked, pair, far, middles):
    chunks = len(middles)
    return call(
        functools.partial(norm_two_back, chunks),
        (vecs, masked, pair, far, *middles),
        [arr(pair.shape[1:], bf16)] * chunks
        + [arr(pair.shape, f32), arr((-(-3 * chunks // 8) * 8, pair.shape[2]), f32)],
        name="norm_two_back",
    )


def attention_backward(
    chunk, items, heads, info, counts, own, other, w_out, proj, w_t, kept,
    gproj, small, small_one, part_own, part_other,
):
    width = heads * HEAD
    first = is_first()
    parts = []
    d = w_t.shape[1]
    sums = [jnp.zeros((1, d), f32)] * 2
    total = jnp.zeros((1, 3 * width), f32)
    for j in range(2):
        live = live_of(info, 2 * chunk + j)
        a, b = (own, other) if j == 0 else (other, own)
        branch = jnp.where(first, a[...], b[...])
        gctx = dot(branch, w_out[...], NT).astype(bf16)
        p_row = proj[j]
        key_live = iota((PAD, PAD), 1) < live
        gq, gk, gv = [], [], []
        for h in range(heads):
            q = p_row[:, h * HEAD : (h + 1) * HEAD]
            k = p_row[:, width + h * HEAD : width + (h + 1) * HEAD]
            v = p_row[:, 2 * width + h * HEAD : 2 * width + (h + 1) * HEAD]
            gc = gctx[:, h * HEAD : (h + 1) * HEAD]
            s = jnp.where(key_live, dot(q, k, NT) * 0.125, -1e30)
            e = jnp.exp(s - jnp.max(s, -1, keepdims=True))
            att = e * (1.0 / jnp.sum(e, -1, keepdims=True))
            ga = dot(gc, v, NT)
            gs = (att * (ga - jnp.sum(ga * att, -1, keepdims=True))).astype(bf16)
            gv.append(dot(att.astype(bf16), gc, TN))
            gq.append(dot(gs, k) * 0.125)
            gk.append(dot(gs, q, TN) * 0.125)
        weight = item_weight(info, items, 2 * chunk + j, counts)
        gp = (jnp.concatenate(gq + gk + gv, axis=1) * weight).astype(bf16)
        gproj[j] = gp
        total = total + jnp.sum(gp.astype(f32), 0, keepdims=True)
        part = dot(gp, w_t[...])
        parts.append(part)
        unit, _ = unit_rows(kept[j].astype(f32))
        sums[0] = sums[0] + jnp.sum(part * unit, 0, keepdims=True)
        sums[1] = sums[1] + jnp.sum(part, 0, keepdims=True)
    small[...] = jnp.zeros_like(small)
    small[0:1, :] = total
    small_one[...] = jnp.zeros_like(small_one)
    for i in range(2):
        small_one[i : i + 1, :] = sums[i]
    part_own[...] = jnp.where(first, parts[0], parts[1]).astype(bf16)
    part_other[...] = jnp.where(first, parts[1], parts[0]).astype(bf16)


def run_attention_backward(call, chunk, items, heads, info, counts, own, other, w_out, proj, w_t, kept):
    width = heads * HEAD
    d = own.shape[1]
    side = arr((PAD, d), bf16)
    return call(
        functools.partial(attention_backward, chunk, items, heads),
        (info, counts, own, other, w_out, proj, w_t, kept),
        [arr((2, PAD, 3 * width), bf16), arr((8, 3 * width), f32), arr((8, d), f32), side, side],
        name="attention_backward_%d" % chunk,
    )


def attention_grads(items, heads, info, counts, *refs):
    width = heads * HEAD
    chunks = items // 2
    own, other, gproj, normed, ctx = (refs[i * chunks : (i + 1) * chunks] for i in range(5))
    send, keep, both = refs[5 * chunks :]
    first = is_first()
    rows = 3 * width
    total = jnp.zeros((rows, keep.shape[1]), f32)
    total_out = jnp.zeros((width, keep.shape[1]), f32)
    for k in range(chunks):
        for j in range(2):
            total = total + dot(gproj[k][j], normed[k][j], TN)
            a, b = (own, other) if j == 0 else (other, own)
            branch = jnp.where(first, a[k][...], b[k][...]).astype(f32)
            branch = (branch * item_weight(info, items, 2 * k + j, counts)).astype(bf16)
            total_out = total_out + dot(ctx[k][:, j * width : (j + 1) * width], branch, TN)
    half = 2 * width
    both[0] = total[:half].astype(bf16)
    both[1, 0 : rows - half] = total[half:].astype(bf16)
    both[1, rows - half :] = total_out.astype(bf16)
    one, _ = places()
    keep[...] = both[one]
    send[...] = both[1 - one]


def run_attention_grads(call, items, heads, info, counts, own, other, gproj, normed, ctx):
    width = heads * HEAD
    d = own[0].shape[1]
    return call(
        functools.partial(attention_grads, items, heads),
        (info, counts, *own, *other, *gproj, *normed, *ctx),
        [arr((2 * width, d), bf16)] * 2,
        [VMEM((2, 2 * width, d), bf16)],
        name="attention_grads",
    )


def norm_one_back(items, info, counts, vecs, grad_mid, pair, far, *refs):
    chunks = items // 2
    kept, grad_own = refs[:chunks], refs[chunks]
    for k in range(chunks):
        x = jnp.where(is_first(), kept[k][0], kept[k][1]).astype(f32)
        unit, scale = unit_rows(x)
        grad = pair[k].astype(f32) + far[k].astype(f32)
        mid = grad_mid[k] * own_weight(info, items, k, counts)
        grad_own[k] = (mid + norm_back(grad, unit, scale, vecs[0:1, :])).astype(bf16)


def run_norm_one_back(call, items, info, counts, vecs, grad_mid, pair, far, kept):
    return call(
        functools.partial(norm_one_back, items),
        (info, counts, vecs, grad_mid, pair, far, *kept),
        [arr(pair.shape, bf16)],
        name="norm_one_back",
    )[0]


def output_rows(items, info, down_bias, pair, far, *refs):
    chunks = items // 2
    middles, out = refs[:chunks], refs[chunks]
    for k in range(chunks):
        bias = jnp.where(own_expert(info, items, k) == 0, down_bias[0:1, :], down_bias[1:2, :])
        out[k] = (middles[k][...] + (pair[k].astype(f32) + far[k].astype(f32)) + bias).astype(bf16)


def run_output_rows(call, items, info, down_bias, pair, far, middles):
    return call(
        functools.partial(output_rows, items),
        (info, down_bias, pair, far, *middles),
        [arr(pair.shape, bf16)],
        name="output_rows",
    )[0]


def assemble(items, own, other, out, buf, low, sem):
    first = is_first()
    for k in range(items // 2):
        for j in range(2):
            a, b = (own, other) if j == 0 else (other, own)
            buf[pl.ds((2 * k + j) * SEQ, PAD), :] = jnp.where(first, a[k], b[k]).astype(f32)
    low[...] = buf[0 : items * SEQ, :].astype(bf16)
    copy = pltpu.make_async_copy(low, out, sem)
    copy.start()
    copy.wait()


def run_assemble(call, items, own, other, name):
    d = own.shape[2]
    return call(
        functools.partial(assemble, items),
        (own, other),
        [arr((items * SEQ, d), bf16)],
        [VMEM((items * SEQ + 16, d), f32), VMEM((items * SEQ, d), bf16), DMA],
        out_specs=[hspec()],
        name=name,
    )[0]


def swap(value, axis, size, bit):
    return lax.ppermute(value, axis, [(i, i ^ bit) for i in range(size)])


def add_kernel(a, b, out):
    out[...] = (a[...].astype(f32) + b[...].astype(f32)).astype(out.dtype)


def run_add(call, a, b, name):
    return call(add_kernel, (a, b), [arr(a.shape, a.dtype)], name=name)[0]


def hand_kernel(a, b, given, out, handed):
    out[...] = a[...] + b[...]
    handed[...] = given[...]


def run_add_and_hand(call, a, b, given, name):
    return call(hand_kernel, (a, b, given), [arr(a.shape, a.dtype), arr(given.shape, given.dtype)], name=name)


def pair_kernel(chunks, *refs):
    own, got, out = refs[:chunks], refs[chunks : 2 * chunks], refs[2 * chunks]
    for k in range(chunks):
        out[k] = (own[k][...].astype(f32) + got[k][...].astype(f32)).astype(bf16)


def run_pair(call, own, got, name):
    return call(
        functools.partial(pair_kernel, len(own)), (*own, *got), [arr((len(own), *own[0].shape), bf16)], name=name
    )[0]


TAIL = 16


def split_rows(rows):
    high = rows.astype(bf16)
    return high, (rows - high.astype(f32)).astype(bf16)


def add_tail(held, got, at):
    return held[...] + got[at : at + TAIL].astype(f32) + got[at + TAIL : at + 2 * TAIL].astype(f32)


def put_tail(out, at, rows):
    out[at : at + TAIL], out[at + TAIL : at + 2 * TAIL] = split_rows(rows)


def attach_kernel(rows, tail, out):
    count = rows.shape[0]
    out[0:count] = rows[...]
    put_tail(out, count, tail[...])


def half_of(ref, index, count):
    return ref[pl.ds(pl.multiple_of(index * count, count), count), :]


def fold_step(tailed, keep, got, *refs):
    refs = list(refs)
    held = refs.pop(0) if tailed else None
    send_next, keep_next = refs[:2]
    count = keep_next.shape[0]
    _, two = places()
    for out, index in ((keep_next, two), (send_next, 1 - two)):
        total = half_of(keep, index, count).astype(f32) + half_of(got, index, count).astype(f32)
        out[0:count] = total.astype(bf16)
    if tailed:
        tail = add_tail(held, got, 2 * count)
        refs[2][...] = tail
        put_tail(send_next, count, tail)


def add_step(tailed, handed, sends, keep, got, *refs):
    refs = list(refs)
    held = refs.pop(0) if tailed else None
    given = [refs.pop(0) for _ in range(handed)]
    out = refs.pop(0)
    count = out.shape[0]
    total = (keep[...].astype(f32) + got[0:count].astype(f32)).astype(bf16)
    out[...] = total
    if tailed:
        tail = add_tail(held, got, count)
        refs.pop(0)[...] = tail
        if sends:
            send = refs.pop(0)
            send[0:count] = total
            put_tail(send, count, tail)
    if handed == 1:
        refs[0][...] = given[0][...]
    if handed == 2:
        attach_kernel(given[0], given[1], refs[0])


def join_kernel(own, other, out):
    _, bit = places()
    out[bit] = own[...]
    out[1 - bit] = other[...]


PIECES = 4


def whole_kernel(scaled, *refs):
    counts = refs[0] if scaled else None
    own, other, out, buf, sems = refs[1:] if scaled else refs
    bit, _ = places()
    rows = own.shape[0] // PIECES
    copies = []
    for side, ref in enumerate((own, other)):
        half = bit if side == 0 else 1 - bit
        weight = 1.0
        if scaled:
            first, second = row_weight(counts)
            weight = jnp.where(half == 0, first, second)
        for i in range(PIECES):
            at = pl.ds(i * rows, rows)
            buf[side, at] = ref[at].astype(f32) * weight
            copy = pltpu.make_async_copy(buf.at[side, at], out.at[half, at], sems.at[side, i])
            copy.start()
            copies.append(copy)
    for copy in copies:
        copy.wait()


def run_whole(call, counts, own, other, name, limit):
    scaled = counts is not None
    shape = (2, *own.shape)
    return call(
        functools.partial(whole_kernel, scaled),
        ((counts,) if scaled else ()) + (own, other),
        [arr(shape, f32)],
        [VMEM(shape, f32), DMA((2, PIECES))],
        out_specs=[hspec()],
        limit=limit,
        name=name,
    )[0]


def attention_whole_kernel(rows, own, other, grad_qkv, grad_out, low, buf, sems):
    bit, _ = places()
    half = own.shape[0]
    low[bit] = own[...]
    low[1 - bit] = other[...]
    copies = []
    spans = [(grad_qkv, 0, 0, half), (grad_qkv, 1, half, rows - half), (grad_out, 1, 0, 2 * half - rows)]
    start = [0, 0, rows - half]
    for i, (out, side, to, count) in enumerate(spans):
        at = pl.ds(start[i], count)
        buf[side, at] = low[side, at].astype(f32)
        copy = pltpu.make_async_copy(buf.at[side, at], out.at[pl.ds(to, count)], sems.at[i])
        copy.start()
        copies.append(copy)
    for copy in copies:
        copy.wait()


def run_attention_whole(call, rows, own, other, name):
    half, d = own.shape
    return call(
        functools.partial(attention_whole_kernel, rows),
        (own, other),
        [arr((rows, d), f32), arr((2 * half - rows, d), f32)],
        [VMEM((2, half, d), bf16), VMEM((2, half, d), f32), DMA((3,))],
        out_specs=[hspec(), hspec()],
        limit=60,
        name=name,
    )


class Sum:
    def __init__(self, call, dp, tp, name, keep, tail=None):
        self.call, self.dp, self.tp, self.name, self.keep, self.tail = call, dp, tp, name, keep, tail

    def start(self, send):
        if self.dp == 8:
            self.got = self.cross(send, (1, 2))
            return
        keep = self.keep
        send = send[: keep.shape[0]]
        low = (lax.axis_index("dp") % 2).astype(jnp.int32)
        high = (lax.axis_index("dp") // 2 % 2).astype(jnp.int32)
        one = jnp.where(lax.axis_index("tensor") % 2 == 0, low, high)
        flat = jnp.where(one == 0, jnp.concatenate([keep, send]), jnp.concatenate([send, keep]))
        share = lax.psum_scatter(flat, "dp", scatter_dimension=0, tiled=True)
        whole = lax.all_gather(share, "dp", axis=0, tiled=True).reshape(2, *keep.shape)
        self.keep = jnp.where(one == 0, whole[0], whole[1])
        self.got = jnp.where(one == 0, whole[1], whole[0])
        if self.tail is not None:
            self.tail = lax.psum(self.tail, "dp")

    def cross(self, value, bits):
        dp, tp = self.dp, self.tp
        route = [(i * tp + t, (i ^ bits[t % 2]) * tp + t) for i in range(dp) for t in range(tp)]
        return lax.ppermute(value, ("dp", "tensor"), route)

    def quarter(self):
        if self.dp != 8:
            return
        rows, d = self.keep.shape
        tailed = self.tail is not None
        ins = (self.keep, self.got) + ((self.tail,) if tailed else ())
        outs = [arr((rows // 2 + (2 * TAIL if tailed else 0), d), bf16), arr((rows // 2, d), bf16)]
        outs += [arr(self.tail.shape, f32)] if tailed else []
        send, self.keep, *tail = self.call(
            functools.partial(fold_step, tailed), ins, outs, name=self.name + "_half"
        )
        self.tail = tail[0] if tailed else None
        self.got = self.cross(send, (2, 1))

    def add(self, name, sends, handed):
        tailed = self.tail is not None
        rows, d = self.keep.shape
        ins = (self.keep, self.got) + ((self.tail,) if tailed else ()) + handed
        outs = [arr((rows, d), bf16)]
        outs += [arr(self.tail.shape, f32)] if tailed else []
        outs += [arr((rows + 2 * TAIL, d), bf16)] if tailed and sends else []
        if handed:
            outs.append(arr((handed[0].shape[0] + 2 * TAIL * (len(handed) - 1), d), bf16))
        out = self.call(
            functools.partial(add_step, tailed, len(handed), sends), ins, outs, name=self.name + name
        )
        self.keep = out[0]
        if tailed:
            self.tail = out[1]
        return out[2] if tailed and sends else out[0], out[-1]

    def middle(self, *handed):
        if self.dp != 8:
            return handed[0] if handed else None
        send, given = self.add("_quarter", True, handed)
        self.got = self.cross(send, (4, 4))
        return given

    def back_half(self):
        if self.dp != 8:
            return
        self.add("_sum", False, ())
        self.got = self.cross(self.keep, (2, 1))

    def back_whole(self):
        if self.dp != 8:
            return
        rows, d = self.keep.shape
        out = self.call(join_kernel, (self.keep, self.got), [arr((2, rows, d), bf16)], name=self.name + "_join")[0]
        self.keep = out.reshape(2 * rows, d)
        self.got = self.cross(self.keep, (1, 2))


def collect(items, heads, info, counts, two, cots, *refs):
    width = heads * HEAD
    chunks = items // 2
    exp, attn, one = (refs[i * chunks : (i + 1) * chunks] for i in range(3))
    (out,) = refs[3 * chunks :]
    out[...] = jnp.zeros_like(out)
    weights = [own_weight(info, items, k, counts) for k in range(chunks)]
    out[0:3, :] = sum(two[3 * k : 3 * k + 3, :] * weights[k] for k in range(chunks)) * 0.5
    out[3:5, :] = sum(r[0:2, :] for r in one)
    out[8:10, :] = sum(r[0:2, :] for r in exp)
    out[10:12, :] = cots[0:2, :]
    out[12:13, 0 : 3 * width] = sum(r[0:1, :] for r in attn)


def small_outputs(heads, counts, small, *outs):
    width = heads * HEAD
    d = small.shape[1]
    for i in range(5):
        outs[i][...] = small[i : i + 1, :].reshape(d)
    for i, weight in enumerate(row_weight(counts)):
        outs[5][i : i + 1, :] = small[8 + i : 9 + i, :] * weight
        outs[6][i : i + 1, :] = small[10 + i : 11 + i, :] * weight
    row = small[12:13, :]
    outs[7][0:1, :] = row[:, 0:width]
    outs[7][1:2, :] = row[:, 2 * width : 3 * width]


def run_small_outputs(call, heads, counts, small):
    d = small.shape[1]
    return call(
        functools.partial(small_outputs, heads),
        (counts, small),
        [arr((d,), f32)] * 5 + [arr((2, d), f32)] * 2 + [arr((2, heads * HEAD), f32)],
        name="small_outputs",
    )


def row_sum_kernel(small, got, out):
    out[0:8, :] = small[0:8, :] + got[0:8, :]
    out[8:, :] = small[8:, :]


def run_row_sum(call, small, got, name):
    return call(row_sum_kernel, (small, got), [arr(small.shape, f32)], name=name)[0]


def local(
    dp, tp,
    tokens, token_mask, expert_type, cotangent, ln1_gain, ln1_bias, w_qkv, qv_bias, w_out, out_bias,
    ln2_gain, ln2_bias, w_up, up_bias, w_down, down_bias,
):
    rows, d = tokens.shape
    items = rows // SEQ
    width = w_qkv.shape[2]
    heads = width // HEAD
    core_swap = lambda v: swap(v, "tensor", tp, 1)
    far_swap = lambda v: swap(v, "tensor", tp, 2)
    chunks = items // 2
    call = Order()
    w_t = w_qkv.transpose(1, 2, 0).reshape(3 * width, d)

    w_far = far_swap(w_out)
    c0, p, n, x, info, totals, vecs = run_front(
        call, items, heads, token_mask, expert_type, tokens, w_t, qv_bias,
        (ln1_gain, ln1_bias, out_bias, ln2_gain, ln2_bias),
    )
    ctx, proj, normed_one, kept, ctx_far, ctxs = [c0], [p], [n], [x], [far_swap(c0)], []
    came = swap(totals, "dp", dp, 1)
    for k in range(1, chunks):
        c0, p, n, x = run_attention_forward(call, k, heads, info, vecs, tokens, w_t, qv_bias)
        if k == 1:
            totals, c0 = run_add_and_hand(call, totals, came, c0, "count_1")
            came = swap(totals, "dp", dp, 2)
        for group, value in zip((ctx, proj, normed_one, kept, ctx_far), (c0, p, n, x, far_swap(c0))):
            group.append(value)
    both = run_pack(call, ctx[0], ctx_far[0], "context_pack_0")
    ctxs.append((both, core_swap(both)))
    w_both = run_pack(call, w_out, w_far, "w_out_pack")
    w_got = core_swap(w_both)
    masked, small_c = run_mask_rows(call, items, info, cotangent)
    w_all = run_slots(call, w_both, w_got, "w_out_all")
    totals = run_add(call, totals, came, "count_2")
    bit = 4
    came = swap(totals, "dp", dp, bit)
    for k in range(1, chunks):
        both = run_pack(call, ctx[k], ctx_far[k], "context_pack_%d" % k)
        ctxs.append((both, core_swap(both)))

    middle, normed_two, active, ghid, small_e, before = [], [], [], [], [], []
    for k in range(chunks):
        out = run_experts(
            call, k, items, heads, info, vecs, kept[k], masked, ctxs[k], w_all, up_bias, w_up, w_down, before
        )
        for group, value in zip((middle, normed_two, active, ghid, small_e), out[:5]):
            group.append(value)
        before += list(out[5:])
        while k == 0 and bit < dp:
            totals = run_add(call, totals, came, "count_%d" % bit)
            bit = 2 * bit
            came = swap(totals, "dp", dp, bit) if bit < dp else None
    part_own, part_other, down_own, down_other = before[-4:]
    part_got = core_swap(part_other)
    down_got = core_swap(down_other)

    send, keep = run_expert_grads(call, items, info, active, [masked], "down_grads")
    sum_down = Sum(call, dp, tp, "down", keep)
    sum_down.start(send)
    part = run_add(call, part_own, part_got, "part")
    part_far = far_swap(part)
    down = run_add(call, down_own, down_got, "expert_rows")
    down_far = far_swap(down)
    up_send, up_keep = run_expert_grads(call, items, info, normed_two, ghid, "up_grads")
    sum_up = Sum(call, dp, tp, "up", up_keep)
    sum_down.quarter()
    *branch_own, grad_mid, small_n = run_norm_two_back(call, vecs, masked, part, part_far, middle)
    branch_other = [core_swap(b) for b in branch_own]
    up_send = sum_down.middle(up_send)
    sum_up.start(up_send)
    gproj, small_a, small_o, one_own, one_got = [], [], [], [], []
    for k in range(chunks):
        g, sa, so, po, pt = run_attention_backward(
            call, k, items, heads, info, totals, branch_own[k], branch_other[k], w_out, proj[k], w_t, kept[k]
        )
        for group, value in zip((gproj, small_a, small_o, one_own, one_got), (g, sa, so, po, core_swap(pt))):
            group.append(value)
    small = call(
        functools.partial(collect, items, heads),
        (info, totals, small_n, small_c, *small_e, *small_a, *small_o),
        [arr((16, d), f32)],
        name="collect",
    )[0]
    attn_send, keep = run_attention_grads(
        call, items, heads, info, totals, branch_own, branch_other, gproj, normed_one, ctx
    )
    small_got = core_swap(small)
    sum_up.quarter()
    sum_down.back_half()
    small = run_row_sum(call, small, small_got, "norm_rows_core")
    small_far = far_swap(small)
    one = run_pair(call, one_own, one_got, "one")
    one_far = far_swap(one)
    small = run_row_sum(call, small, small_far, "norm_rows_far")
    sum_attn = Sum(call, dp, tp, "attn", keep, tail=small)
    attn_send = sum_up.middle(attn_send, small)
    sum_attn.start(attn_send)
    sum_down.back_whole()
    sum_attn.quarter()
    grad_own = run_norm_one_back(call, items, info, totals, vecs, grad_mid, one, one_far, kept)
    grad_other = core_swap(grad_own)
    sum_up.back_half()
    sum_attn.middle()
    out_own = run_output_rows(call, items, info, down_bias, down, down_far, middle)
    out_other = core_swap(out_own)
    grad_tokens = run_assemble(call, items, grad_own, grad_other, "grad_tokens")
    sum_up.back_whole()
    output = run_assemble(call, items, out_own, out_other, "output")
    sum_attn.back_half()
    sum_attn.back_whole()
    smalls = run_small_outputs(call, heads, totals, sum_attn.tail)
    grad_down = run_whole(call, totals, sum_down.keep, sum_down.got, "down_whole", 20)
    grad_up = run_whole(call, totals, sum_up.keep, sum_up.got, "up_whole", 60)
    grad_qkv, grad_out = run_attention_whole(call, 3 * width, sum_attn.keep, sum_attn.got, "attn_whole")
    return (
        output,
        grad_tokens,
        smalls[3],
        smalls[4],
        grad_qkv.reshape(3, width, d).transpose(2, 0, 1),
        smalls[7],
        grad_out,
        smalls[2],
        smalls[0],
        smalls[1],
        grad_up.reshape(w_up.shape),
        smalls[5],
        grad_down.reshape(w_down.shape),
        smalls[6],
        totals[:2, 0].astype(jnp.int32),
    )


def solution(mesh):
    in_specs = (
        P("dp", None),
        P("dp"),
        P("dp"),
        P("dp", None),
        P(),
        P(),
        P(None, None, "tensor"),
        P(None, "tensor"),
        P("tensor", None),
        P(),
        P(),
        P(),
        P(None, None, "tensor"),
        P(None, "tensor"),
        P(None, "tensor", None),
        P(),
    )
    out_specs = (
        P("dp", None),
        P("dp", None),
        P(),
        P(),
        P(None, None, "tensor"),
        P(None, "tensor"),
        P("tensor", None),
        P(),
        P(),
        P(),
        P(None, None, "tensor"),
        P(None, "tensor"),
        P(None, "tensor", None),
        P(),
        P(),
    )
    return jax.shard_map(
        functools.partial(local, mesh.shape["dp"], mesh.shape["tensor"]),
        mesh=mesh,
        in_specs=in_specs,
        out_specs=out_specs,
        check_vma=False,
    )
```

```python
import functools

import jax
import jax.numpy as jnp
from jax import lax
from jax.experimental import pallas as pl
from jax.experimental.pallas import tpu as pltpu
from jax.sharding import PartitionSpec as P

HEAD = 64
PATCHES = 197
CAP = 40
SEQ = PATCHES + CAP
PAD = 240
ATT = 256
STAGE = 2 * SEQ + 32
TAIL = 16

epsilon = 1e-05
f32 = jnp.float32
bf16 = jnp.bfloat16

NT = (((1,), (1,)), ((), ()))
NN = (((1,), (0,)), ((), ()))
TN = (((0,), (0,)), ((), ()))

VMEM = pltpu.VMEM
SMEM = pltpu.SMEM
DMA = pltpu.SemaphoreType.DMA


def dot(a, b, dims=NN):
    return lax.dot_general(a, b, dims, preferred_element_type=f32)


def iota(shape, dim):
    return lax.broadcasted_iota(jnp.int32, shape, dim)


def unit_rows(x):
    mean = jnp.mean(x, -1, keepdims=True)
    centered = x - mean
    scale = lax.rsqrt(jnp.mean(centered * centered, -1, keepdims=True) + epsilon)
    return centered * scale, scale


def norm_back(grad, unit, scale, gain):
    t = grad * gain
    return scale * (
        t - jnp.mean(t, -1, keepdims=True) - unit * jnp.mean(t * unit, -1, keepdims=True)
    )


def vspec():
    return pl.BlockSpec(memory_space=VMEM)


def hspec():
    return pl.BlockSpec(memory_space=pltpu.HBM)


def aspec():
    return pl.BlockSpec(memory_space=pl.ANY)


class Order:
    def __init__(self):
        self.last = None

    def __call__(self, kernel, ins, outs, scratch=(), limit=16, specs=None, out_specs=None, name=None):
        taken = len(ins)
        behind = () if self.last is None or any(a is self.last for a in ins) else (self.last,)

        def body(*refs):
            kernel(*refs[:taken], *refs[taken + len(behind) :])

        results = pl.pallas_call(
            body,
            out_shape=list(outs),
            in_specs=list(specs or [vspec() for _ in ins]) + [aspec() for _ in behind],
            out_specs=list(out_specs or [vspec() for _ in outs]),
            scratch_shapes=list(scratch),
            compiler_params=pltpu.CompilerParams(vmem_limit_bytes=limit * 1024 * 1024),
            cost_estimate=pl.CostEstimate(flops=1, bytes_accessed=1, transcendentals=0),
            name=name,
        )(*ins, *behind)
        self.last = results[0]
        return results


def arr(shape, dtype):
    return jax.ShapeDtypeStruct(shape, dtype)


def position():
    return lax.axis_index("tensor")


def is_first():
    return lax.rem(position(), 2) == 0


def places(turned):
    place = lax.axis_index("dp")
    low = lax.rem(place, 2)
    high = lax.rem(lax.div(place, 2), 2)
    if not turned:
        return low, high
    first = is_first()
    return jnp.where(first, low, high), jnp.where(first, high, low)


def stage_rows(rows, buf, chunk):
    low = 2 * chunk * SEQ
    high = low + 2 * SEQ
    base = low // 16 * 16
    top = min(rows.shape[0], -(-high // 16) * 16)
    buf[0 : top - base] = rows[base:top].astype(f32)
    return [low - base, low - base + SEQ]


def item_rows(buf, offset, count, live=SEQ):
    rows = buf[pl.ds(offset, count), :]
    return jnp.where(iota(rows.shape, 0) < live, rows, 0.0)


def live_of(info, item):
    return info[item : item + 1, 0:1].astype(jnp.int32)


def expert_vector(info, items, item):
    return info[items + item : items + item + 1, 0:1]


def expert_of(info, items, item):
    return jnp.max(info[items + item : items + item + 1, :]).astype(jnp.int32)


def row_weight(counts):
    both = counts[0:1, 0:1] + counts[1:2, 0:1]
    return both / (2.0 * counts[0:1, 0:1]), both / (2.0 * counts[1:2, 0:1])


def attention_items(chunk, heads, info, rows, w_t, qv_bias, gain, bias, ctx, proj, normed, kept, buf):
    width = heads * HEAD
    offsets = stage_rows(rows, buf, chunk)
    b_three = jnp.concatenate([qv_bias[0:1, :], jnp.zeros((1, width), f32), qv_bias[1:2, :]], axis=1)
    for j in range(2):
        live = live_of(info, 2 * chunk + j)
        x = item_rows(buf, offsets[j], ATT)
        kept[j] = x[:PAD].astype(bf16)
        unit, _ = unit_rows(x)
        n_row = (unit * gain + bias).astype(bf16)
        normed[j] = n_row[:PAD]
        p_row = (dot(n_row, w_t[...], NT) + b_three).astype(bf16)
        proj[j] = p_row[:PAD]
        key_live = iota((ATT, ATT), 1) < live
        for h in range(heads):
            q = p_row[:, h * HEAD : (h + 1) * HEAD]
            k = p_row[:, width + h * HEAD : width + (h + 1) * HEAD]
            v = p_row[:, 2 * width + h * HEAD : 2 * width + (h + 1) * HEAD]
            s = jnp.where(key_live, dot(q, k, NT) * 0.125, -1e30)
            e = jnp.exp(s - jnp.max(s, -1, keepdims=True))
            att = (e * (1.0 / jnp.sum(e, -1, keepdims=True))).astype(bf16)
            c = dot(att, v).astype(bf16)
            at = j * width + h * HEAD
            ctx[:, at : at + HEAD] = c[:PAD]


def front(
    items, heads, mask_h, kind_h, tokens_h, w_h, qv_h, *refs
):
    vectors_h, refs = refs[:5], refs[5:]
    ctx, proj, normed, kept, info, counts, vecs = refs[:7]
    mask, kind, tokens, w_t, qv_bias, lines, buf, sems = refs[7:]
    pairs = [(mask_h, mask), (kind_h, kind), (tokens_h, tokens), (w_h, w_t), (qv_h, qv_bias)]
    pairs += [(v, lines.at[i]) for i, v in enumerate(vectors_h)]
    copies = [pltpu.make_async_copy(a, b, sems.at[i]) for i, (a, b) in enumerate(pairs)]
    for c in copies:
        c.start()
    copies[0].wait()
    copies[1].wait()
    total = 0
    second = 0
    row = iota(info.shape, 0)
    value = jnp.zeros(info.shape, f32)
    for i in range(items):
        n = PATCHES
        for slot in range(CAP):
            n = n + mask[i * SEQ + PATCHES + slot]
        e = kind[i * SEQ]
        total = total + n
        second = second + n * e
        value = jnp.where(row == i, n.astype(f32), value)
        value = jnp.where(row == items + i, e.astype(f32), value)
    info[...] = value
    row = iota(counts.shape, 0)
    counts[...] = jnp.where(
        row == 0, (total - second).astype(f32), jnp.where(row == 1, second.astype(f32), 0.0)
    )
    for c in copies[2:]:
        c.wait()
    for i in range(5):
        vecs[i : i + 1, :] = lines[i : i + 1, :]
    attention_items(
        0, heads, info, tokens[...], w_t, qv_bias, lines[0:1, :], lines[1:2, :], ctx, proj, normed, kept, buf
    )


def run_front(call, items, heads, mask, kind, tokens, w_t, qv_bias, vectors):
    width = heads * HEAD
    rows, d = tokens.shape
    ins = (mask, kind, tokens, w_t, qv_bias, *vectors)
    return call(
        functools.partial(front, items, heads),
        ins,
        [
            arr((PAD, 2 * width), bf16),
            arr((2, PAD, 3 * width), bf16),
            arr((2, PAD, d), bf16),
            arr((2, PAD, d), bf16),
            arr((2 * items, 128), f32),
            arr((TAIL, d), f32),
            arr((8, d), f32),
        ],
        [
            SMEM(mask.shape, jnp.int32),
            SMEM(kind.shape, jnp.int32),
            VMEM(tokens.shape, bf16),
            VMEM(w_t.shape, bf16),
            VMEM(qv_bias.shape, f32),
            VMEM((8, d), f32),
            VMEM((STAGE, d), f32),
            DMA((len(ins),)),
        ],
        specs=[hspec() for _ in ins],
        limit=60,
        name="front",
    )


def attention_forward(chunk, heads, *refs):
    hbm, outs, local, sems = refs[:5], refs[5:9], refs[9:14], refs[15]
    copies = [pltpu.make_async_copy(a, b, sems.at[i]) for i, (a, b) in enumerate(zip(hbm, local))]
    for c in copies:
        c.start()
    for c in copies:
        c.wait()
    info, vecs, tokens, w_t, qv_bias = local
    attention_items(
        chunk, heads, info, tokens[...], w_t, qv_bias, vecs[0:1, :], vecs[1:2, :], *outs, refs[14]
    )


def run_attention_forward(call, chunk, heads, info, vecs, tokens, w_t, qv_bias):
    width = heads * HEAD
    d = tokens.shape[1]
    ins = (info, vecs, tokens, w_t, qv_bias)
    return call(
        functools.partial(attention_forward, chunk, heads),
        ins,
        [arr((PAD, 2 * width), bf16), arr((2, PAD, 3 * width), bf16), arr((2, PAD, d), bf16), arr((2, PAD, d), bf16)],
        [VMEM(a.shape, a.dtype) for a in ins] + [VMEM((STAGE, d), f32), DMA((len(ins),))],
        specs=[hspec() for _ in ins],
        limit=60,
        name="attention_forward_%d" % chunk,
    )


def mask_rows(items, info, cot, masked, small, buf):
    d = cot.shape[1]
    buf[0 : items * SEQ] = cot[...].astype(f32)
    zero = jnp.zeros((1, d), f32)
    sums = [zero, zero]
    for i in range(items):
        rows = item_rows(buf, i * SEQ, PAD, live_of(info, i))
        masked[i] = rows.astype(bf16)
        line = jnp.sum(rows, 0, keepdims=True)
        e = expert_vector(info, items, i)
        for x in range(2):
            sums[x] = sums[x] + jnp.where(e == x, line, 0.0)
    small[...] = jnp.zeros_like(small)
    small[0:1, :] = sums[0]
    small[1:2, :] = sums[1]


def run_mask_rows(call, items, info, cot):
    d = cot.shape[1]
    return call(
        functools.partial(mask_rows, items),
        (info, cot),
        [arr((items, PAD, d), bf16), arr((8, d), f32)],
        [VMEM((items * SEQ + 16, d), f32)],
        name="mask_rows",
    )


def gather_slots():
    t = position()
    core = lax.rem(t, 2)
    return (t, t + 1 - 2 * core, lax.rem(t + 2, 4), lax.rem(t + 3 - 2 * core, 4))


def pack_kernel(own, far, out):
    out[0] = own[...]
    out[1] = far[...]


def run_pack(call, own, far, name):
    return call(pack_kernel, (own, far), [arr((2, *own.shape), own.dtype)], name=name)[0]


def put_slots(out, both, got):
    t, near, far, across = gather_slots()
    out[t] = both[0]
    out[far] = both[1]
    out[near] = got[0]
    out[across] = got[1]


def slot_kernel(both, got, out):
    put_slots(out, both, got)


def run_slots(call, both, got, name):
    return call(slot_kernel, (both, got), [arr((4, *both.shape[1:]), both.dtype)], name=name)[0]


def gelu_parts(h):
    cdf = 0.5 * (1.0 + lax.erf(h * 0.7071067811865476))
    density = jnp.exp(-0.5 * h * h) * 0.3989422804014327
    return h * cdf, cdf + h * density


def experts(chunk, items, heads, last, info, vecs, kept, masked, both, got, w_out, up_bias, w_up, w_down, *refs):
    width = heads * HEAD
    d = kept.shape[2]
    before, refs = (refs[: 4 * chunk], refs[4 * chunk :]) if last else ((), refs)
    middle, normed, active, ghid, small = refs[:5]
    sides = refs[5:9]
    ctx = refs[9]
    first = is_first()
    put_slots(ctx, both, got)
    mids, n_rows = [], []
    for j in range(2):
        total = jnp.zeros((PAD, d), f32)
        for s in range(4):
            total = total + dot(ctx[s][:, j * width : (j + 1) * width], w_out[s])
        mid = kept[j].astype(f32) + total + vecs[2:3, :]
        mids.append(mid)
        unit, _ = unit_rows(mid)
        n_row = (unit * vecs[3:4, :] + vecs[4:5, :]).astype(bf16)
        normed[j] = n_row
        n_rows.append(n_row)
    middle[...] = jnp.where(first, mids[0], mids[1])
    parts, downs = [], []
    zero = jnp.zeros((1, w_up.shape[2]), f32)
    sums = [zero, zero]
    for j in range(2):
        e = expert_of(info, items, 2 * chunk + j)
        wu = w_up[e]
        wd = w_down[e]
        h = dot(n_rows[j], wu) + up_bias[pl.ds(e, 1), :]
        value, slope = gelu_parts(h)
        act = value.astype(bf16)
        active[j] = act
        gh = (dot(masked[2 * chunk + j], wd, NT) * slope).astype(bf16)
        ghid[j] = gh
        parts.append(dot(gh, wu, NT))
        downs.append(dot(act, wd))
        line = jnp.sum(gh.astype(f32), 0, keepdims=True)
        flag = expert_vector(info, items, 2 * chunk + j)
        for x in range(2):
            sums[x] = sums[x] + jnp.where(flag == x, line, 0.0)
    small[...] = jnp.zeros_like(small)
    small[0:1, :] = sums[0]
    small[1:2, :] = sums[1]
    values = (
        jnp.where(first, parts[0], parts[1]),
        jnp.where(first, parts[1], parts[0]),
        jnp.where(first, downs[0], downs[1]),
        jnp.where(first, downs[1], downs[0]),
    )
    for i, (side, value) in enumerate(zip(sides, values)):
        if last:
            for k in range(chunk):
                side[k] = before[4 * k + i][...]
            side[chunk] = value.astype(bf16)
        else:
            side[...] = value.astype(bf16)


def run_experts(call, chunk, items, heads, info, vecs, kept, masked, ctxs, w_out, up_bias, w_up, w_down, before):
    width = heads * HEAD
    d = kept.shape[2]
    ff = w_up.shape[2]
    last = chunk == items // 2 - 1
    side = arr((chunk + 1, PAD, d), bf16) if last else arr((PAD, d), bf16)
    return call(
        functools.partial(experts, chunk, items, heads, last),
        (info, vecs, kept, masked, *ctxs, w_out, up_bias, w_up, w_down, *(before if last else ())),
        [
            arr((PAD, d), f32),
            arr((2, PAD, d), bf16),
            arr((2, PAD, ff), bf16),
            arr((2, PAD, ff), bf16),
            arr((8, d), f32),
        ]
        + [side] * 4,
        [VMEM((4, PAD, 2 * width), bf16)],
        limit=20,
        name="experts_%d" % chunk,
    )


def expert_grads(items, merged, tailed, info, *refs):
    chunks = items // 2
    tail, refs = (refs[0], refs[1:]) if tailed else (None, refs)
    lefts, refs = refs[:chunks], refs[chunks:]
    rights = refs[: 1 if merged else chunks]
    send, keep, total = refs[len(rights) :]
    for i in range(items):
        e = expert_of(info, items, i)
        right = rights[0][i] if merged else rights[i // 2][i % 2]
        term = dot(lefts[i // 2][i % 2], right, TN)
        if i == 0:
            total[e] = term
            total[1 - e] = jnp.zeros_like(term)
        else:
            total[e] += term
    one, _ = places(True)
    count = keep.shape[0]
    keep[...] = total[one].astype(bf16)
    send[0:count] = total[1 - one].astype(bf16)
    if tailed:
        put_tail(send, count, tail[...])


def run_expert_grads(call, items, info, lefts, rights, name, tail=()):
    merged = len(rights) == 1
    shape = (lefts[0].shape[2], rights[0].shape[2])
    return call(
        functools.partial(expert_grads, items, merged, len(tail) > 0),
        (info, *tail, *lefts, *rights),
        [arr((shape[0] + 2 * TAIL * len(tail), shape[1]), bf16), arr(shape, bf16)],
        [VMEM((2, *shape), f32)],
        name=name,
    )


def own_expert(info, items, chunk):
    return jnp.where(is_first(), expert_vector(info, items, 2 * chunk), expert_vector(info, items, 2 * chunk + 1))


def item_weight(info, items, item, counts):
    first, second = row_weight(counts)
    return jnp.where(expert_vector(info, items, item) == 0, first, second)


def own_weight(info, items, chunk, counts):
    first, second = row_weight(counts)
    return jnp.where(own_expert(info, items, chunk) == 0, first, second)


def norm_two_back(chunks, vecs, masked, pair, far, *refs):
    middles, branch, (grad_mid, small) = refs[:chunks], refs[chunks : 2 * chunks], refs[2 * chunks :]
    small[...] = jnp.zeros_like(small)
    for k in range(chunks):
        own_cot = jnp.where(is_first(), masked[2 * k], masked[2 * k + 1]).astype(f32)
        unit, scale = unit_rows(middles[k][...])
        grad = pair[k].astype(f32) + far[k].astype(f32)
        out = own_cot + norm_back(grad, unit, scale, vecs[3:4, :])
        grad_mid[k] = out
        branch[k][...] = out.astype(bf16)
        for i, value in enumerate((grad * unit, grad, out)):
            small[3 * k + i : 3 * k + i + 1, :] = jnp.sum(value, 0, keepdims=True)


def run_norm_two_back(call, vecs, masked, pair, far, middles):
    chunks = len(middles)
    return call(
        functools.partial(norm_two_back, chunks),
        (vecs, masked, pair, far, *middles),
        [arr(pair.shape[1:], bf16)] * chunks
        + [arr(pair.shape, f32), arr((-(-3 * chunks // 8) * 8, pair.shape[2]), f32)],
        name="norm_two_back",
    )


def attention_backward(
    chunk, heads, info, own, other, w_out, proj, w_t, kept,
    gproj, small, small_one, part_own, part_other,
):
    width = heads * HEAD
    first = is_first()
    parts = []
    small[...] = jnp.zeros_like(small)
    small_one[...] = jnp.zeros_like(small_one)
    for j in range(2):
        live = live_of(info, 2 * chunk + j)
        a, b = (own, other) if j == 0 else (other, own)
        branch = jnp.where(first, a[...], b[...])
        gctx = dot(branch, w_out[...], NT).astype(bf16)
        p_row = proj[j]
        key_live = iota((PAD, PAD), 1) < live
        gq, gk, gv = [], [], []
        for h in range(heads):
            q = p_row[:, h * HEAD : (h + 1) * HEAD]
            k = p_row[:, width + h * HEAD : width + (h + 1) * HEAD]
            v = p_row[:, 2 * width + h * HEAD : 2 * width + (h + 1) * HEAD]
            gc = gctx[:, h * HEAD : (h + 1) * HEAD]
            s = jnp.where(key_live, dot(q, k, NT) * 0.125, -1e30)
            e = jnp.exp(s - jnp.max(s, -1, keepdims=True))
            att = e * (1.0 / jnp.sum(e, -1, keepdims=True))
            ga = dot(gc, v, NT)
            gs = (att * (ga - jnp.sum(ga * att, -1, keepdims=True))).astype(bf16)
            gv.append(dot(att.astype(bf16), gc, TN))
            gq.append(dot(gs, k) * 0.125)
            gk.append(dot(gs, q, TN) * 0.125)
        gp = jnp.concatenate(gq + gk + gv, axis=1).astype(bf16)
        gproj[j] = gp
        small[j : j + 1, :] = jnp.sum(gp.astype(f32), 0, keepdims=True)
        part = dot(gp, w_t[...])
        parts.append(part)
        unit, _ = unit_rows(kept[j].astype(f32))
        small_one[2 * j : 2 * j + 1, :] = jnp.sum(part * unit, 0, keepdims=True)
        small_one[2 * j + 1 : 2 * j + 2, :] = jnp.sum(part, 0, keepdims=True)
    part_own[...] = jnp.where(first, parts[0], parts[1]).astype(bf16)
    part_other[...] = jnp.where(first, parts[1], parts[0]).astype(bf16)


def run_attention_backward(call, chunk, heads, info, own, other, w_out, proj, w_t, kept):
    width = heads * HEAD
    d = own.shape[1]
    side = arr((PAD, d), bf16)
    return call(
        functools.partial(attention_backward, chunk, heads),
        (info, own, other, w_out, proj, w_t, kept),
        [arr((2, PAD, 3 * width), bf16), arr((8, 3 * width), f32), arr((8, d), f32), side, side],
        name="attention_backward_%d" % chunk,
    )


def attention_grads(items, heads, info, counts, *refs):
    width = heads * HEAD
    chunks = items // 2
    own, other, gproj, normed, ctx = (refs[i * chunks : (i + 1) * chunks] for i in range(5))
    send, keep, both = refs[5 * chunks :]
    first = is_first()
    rows = 3 * width
    total = jnp.zeros((rows, keep.shape[1]), f32)
    total_out = jnp.zeros((width, keep.shape[1]), f32)
    for k in range(chunks):
        for j in range(2):
            weight = item_weight(info, items, 2 * k + j, counts)
            total = total + dot((gproj[k][j].astype(f32) * weight).astype(bf16), normed[k][j], TN)
            a, b = (own, other) if j == 0 else (other, own)
            branch = jnp.where(first, a[k][...], b[k][...]).astype(f32)
            branch = (branch * weight).astype(bf16)
            total_out = total_out + dot(ctx[k][:, j * width : (j + 1) * width], branch, TN)
    half = 2 * width
    both[0] = total[:half].astype(bf16)
    both[1, 0 : rows - half] = total[half:].astype(bf16)
    both[1, rows - half :] = total_out.astype(bf16)
    one, _ = places(True)
    keep[...] = both[one]
    send[...] = both[1 - one]


def run_attention_grads(call, items, heads, info, counts, own, other, gproj, normed, ctx):
    width = heads * HEAD
    d = own[0].shape[1]
    return call(
        functools.partial(attention_grads, items, heads),
        (info, counts, *own, *other, *gproj, *normed, *ctx),
        [arr((2 * width, d), bf16)] * 2,
        [VMEM((2, 2 * width, d), bf16)],
        name="attention_grads",
    )


def norm_one_back(items, info, counts, vecs, grad_mid, pair, far, *refs):
    chunks = items // 2
    kept, grad_own = refs[:chunks], refs[chunks]
    for k in range(chunks):
        x = jnp.where(is_first(), kept[k][0], kept[k][1]).astype(f32)
        unit, scale = unit_rows(x)
        grad = pair[k].astype(f32) + far[k].astype(f32)
        total = grad_mid[k] + norm_back(grad, unit, scale, vecs[0:1, :])
        grad_own[k] = (total * own_weight(info, items, k, counts)).astype(bf16)


def run_norm_one_back(call, items, info, counts, vecs, grad_mid, pair, far, kept):
    return call(
        functools.partial(norm_one_back, items),
        (info, counts, vecs, grad_mid, pair, far, *kept),
        [arr(pair.shape, bf16)],
        name="norm_one_back",
    )[0]


def output_rows(items, info, down_bias, pair, far, *refs):
    chunks = items // 2
    middles, out = refs[:chunks], refs[chunks]
    for k in range(chunks):
        bias = jnp.where(own_expert(info, items, k) == 0, down_bias[0:1, :], down_bias[1:2, :])
        out[k] = (middles[k][...] + (pair[k].astype(f32) + far[k].astype(f32)) + bias).astype(bf16)


def run_output_rows(call, items, info, down_bias, pair, far, middles):
    return call(
        functools.partial(output_rows, items),
        (info, down_bias, pair, far, *middles),
        [arr(pair.shape, bf16)],
        name="output_rows",
    )[0]


def assemble(items, own, other, out, buf, low, sem):
    first = is_first()
    for k in range(items // 2):
        for j in range(2):
            a, b = (own, other) if j == 0 else (other, own)
            buf[pl.ds((2 * k + j) * SEQ, PAD), :] = jnp.where(first, a[k], b[k]).astype(f32)
    low[...] = buf[0 : items * SEQ, :].astype(bf16)
    copy = pltpu.make_async_copy(low, out, sem)
    copy.start()
    copy.wait()


def run_assemble(call, items, own, other, name):
    d = own.shape[2]
    return call(
        functools.partial(assemble, items),
        (own, other),
        [arr((items * SEQ, d), bf16)],
        [VMEM((items * SEQ + 16, d), f32), VMEM((items * SEQ, d), bf16), DMA],
        out_specs=[hspec()],
        name=name,
    )[0]


def swap(value, axis, size, bit):
    return lax.ppermute(value, axis, [(i, i ^ bit) for i in range(size)])


def add_kernel(a, b, out):
    out[...] = (a[...].astype(f32) + b[...].astype(f32)).astype(out.dtype)


def run_add(call, a, b, name):
    return call(add_kernel, (a, b), [arr(a.shape, a.dtype)], name=name)[0]


def pair_kernel(chunks, *refs):
    own, got, out = refs[:chunks], refs[chunks : 2 * chunks], refs[2 * chunks]
    for k in range(chunks):
        out[k] = (own[k][...].astype(f32) + got[k][...].astype(f32)).astype(bf16)


def run_pair(call, own, got, name):
    return call(
        functools.partial(pair_kernel, len(own)), (*own, *got), [arr((len(own), *own[0].shape), bf16)], name=name
    )[0]


def split_rows(rows):
    high = rows.astype(bf16)
    return high, (rows - high.astype(f32)).astype(bf16)


def add_tail(held, got, at):
    return held[...] + got[at : at + TAIL].astype(f32) + got[at + TAIL : at + 2 * TAIL].astype(f32)


def put_tail(out, at, rows):
    out[at : at + TAIL], out[at + TAIL : at + 2 * TAIL] = split_rows(rows)


def attach_kernel(rows, tail, out):
    count = rows.shape[0]
    out[0:count] = rows[...]
    put_tail(out, count, tail[...])


def half_of(ref, index, count):
    return ref[pl.ds(pl.multiple_of(index * count, count), count), :]


def fold_step(turned, tailed, keep, got, *refs):
    refs = list(refs)
    held = refs.pop(0) if tailed else None
    send_next, keep_next = refs[:2]
    count = keep_next.shape[0]
    _, two = places(turned)
    for out, index in ((keep_next, two), (send_next, 1 - two)):
        total = half_of(keep, index, count).astype(f32) + half_of(got, index, count).astype(f32)
        out[0:count] = total.astype(bf16)
    if tailed:
        tail = add_tail(held, got, 2 * count)
        refs[2][...] = tail
        put_tail(send_next, count, tail)


def add_step(tailed, handed, sends, keep, got, *refs):
    refs = list(refs)
    held = refs.pop(0) if tailed else None
    given = [refs.pop(0) for _ in range(handed)]
    out = refs.pop(0)
    count = out.shape[0]
    total = (keep[...].astype(f32) + got[0:count].astype(f32)).astype(bf16)
    out[...] = total
    if tailed:
        tail = add_tail(held, got, count)
        refs.pop(0)[...] = tail
        if sends:
            send = refs.pop(0)
            send[0:count] = total
            put_tail(send, count, tail)
    if handed == 1:
        refs[0][...] = given[0][...]
    if handed == 2:
        attach_kernel(given[0], given[1], refs[0])


def join_kernel(turned, own, other, out):
    _, bit = places(turned)
    out[bit] = own[...]
    out[1 - bit] = other[...]


PIECES = 4


def whole_kernel(scaled, *refs):
    counts = refs[0] if scaled else None
    own, other, out, buf, sems = refs[1:] if scaled else refs
    bit, _ = places(True)
    rows = own.shape[0] // PIECES
    copies = []
    for side, ref in enumerate((own, other)):
        half = bit if side == 0 else 1 - bit
        weight = 1.0
        if scaled:
            first, second = row_weight(counts)
            weight = jnp.where(half == 0, first, second)
        for i in range(PIECES):
            at = pl.ds(i * rows, rows)
            buf[side, at] = ref[at].astype(f32) * weight
            copy = pltpu.make_async_copy(buf.at[side, at], out.at[half, at], sems.at[side, i])
            copy.start()
            copies.append(copy)
    for copy in copies:
        copy.wait()


def run_whole(call, counts, own, other, name, limit):
    scaled = counts is not None
    shape = (2, *own.shape)
    return call(
        functools.partial(whole_kernel, scaled),
        ((counts,) if scaled else ()) + (own, other),
        [arr(shape, f32)],
        [VMEM(shape, f32), DMA((2, PIECES))],
        out_specs=[hspec()],
        limit=limit,
        name=name,
    )[0]


def attention_whole_kernel(rows, own, other, grad_qkv, grad_out, low, buf, sems):
    bit, _ = places(True)
    half = own.shape[0]
    low[bit] = own[...]
    low[1 - bit] = other[...]
    copies = []
    spans = [(grad_qkv, 0, 0, half), (grad_qkv, 1, half, rows - half), (grad_out, 1, 0, 2 * half - rows)]
    start = [0, 0, rows - half]
    for i, (out, side, to, count) in enumerate(spans):
        at = pl.ds(start[i], count)
        buf[side, at] = low[side, at].astype(f32)
        copy = pltpu.make_async_copy(buf.at[side, at], out.at[pl.ds(to, count)], sems.at[i])
        copy.start()
        copies.append(copy)
    for copy in copies:
        copy.wait()


def run_attention_whole(call, rows, own, other, name):
    half, d = own.shape
    return call(
        functools.partial(attention_whole_kernel, rows),
        (own, other),
        [arr((rows, d), f32), arr((2 * half - rows, d), f32)],
        [VMEM((2, half, d), bf16), VMEM((2, half, d), f32), DMA((3,))],
        out_specs=[hspec(), hspec()],
        limit=60,
        name=name,
    )


class Sum:
    def __init__(self, call, dp, tp, name, turned, keep, tail=None):
        self.call, self.dp, self.tp, self.name, self.keep, self.tail = call, dp, tp, name, keep, tail
        self.turned = turned
        self.steps = ((1, 2), (2, 1), (4, 4)) if turned else ((1, 1), (2, 2), (4, 4))

    def start(self, send):
        if self.dp == 8:
            self.got = self.cross(send, self.steps[0])
            return
        keep = self.keep
        send = send[: keep.shape[0]]
        low = (lax.axis_index("dp") % 2).astype(jnp.int32)
        high = (lax.axis_index("dp") // 2 % 2).astype(jnp.int32)
        one = jnp.where(lax.axis_index("tensor") % 2 == 0, low, high) if self.turned else low
        flat = jnp.where(one == 0, jnp.concatenate([keep, send]), jnp.concatenate([send, keep]))
        share = lax.psum_scatter(flat, "dp", scatter_dimension=0, tiled=True)
        whole = lax.all_gather(share, "dp", axis=0, tiled=True).reshape(2, *keep.shape)
        self.keep = jnp.where(one == 0, whole[0], whole[1])
        self.got = jnp.where(one == 0, whole[1], whole[0])
        if self.tail is not None:
            self.tail = lax.psum(self.tail, "dp")

    def cross(self, value, bits):
        dp, tp = self.dp, self.tp
        route = [(i * tp + t, (i ^ bits[t % 2]) * tp + t) for i in range(dp) for t in range(tp)]
        return lax.ppermute(value, ("dp", "tensor"), route)

    def quarter(self):
        if self.dp != 8:
            return
        rows, d = self.keep.shape
        tailed = self.tail is not None
        ins = (self.keep, self.got) + ((self.tail,) if tailed else ())
        outs = [arr((rows // 2 + (2 * TAIL if tailed else 0), d), bf16), arr((rows // 2, d), bf16)]
        outs += [arr(self.tail.shape, f32)] if tailed else []
        send, self.keep, *tail = self.call(
            functools.partial(fold_step, self.turned, tailed), ins, outs, name=self.name + "_half"
        )
        self.tail = tail[0] if tailed else None
        self.got = self.cross(send, self.steps[1])

    def add(self, name, sends, handed):
        tailed = self.tail is not None
        rows, d = self.keep.shape
        ins = (self.keep, self.got) + ((self.tail,) if tailed else ()) + handed
        outs = [arr((rows, d), bf16)]
        outs += [arr(self.tail.shape, f32)] if tailed else []
        outs += [arr((rows + 2 * TAIL, d), bf16)] if tailed and sends else []
        if handed:
            outs.append(arr((handed[0].shape[0] + 2 * TAIL * (len(handed) - 1), d), bf16))
        out = self.call(
            functools.partial(add_step, tailed, len(handed), sends), ins, outs, name=self.name + name
        )
        self.keep = out[0]
        if tailed:
            self.tail = out[1]
        return out[2] if tailed and sends else out[0], out[-1]

    def middle(self, *handed):
        if self.dp != 8:
            return handed[0] if handed else None
        send, given = self.add("_quarter", True, handed)
        self.got = self.cross(send, self.steps[2])
        return given

    def back_half(self):
        if self.dp != 8:
            return
        self.add("_sum", False, ())
        self.got = self.cross(self.keep, self.steps[1])

    def back_whole(self):
        if self.dp != 8:
            return
        rows, d = self.keep.shape
        out = self.call(functools.partial(join_kernel, self.turned), (self.keep, self.got), [arr((2, rows, d), bf16)], name=self.name + "_join")[0]
        self.keep = out.reshape(2 * rows, d)
        self.got = self.cross(self.keep, self.steps[0])


def collect(items, heads, info, counts, two, cots, *refs):
    width = heads * HEAD
    chunks = items // 2
    exp, attn, one = (refs[i * chunks : (i + 1) * chunks] for i in range(3))
    (out,) = refs[3 * chunks :]
    out[...] = jnp.zeros_like(out)
    weights = [own_weight(info, items, k, counts) for k in range(chunks)]
    out[0:3, :] = sum(two[3 * k : 3 * k + 3, :] * weights[k] for k in range(chunks)) * 0.5
    each = [item_weight(info, items, i, counts) for i in range(items)]
    out[3:5, :] = sum(one[i // 2][2 * (i % 2) : 2 * (i % 2) + 2, :] * each[i] for i in range(items))
    out[8:10, :] = sum(r[0:2, :] for r in exp)
    out[10:12, :] = cots[0:2, :]
    out[12:13, 0 : 3 * width] = sum(attn[i // 2][i % 2 : i % 2 + 1, :] * each[i] for i in range(items))


def small_outputs(heads, counts, small, *outs):
    width = heads * HEAD
    d = small.shape[1]
    for i in range(5):
        outs[i][...] = small[i : i + 1, :].reshape(d)
    for i, weight in enumerate(row_weight(counts)):
        outs[5][i : i + 1, :] = small[8 + i : 9 + i, :] * weight
        outs[6][i : i + 1, :] = small[10 + i : 11 + i, :] * weight
    row = small[12:13, :]
    outs[7][0:1, :] = row[:, 0:width]
    outs[7][1:2, :] = row[:, 2 * width : 3 * width]


def run_small_outputs(call, heads, counts, small):
    d = small.shape[1]
    return call(
        functools.partial(small_outputs, heads),
        (counts, small),
        [arr((d,), f32)] * 5 + [arr((2, d), f32)] * 2 + [arr((2, heads * HEAD), f32)],
        name="small_outputs",
    )


def row_sum_kernel(small, got, out):
    out[0:8, :] = small[0:8, :] + got[0:8, :]
    out[8:, :] = small[8:, :]


def run_row_sum(call, small, got, name):
    return call(row_sum_kernel, (small, got), [arr(small.shape, f32)], name=name)[0]


def local(
    dp, tp,
    tokens, token_mask, expert_type, cotangent, ln1_gain, ln1_bias, w_qkv, qv_bias, w_out, out_bias,
    ln2_gain, ln2_bias, w_up, up_bias, w_down, down_bias,
):
    rows, d = tokens.shape
    items = rows // SEQ
    width = w_qkv.shape[2]
    heads = width // HEAD
    core_swap = lambda v: swap(v, "tensor", tp, 1)
    far_swap = lambda v: swap(v, "tensor", tp, 2)
    chunks = items // 2
    call = Order()
    w_t = w_qkv.transpose(1, 2, 0).reshape(3 * width, d)

    w_far = far_swap(w_out)
    c0, p, n, x, info, totals, vecs = run_front(
        call, items, heads, token_mask, expert_type, tokens, w_t, qv_bias,
        (ln1_gain, ln1_bias, out_bias, ln2_gain, ln2_bias),
    )
    ctx, proj, normed_one, kept, ctx_far, ctxs = [c0], [p], [n], [x], [far_swap(c0)], []
    for k in range(1, chunks):
        c0, p, n, x = run_attention_forward(call, k, heads, info, vecs, tokens, w_t, qv_bias)
        for group, value in zip((ctx, proj, normed_one, kept, ctx_far), (c0, p, n, x, far_swap(c0))):
            group.append(value)
    both = run_pack(call, ctx[0], ctx_far[0], "context_pack_0")
    ctxs.append((both, core_swap(both)))
    w_both = run_pack(call, w_out, w_far, "w_out_pack")
    w_got = core_swap(w_both)
    masked, small_c = run_mask_rows(call, items, info, cotangent)
    w_all = run_slots(call, w_both, w_got, "w_out_all")
    middle, normed_two, active, ghid, small_e, before = [], [], [], [], [], []
    for k in range(chunks):
        out = run_experts(
            call, k, items, heads, info, vecs, kept[k], masked, ctxs[k], w_all, up_bias, w_up, w_down, before
        )
        for group, value in zip((middle, normed_two, active, ghid, small_e), out[:5]):
            group.append(value)
        before += list(out[5:])
        if k + 1 < chunks:
            both = run_pack(call, ctx[k + 1], ctx_far[k + 1], "context_pack_%d" % (k + 1))
            ctxs.append((both, core_swap(both)))
    part_own, part_other, down_own, down_other = before[-4:]
    part_got = core_swap(part_other)
    down_got = core_swap(down_other)

    send, keep = run_expert_grads(call, items, info, active, [masked], "down_grads", (totals,))
    sum_down = Sum(call, dp, tp, "down", True, keep, totals)
    sum_down.start(send)
    part = run_add(call, part_own, part_got, "part")
    part_far = far_swap(part)
    down = run_add(call, down_own, down_got, "expert_rows")
    down_far = far_swap(down)
    up_send, up_keep = run_expert_grads(call, items, info, normed_two, ghid, "up_grads")
    sum_up = Sum(call, dp, tp, "up", True, up_keep)
    sum_down.quarter()
    *branch_own, grad_mid, small_n = run_norm_two_back(call, vecs, masked, part, part_far, middle)
    branch_other = [core_swap(b) for b in branch_own]
    up_send = sum_down.middle(up_send)
    sum_up.start(up_send)
    gproj, small_a, small_o, one_own, one_got = [], [], [], [], []
    for k in range(chunks):
        g, sa, so, po, pt = run_attention_backward(
            call, k, heads, info, branch_own[k], branch_other[k], w_out, proj[k], w_t, kept[k]
        )
        for group, value in zip((gproj, small_a, small_o, one_own, one_got), (g, sa, so, po, core_swap(pt))):
            group.append(value)
    sum_up.quarter()
    sum_down.back_half()
    totals = sum_down.tail
    small = call(
        functools.partial(collect, items, heads),
        (info, totals, small_n, small_c, *small_e, *small_a, *small_o),
        [arr((TAIL, d), f32)],
        name="collect",
    )[0]
    attn_send, keep = run_attention_grads(
        call, items, heads, info, totals, branch_own, branch_other, gproj, normed_one, ctx
    )
    one = run_pair(call, one_own, one_got, "one")
    one_far = far_swap(one)
    sum_attn = Sum(call, dp, tp, "attn", True, keep, small)
    attn_send = sum_up.middle(attn_send, small)
    sum_attn.start(attn_send)
    sum_down.back_whole()
    sum_attn.quarter()
    grad_own = run_norm_one_back(call, items, info, totals, vecs, grad_mid, one, one_far, kept)
    grad_other = core_swap(grad_own)
    sum_up.back_half()
    sum_attn.middle()
    out_own = run_output_rows(call, items, info, down_bias, down, down_far, middle)
    out_other = core_swap(out_own)
    grad_tokens = run_assemble(call, items, grad_own, grad_other, "grad_tokens")
    sum_up.back_whole()
    output = run_assemble(call, items, out_own, out_other, "output")
    sum_attn.back_half()
    small = sum_attn.tail
    small = run_row_sum(call, small, core_swap(small), "norm_rows_core")
    small_far = far_swap(small)
    sum_attn.back_whole()
    small = run_row_sum(call, small, small_far, "norm_rows_far")
    smalls = run_small_outputs(call, heads, totals, small)
    grad_down = run_whole(call, totals, sum_down.keep, sum_down.got, "down_whole", 20)
    grad_up = run_whole(call, totals, sum_up.keep, sum_up.got, "up_whole", 60)
    grad_qkv, grad_out = run_attention_whole(call, 3 * width, sum_attn.keep, sum_attn.got, "attn_whole")
    return (
        output,
        grad_tokens,
        smalls[3],
        smalls[4],
        grad_qkv.reshape(3, width, d).transpose(2, 0, 1),
        smalls[7],
        grad_out,
        smalls[2],
        smalls[0],
        smalls[1],
        grad_up.reshape(w_up.shape),
        smalls[5],
        grad_down.reshape(w_down.shape),
        smalls[6],
        totals[:2, 0].astype(jnp.int32),
    )


def solution(mesh):
    in_specs = (
        P("dp", None),
        P("dp"),
        P("dp"),
        P("dp", None),
        P(),
        P(),
        P(None, None, "tensor"),
        P(None, "tensor"),
        P("tensor", None),
        P(),
        P(),
        P(),
        P(None, None, "tensor"),
        P(None, "tensor"),
        P(None, "tensor", None),
        P(),
    )
    out_specs = (
        P("dp", None),
        P("dp", None),
        P(),
        P(),
        P(None, None, "tensor"),
        P(None, "tensor"),
        P("tensor", None),
        P(),
        P(),
        P(),
        P(None, None, "tensor"),
        P(None, "tensor"),
        P(None, "tensor", None),
        P(),
        P(),
    )
    return jax.shard_map(
        functools.partial(local, mesh.shape["dp"], mesh.shape["tensor"]),
        mesh=mesh,
        in_specs=in_specs,
        out_specs=out_specs,
        check_vma=False,
    )
```

```python
import functools

import jax
import jax.numpy as jnp
from jax import lax
from jax.experimental import pallas as pl
from jax.experimental.pallas import tpu as pltpu
from jax.sharding import PartitionSpec as P

HEAD = 64
PATCHES = 197
CAP = 40
SEQ = PATCHES + CAP
PAD = 240
ATT = 256
STAGE = 2 * SEQ + 32
TAIL = 16

epsilon = 1e-05
f32 = jnp.float32
bf16 = jnp.bfloat16

NT = (((1,), (1,)), ((), ()))
NN = (((1,), (0,)), ((), ()))
TN = (((0,), (0,)), ((), ()))

VMEM = pltpu.VMEM
SMEM = pltpu.SMEM
DMA = pltpu.SemaphoreType.DMA


def dot(a, b, dims=NN):
    return lax.dot_general(a, b, dims, preferred_element_type=f32)


def iota(shape, dim):
    return lax.broadcasted_iota(jnp.int32, shape, dim)


def unit_rows(x):
    mean = jnp.mean(x, -1, keepdims=True)
    centered = x - mean
    scale = lax.rsqrt(jnp.mean(centered * centered, -1, keepdims=True) + epsilon)
    return centered * scale, scale


def norm_back(grad, unit, scale, gain):
    t = grad * gain
    return scale * (
        t - jnp.mean(t, -1, keepdims=True) - unit * jnp.mean(t * unit, -1, keepdims=True)
    )


def vspec():
    return pl.BlockSpec(memory_space=VMEM)


def hspec():
    return pl.BlockSpec(memory_space=pltpu.HBM)


def aspec():
    return pl.BlockSpec(memory_space=pl.ANY)


class Order:
    def __init__(self):
        self.last = None

    def __call__(self, kernel, ins, outs, scratch=(), limit=16, specs=None, out_specs=None, name=None):
        taken = len(ins)
        behind = () if self.last is None or any(a is self.last for a in ins) else (self.last,)

        def body(*refs):
            kernel(*refs[:taken], *refs[taken + len(behind) :])

        results = pl.pallas_call(
            body,
            out_shape=list(outs),
            in_specs=list(specs or [vspec() for _ in ins]) + [aspec() for _ in behind],
            out_specs=list(out_specs or [vspec() for _ in outs]),
            scratch_shapes=list(scratch),
            compiler_params=pltpu.CompilerParams(vmem_limit_bytes=limit * 1024 * 1024),
            cost_estimate=pl.CostEstimate(flops=1, bytes_accessed=1, transcendentals=0),
            name=name,
        )(*ins, *behind)
        self.last = results[0]
        return results


def arr(shape, dtype):
    return jax.ShapeDtypeStruct(shape, dtype)


def position():
    return lax.axis_index("tensor")


def is_first():
    return lax.rem(position(), 2) == 0


def places(turned):
    place = lax.axis_index("dp")
    low = lax.rem(place, 2)
    high = lax.rem(lax.div(place, 2), 2)
    if not turned:
        return low, high
    first = is_first()
    return jnp.where(first, low, high), jnp.where(first, high, low)


def stage_rows(rows, buf, chunk):
    low = 2 * chunk * SEQ
    high = low + 2 * SEQ
    base = low // 16 * 16
    top = min(rows.shape[0], -(-high // 16) * 16)
    buf[0 : top - base] = rows[base:top].astype(f32)
    return [low - base, low - base + SEQ]


def item_rows(buf, offset, count, live=SEQ):
    rows = buf[pl.ds(offset, count), :]
    return jnp.where(iota(rows.shape, 0) < live, rows, 0.0)


def live_of(info, item):
    return info[item : item + 1, 0:1].astype(jnp.int32)


def expert_vector(info, items, item):
    return info[items + item : items + item + 1, 0:1]


def expert_of(info, items, item):
    return jnp.max(info[items + item : items + item + 1, :]).astype(jnp.int32)


def row_weight(counts):
    both = counts[0:1, 0:1] + counts[1:2, 0:1]
    return both / (2.0 * counts[0:1, 0:1]), both / (2.0 * counts[1:2, 0:1])


def attention_items(chunk, heads, info, rows, w_t, qv_bias, gain, bias, ctx, proj, normed, kept, buf):
    width = heads * HEAD
    offsets = stage_rows(rows, buf, chunk)
    b_three = jnp.concatenate([qv_bias[0:1, :], jnp.zeros((1, width), f32), qv_bias[1:2, :]], axis=1)
    for j in range(2):
        live = live_of(info, 2 * chunk + j)
        x = item_rows(buf, offsets[j], ATT)
        kept[j] = x[:PAD].astype(bf16)
        unit, _ = unit_rows(x)
        n_row = (unit * gain + bias).astype(bf16)
        normed[j] = n_row[:PAD]
        p_row = (dot(n_row, w_t[...], NT) + b_three).astype(bf16)
        proj[j] = p_row[:PAD]
        key_live = iota((ATT, ATT), 1) < live
        for h in range(heads):
            q = p_row[:, h * HEAD : (h + 1) * HEAD]
            k = p_row[:, width + h * HEAD : width + (h + 1) * HEAD]
            v = p_row[:, 2 * width + h * HEAD : 2 * width + (h + 1) * HEAD]
            s = jnp.where(key_live, dot(q, k, NT) * 0.125, -1e30)
            e = jnp.exp(s - jnp.max(s, -1, keepdims=True))
            att = (e * (1.0 / jnp.sum(e, -1, keepdims=True))).astype(bf16)
            c = dot(att, v).astype(bf16)
            at = j * width + h * HEAD
            ctx[:, at : at + HEAD] = c[:PAD]


def front(
    items, heads, mask_h, kind_h, tokens_h, w_h, qv_h, *refs
):
    vectors_h, refs = refs[:5], refs[5:]
    ctx, proj, normed, kept, info, counts, vecs = refs[:7]
    mask, kind, tokens, w_t, qv_bias, lines, buf, sems = refs[7:]
    pairs = [(mask_h, mask), (kind_h, kind), (tokens_h, tokens), (w_h, w_t), (qv_h, qv_bias)]
    pairs += [(v, lines.at[i]) for i, v in enumerate(vectors_h)]
    copies = [pltpu.make_async_copy(a, b, sems.at[i]) for i, (a, b) in enumerate(pairs)]
    for c in copies:
        c.start()
    copies[0].wait()
    copies[1].wait()
    total = 0
    second = 0
    row = iota(info.shape, 0)
    value = jnp.zeros(info.shape, f32)
    for i in range(items):
        n = PATCHES
        for slot in range(CAP):
            n = n + mask[i * SEQ + PATCHES + slot]
        e = kind[i * SEQ]
        total = total + n
        second = second + n * e
        value = jnp.where(row == i, n.astype(f32), value)
        value = jnp.where(row == items + i, e.astype(f32), value)
    info[...] = value
    row = iota(counts.shape, 0)
    counts[...] = jnp.where(
        row == 0, (total - second).astype(f32), jnp.where(row == 1, second.astype(f32), 0.0)
    )
    for c in copies[2:]:
        c.wait()
    for i in range(5):
        vecs[i : i + 1, :] = lines[i : i + 1, :]
    attention_items(
        0, heads, info, tokens[...], w_t, qv_bias, lines[0:1, :], lines[1:2, :], ctx, proj, normed, kept, buf
    )


def run_front(call, items, heads, mask, kind, tokens, w_t, qv_bias, vectors):
    width = heads * HEAD
    rows, d = tokens.shape
    ins = (mask, kind, tokens, w_t, qv_bias, *vectors)
    return call(
        functools.partial(front, items, heads),
        ins,
        [
            arr((PAD, 2 * width), bf16),
            arr((2, PAD, 3 * width), bf16),
            arr((2, PAD, d), bf16),
            arr((2, PAD, d), bf16),
            arr((2 * items, 128), f32),
            arr((TAIL, d), f32),
            arr((8, d), f32),
        ],
        [
            SMEM(mask.shape, jnp.int32),
            SMEM(kind.shape, jnp.int32),
            VMEM(tokens.shape, bf16),
            VMEM(w_t.shape, bf16),
            VMEM(qv_bias.shape, f32),
            VMEM((8, d), f32),
            VMEM((STAGE, d), f32),
            DMA((len(ins),)),
        ],
        specs=[hspec() for _ in ins],
        limit=60,
        name="front",
    )


def attention_forward(chunk, heads, *refs):
    hbm, outs, local, sems = refs[:5], refs[5:9], refs[9:14], refs[15]
    copies = [pltpu.make_async_copy(a, b, sems.at[i]) for i, (a, b) in enumerate(zip(hbm, local))]
    for c in copies:
        c.start()
    for c in copies:
        c.wait()
    info, vecs, tokens, w_t, qv_bias = local
    attention_items(
        chunk, heads, info, tokens[...], w_t, qv_bias, vecs[0:1, :], vecs[1:2, :], *outs, refs[14]
    )


def run_attention_forward(call, chunk, heads, info, vecs, tokens, w_t, qv_bias):
    width = heads * HEAD
    d = tokens.shape[1]
    ins = (info, vecs, tokens, w_t, qv_bias)
    return call(
        functools.partial(attention_forward, chunk, heads),
        ins,
        [arr((PAD, 2 * width), bf16), arr((2, PAD, 3 * width), bf16), arr((2, PAD, d), bf16), arr((2, PAD, d), bf16)],
        [VMEM(a.shape, a.dtype) for a in ins] + [VMEM((STAGE, d), f32), DMA((len(ins),))],
        specs=[hspec() for _ in ins],
        limit=60,
        name="attention_forward_%d" % chunk,
    )


def mask_rows(items, info, cot, masked, small, buf):
    d = cot.shape[1]
    buf[0 : items * SEQ] = cot[...].astype(f32)
    zero = jnp.zeros((1, d), f32)
    sums = [zero, zero]
    for i in range(items):
        rows = item_rows(buf, i * SEQ, PAD, live_of(info, i))
        masked[i] = rows.astype(bf16)
        line = jnp.sum(rows, 0, keepdims=True)
        e = expert_vector(info, items, i)
        for x in range(2):
            sums[x] = sums[x] + jnp.where(e == x, line, 0.0)
    small[...] = jnp.zeros_like(small)
    small[0:1, :] = sums[0]
    small[1:2, :] = sums[1]


def run_mask_rows(call, items, info, cot):
    d = cot.shape[1]
    return call(
        functools.partial(mask_rows, items),
        (info, cot),
        [arr((items, PAD, d), bf16), arr((8, d), f32)],
        [VMEM((items * SEQ + 16, d), f32)],
        name="mask_rows",
    )


def gather_slots():
    t = position()
    core = lax.rem(t, 2)
    return (t, t + 1 - 2 * core, lax.rem(t + 2, 4), lax.rem(t + 3 - 2 * core, 4))


def pack_kernel(own, far, out):
    out[0] = own[...]
    out[1] = far[...]


def run_pack(call, own, far, name):
    return call(pack_kernel, (own, far), [arr((2, *own.shape), own.dtype)], name=name)[0]


def put_slots(out, both, got):
    t, near, far, across = gather_slots()
    out[t] = both[0]
    out[far] = both[1]
    out[near] = got[0]
    out[across] = got[1]


def slot_kernel(both, got, out):
    put_slots(out, both, got)


def run_slots(call, both, got, name):
    return call(slot_kernel, (both, got), [arr((4, *both.shape[1:]), both.dtype)], name=name)[0]


def gelu_parts(h):
    cdf = 0.5 * (1.0 + lax.erf(h * 0.7071067811865476))
    density = jnp.exp(-0.5 * h * h) * 0.3989422804014327
    return h * cdf, cdf + h * density


def experts_up(chunk, items, heads, info, vecs, kept, both, got, w_out, up_bias, w_up, *refs):
    width = heads * HEAD
    d = kept.shape[2]
    middle, normed, active, slopes, ctx = refs
    first = is_first()
    put_slots(ctx, both, got)
    mids, n_rows = [], []
    for j in range(2):
        total = jnp.zeros((PAD, d), f32)
        for s in range(4):
            total = total + dot(ctx[s][:, j * width : (j + 1) * width], w_out[s])
        mid = kept[j].astype(f32) + total + vecs[2:3, :]
        mids.append(mid)
        unit, _ = unit_rows(mid)
        n_row = (unit * vecs[3:4, :] + vecs[4:5, :]).astype(bf16)
        normed[j] = n_row
        n_rows.append(n_row)
    middle[...] = jnp.where(first, mids[0], mids[1])
    for j in range(2):
        e = expert_of(info, items, 2 * chunk + j)
        h = dot(n_rows[j], w_up[e]) + up_bias[pl.ds(e, 1), :]
        value, slope = gelu_parts(h)
        active[j] = value.astype(bf16)
        slopes[j] = slope


def run_experts_up(call, chunk, items, heads, info, vecs, kept, ctxs, w_out, up_bias, w_up):
    width = heads * HEAD
    d = kept.shape[2]
    ff = w_up.shape[2]
    return call(
        functools.partial(experts_up, chunk, items, heads),
        (info, vecs, kept, *ctxs, w_out, up_bias, w_up),
        [
            arr((PAD, d), f32),
            arr((2, PAD, d), bf16),
            arr((2, PAD, ff), bf16),
            arr((2, PAD, ff), f32),
        ],
        [VMEM((4, PAD, 2 * width), bf16)],
        name="experts_up_%d" % chunk,
    )


def experts_back(items, info, masked, w_up, w_down, *refs):
    chunks = items // 2
    active, slopes, refs = refs[:chunks], refs[chunks : 2 * chunks], refs[2 * chunks :]
    sides, small, ghid = refs[:4], refs[4], refs[5:]
    first = is_first()
    zero = jnp.zeros((1, w_up.shape[2]), f32)
    sums = [zero, zero]
    for k in range(chunks):
        parts, downs = [], []
        for j in range(2):
            e = expert_of(info, items, 2 * k + j)
            wu = w_up[e]
            wd = w_down[e]
            gh = (dot(masked[2 * k + j], wd, NT) * slopes[k][j]).astype(bf16)
            ghid[k][j] = gh
            parts.append(dot(gh, wu, NT))
            downs.append(dot(active[k][j], wd))
            line = jnp.sum(gh.astype(f32), 0, keepdims=True)
            flag = expert_vector(info, items, 2 * k + j)
            for x in range(2):
                sums[x] = sums[x] + jnp.where(flag == x, line, 0.0)
        values = (
            jnp.where(first, parts[0], parts[1]),
            jnp.where(first, parts[1], parts[0]),
            jnp.where(first, downs[0], downs[1]),
            jnp.where(first, downs[1], downs[0]),
        )
        for side, value in zip(sides, values):
            side[k] = value.astype(bf16)
    small[...] = jnp.zeros_like(small)
    small[0:1, :] = sums[0]
    small[1:2, :] = sums[1]


def run_experts_back(call, items, info, masked, w_up, w_down, active, slopes):
    d = masked.shape[2]
    ff = w_up.shape[2]
    chunks = items // 2
    return call(
        functools.partial(experts_back, items),
        (info, masked, w_up, w_down, *active, *slopes),
        [arr((chunks, PAD, d), bf16)] * 4 + [arr((8, ff), f32)] + [arr((2, PAD, ff), bf16)] * chunks,
        limit=20,
        name="experts_back",
    )


def expert_grads(items, merged, tailed, info, *refs):
    chunks = items // 2
    tail, refs = (refs[0], refs[1:]) if tailed else (None, refs)
    lefts, refs = refs[:chunks], refs[chunks:]
    rights = refs[: 1 if merged else chunks]
    send, keep, total = refs[len(rights) :]
    for i in range(items):
        e = expert_of(info, items, i)
        right = rights[0][i] if merged else rights[i // 2][i % 2]
        term = dot(lefts[i // 2][i % 2], right, TN)
        if i == 0:
            total[e] = term
            total[1 - e] = jnp.zeros_like(term)
        else:
            total[e] += term
    one, _ = places(True)
    count = keep.shape[0]
    keep[...] = total[one].astype(bf16)
    send[0:count] = total[1 - one].astype(bf16)
    if tailed:
        put_tail(send, count, tail[...])


def run_expert_grads(call, items, info, lefts, rights, name, tail=()):
    merged = len(rights) == 1
    shape = (lefts[0].shape[2], rights[0].shape[2])
    return call(
        functools.partial(expert_grads, items, merged, len(tail) > 0),
        (info, *tail, *lefts, *rights),
        [arr((shape[0] + 2 * TAIL * len(tail), shape[1]), bf16), arr(shape, bf16)],
        [VMEM((2, *shape), f32)],
        name=name,
    )


def own_expert(info, items, chunk):
    return jnp.where(is_first(), expert_vector(info, items, 2 * chunk), expert_vector(info, items, 2 * chunk + 1))


def item_weight(info, items, item, counts):
    first, second = row_weight(counts)
    return jnp.where(expert_vector(info, items, item) == 0, first, second)


def own_weight(info, items, chunk, counts):
    first, second = row_weight(counts)
    return jnp.where(own_expert(info, items, chunk) == 0, first, second)


def norm_two_back(chunks, vecs, masked, pair, far, *refs):
    middles, branch, (grad_mid, small) = refs[:chunks], refs[chunks : 2 * chunks], refs[2 * chunks :]
    small[...] = jnp.zeros_like(small)
    for k in range(chunks):
        own_cot = jnp.where(is_first(), masked[2 * k], masked[2 * k + 1]).astype(f32)
        unit, scale = unit_rows(middles[k][...])
        grad = pair[k].astype(f32) + far[k].astype(f32)
        out = own_cot + norm_back(grad, unit, scale, vecs[3:4, :])
        grad_mid[k] = out
        branch[k][...] = out.astype(bf16)
        for i, value in enumerate((grad * unit, grad, out)):
            small[3 * k + i : 3 * k + i + 1, :] = jnp.sum(value, 0, keepdims=True)


def run_norm_two_back(call, vecs, masked, pair, far, middles):
    chunks = len(middles)
    return call(
        functools.partial(norm_two_back, chunks),
        (vecs, masked, pair, far, *middles),
        [arr(pair.shape[1:], bf16)] * chunks
        + [arr(pair.shape, f32), arr((-(-3 * chunks // 8) * 8, pair.shape[2]), f32)],
        name="norm_two_back",
    )


def attention_backward(
    chunk, heads, info, own, other, w_out, proj, w_t, kept,
    gproj, small, small_one, part_own, part_other,
):
    width = heads * HEAD
    first = is_first()
    parts = []
    small[...] = jnp.zeros_like(small)
    small_one[...] = jnp.zeros_like(small_one)
    for j in range(2):
        live = live_of(info, 2 * chunk + j)
        a, b = (own, other) if j == 0 else (other, own)
        branch = jnp.where(first, a[...], b[...])
        gctx = dot(branch, w_out[...], NT).astype(bf16)
        p_row = proj[j]
        key_live = iota((PAD, PAD), 1) < live
        gq, gk, gv = [], [], []
        for h in range(heads):
            q = p_row[:, h * HEAD : (h + 1) * HEAD]
            k = p_row[:, width + h * HEAD : width + (h + 1) * HEAD]
            v = p_row[:, 2 * width + h * HEAD : 2 * width + (h + 1) * HEAD]
            gc = gctx[:, h * HEAD : (h + 1) * HEAD]
            s = jnp.where(key_live, dot(q, k, NT) * 0.125, -1e30)
            e = jnp.exp(s - jnp.max(s, -1, keepdims=True))
            att = e * (1.0 / jnp.sum(e, -1, keepdims=True))
            ga = dot(gc, v, NT)
            gs = (att * (ga - jnp.sum(ga * att, -1, keepdims=True))).astype(bf16)
            gv.append(dot(att.astype(bf16), gc, TN))
            gq.append(dot(gs, k) * 0.125)
            gk.append(dot(gs, q, TN) * 0.125)
        gp = jnp.concatenate(gq + gk + gv, axis=1).astype(bf16)
        gproj[j] = gp
        small[j : j + 1, :] = jnp.sum(gp.astype(f32), 0, keepdims=True)
        part = dot(gp, w_t[...])
        parts.append(part)
        unit, _ = unit_rows(kept[j].astype(f32))
        small_one[2 * j : 2 * j + 1, :] = jnp.sum(part * unit, 0, keepdims=True)
        small_one[2 * j + 1 : 2 * j + 2, :] = jnp.sum(part, 0, keepdims=True)
    part_own[...] = jnp.where(first, parts[0], parts[1]).astype(bf16)
    part_other[...] = jnp.where(first, parts[1], parts[0]).astype(bf16)


def run_attention_backward(call, chunk, heads, info, own, other, w_out, proj, w_t, kept):
    width = heads * HEAD
    d = own.shape[1]
    side = arr((PAD, d), bf16)
    return call(
        functools.partial(attention_backward, chunk, heads),
        (info, own, other, w_out, proj, w_t, kept),
        [arr((2, PAD, 3 * width), bf16), arr((8, 3 * width), f32), arr((8, d), f32), side, side],
        name="attention_backward_%d" % chunk,
    )


def attention_grads(items, heads, info, counts, *refs):
    width = heads * HEAD
    chunks = items // 2
    own, other, gproj, normed, ctx = (refs[i * chunks : (i + 1) * chunks] for i in range(5))
    send, keep, both = refs[5 * chunks :]
    first = is_first()
    rows = 3 * width
    total = jnp.zeros((rows, keep.shape[1]), f32)
    total_out = jnp.zeros((width, keep.shape[1]), f32)
    for k in range(chunks):
        for j in range(2):
            weight = item_weight(info, items, 2 * k + j, counts)
            total = total + dot((gproj[k][j].astype(f32) * weight).astype(bf16), normed[k][j], TN)
            a, b = (own, other) if j == 0 else (other, own)
            branch = jnp.where(first, a[k][...], b[k][...]).astype(f32)
            branch = (branch * weight).astype(bf16)
            total_out = total_out + dot(ctx[k][:, j * width : (j + 1) * width], branch, TN)
    half = 2 * width
    both[0] = total[:half].astype(bf16)
    both[1, 0 : rows - half] = total[half:].astype(bf16)
    both[1, rows - half :] = total_out.astype(bf16)
    one, _ = places(True)
    keep[...] = both[one]
    send[...] = both[1 - one]


def run_attention_grads(call, items, heads, info, counts, own, other, gproj, normed, ctx):
    width = heads * HEAD
    d = own[0].shape[1]
    return call(
        functools.partial(attention_grads, items, heads),
        (info, counts, *own, *other, *gproj, *normed, *ctx),
        [arr((2 * width, d), bf16)] * 2,
        [VMEM((2, 2 * width, d), bf16)],
        name="attention_grads",
    )


def norm_one_back(items, info, counts, vecs, grad_mid, pair, far, *refs):
    chunks = items // 2
    kept, grad_own = refs[:chunks], refs[chunks]
    for k in range(chunks):
        x = jnp.where(is_first(), kept[k][0], kept[k][1]).astype(f32)
        unit, scale = unit_rows(x)
        grad = pair[k].astype(f32) + far[k].astype(f32)
        total = grad_mid[k] + norm_back(grad, unit, scale, vecs[0:1, :])
        grad_own[k] = (total * own_weight(info, items, k, counts)).astype(bf16)


def run_norm_one_back(call, items, info, counts, vecs, grad_mid, pair, far, kept):
    return call(
        functools.partial(norm_one_back, items),
        (info, counts, vecs, grad_mid, pair, far, *kept),
        [arr(pair.shape, bf16)],
        name="norm_one_back",
    )[0]


def output_rows(items, info, down_bias, pair, far, *refs):
    chunks = items // 2
    middles, out = refs[:chunks], refs[chunks]
    for k in range(chunks):
        bias = jnp.where(own_expert(info, items, k) == 0, down_bias[0:1, :], down_bias[1:2, :])
        out[k] = (middles[k][...] + (pair[k].astype(f32) + far[k].astype(f32)) + bias).astype(bf16)


def run_output_rows(call, items, info, down_bias, pair, far, middles):
    return call(
        functools.partial(output_rows, items),
        (info, down_bias, pair, far, *middles),
        [arr(pair.shape, bf16)],
        name="output_rows",
    )[0]


def assemble(items, own, other, out, buf, low, sem):
    first = is_first()
    for k in range(items // 2):
        for j in range(2):
            a, b = (own, other) if j == 0 else (other, own)
            buf[pl.ds((2 * k + j) * SEQ, PAD), :] = jnp.where(first, a[k], b[k]).astype(f32)
    low[...] = buf[0 : items * SEQ, :].astype(bf16)
    copy = pltpu.make_async_copy(low, out, sem)
    copy.start()
    copy.wait()


def run_assemble(call, items, own, other, name):
    d = own.shape[2]
    return call(
        functools.partial(assemble, items),
        (own, other),
        [arr((items * SEQ, d), bf16)],
        [VMEM((items * SEQ + 16, d), f32), VMEM((items * SEQ, d), bf16), DMA],
        out_specs=[hspec()],
        name=name,
    )[0]


def swap(value, axis, size, bit):
    return lax.ppermute(value, axis, [(i, i ^ bit) for i in range(size)])


def add_kernel(a, b, out):
    out[...] = (a[...].astype(f32) + b[...].astype(f32)).astype(out.dtype)


def run_add(call, a, b, name):
    return call(add_kernel, (a, b), [arr(a.shape, a.dtype)], name=name)[0]


def pair_kernel(chunks, *refs):
    own, got, out = refs[:chunks], refs[chunks : 2 * chunks], refs[2 * chunks]
    for k in range(chunks):
        out[k] = (own[k][...].astype(f32) + got[k][...].astype(f32)).astype(bf16)


def run_pair(call, own, got, name):
    return call(
        functools.partial(pair_kernel, len(own)), (*own, *got), [arr((len(own), *own[0].shape), bf16)], name=name
    )[0]


def split_rows(rows):
    high = rows.astype(bf16)
    return high, (rows - high.astype(f32)).astype(bf16)


def add_tail(held, got, at):
    return held[...] + got[at : at + TAIL].astype(f32) + got[at + TAIL : at + 2 * TAIL].astype(f32)


def put_tail(out, at, rows):
    out[at : at + TAIL], out[at + TAIL : at + 2 * TAIL] = split_rows(rows)


def attach_kernel(rows, tail, out):
    count = rows.shape[0]
    out[0:count] = rows[...]
    put_tail(out, count, tail[...])


def half_of(ref, index, count):
    return ref[pl.ds(pl.multiple_of(index * count, count), count), :]


def fold_step(turned, tailed, keep, got, *refs):
    refs = list(refs)
    held = refs.pop(0) if tailed else None
    send_next, keep_next = refs[:2]
    count = keep_next.shape[0]
    _, two = places(turned)
    for out, index in ((keep_next, two), (send_next, 1 - two)):
        total = half_of(keep, index, count).astype(f32) + half_of(got, index, count).astype(f32)
        out[0:count] = total.astype(bf16)
    if tailed:
        tail = add_tail(held, got, 2 * count)
        refs[2][...] = tail
        put_tail(send_next, count, tail)


def add_step(tailed, handed, sends, keep, got, *refs):
    refs = list(refs)
    held = refs.pop(0) if tailed else None
    given = [refs.pop(0) for _ in range(handed)]
    out = refs.pop(0)
    count = out.shape[0]
    total = (keep[...].astype(f32) + got[0:count].astype(f32)).astype(bf16)
    out[...] = total
    if tailed:
        tail = add_tail(held, got, count)
        refs.pop(0)[...] = tail
        if sends:
            send = refs.pop(0)
            send[0:count] = total
            put_tail(send, count, tail)
    if handed == 1:
        refs[0][...] = given[0][...]
    if handed == 2:
        attach_kernel(given[0], given[1], refs[0])


def join_kernel(turned, own, other, out):
    _, bit = places(turned)
    out[bit] = own[...]
    out[1 - bit] = other[...]


PIECES = 4


def whole_kernel(scaled, *refs):
    counts = refs[0] if scaled else None
    own, other, out, buf, sems = refs[1:] if scaled else refs
    bit, _ = places(True)
    rows = own.shape[0] // PIECES
    copies = []
    for side, ref in enumerate((own, other)):
        half = bit if side == 0 else 1 - bit
        weight = 1.0
        if scaled:
            first, second = row_weight(counts)
            weight = jnp.where(half == 0, first, second)
        for i in range(PIECES):
            at = pl.ds(i * rows, rows)
            buf[side, at] = ref[at].astype(f32) * weight
            copy = pltpu.make_async_copy(buf.at[side, at], out.at[half, at], sems.at[side, i])
            copy.start()
            copies.append(copy)
    for copy in copies:
        copy.wait()


def run_whole(call, counts, own, other, name, limit):
    scaled = counts is not None
    shape = (2, *own.shape)
    return call(
        functools.partial(whole_kernel, scaled),
        ((counts,) if scaled else ()) + (own, other),
        [arr(shape, f32)],
        [VMEM(shape, f32), DMA((2, PIECES))],
        out_specs=[hspec()],
        limit=limit,
        name=name,
    )[0]


def attention_whole_kernel(rows, own, other, grad_qkv, grad_out, low, buf, sems):
    bit, _ = places(True)
    half = own.shape[0]
    low[bit] = own[...]
    low[1 - bit] = other[...]
    copies = []
    spans = [(grad_qkv, 0, 0, half), (grad_qkv, 1, half, rows - half), (grad_out, 1, 0, 2 * half - rows)]
    start = [0, 0, rows - half]
    for i, (out, side, to, count) in enumerate(spans):
        at = pl.ds(start[i], count)
        buf[side, at] = low[side, at].astype(f32)
        copy = pltpu.make_async_copy(buf.at[side, at], out.at[pl.ds(to, count)], sems.at[i])
        copy.start()
        copies.append(copy)
    for copy in copies:
        copy.wait()


def run_attention_whole(call, rows, own, other, name):
    half, d = own.shape
    return call(
        functools.partial(attention_whole_kernel, rows),
        (own, other),
        [arr((rows, d), f32), arr((2 * half - rows, d), f32)],
        [VMEM((2, half, d), bf16), VMEM((2, half, d), f32), DMA((3,))],
        out_specs=[hspec(), hspec()],
        limit=60,
        name=name,
    )


class Sum:
    def __init__(self, call, dp, tp, name, turned, keep, tail=None):
        self.call, self.dp, self.tp, self.name, self.keep, self.tail = call, dp, tp, name, keep, tail
        self.turned = turned
        self.steps = ((1, 2), (2, 1), (4, 4)) if turned else ((1, 1), (2, 2), (4, 4))

    def start(self, send):
        if self.dp == 8:
            self.got = self.cross(send, self.steps[0])
            return
        keep = self.keep
        send = send[: keep.shape[0]]
        low = (lax.axis_index("dp") % 2).astype(jnp.int32)
        high = (lax.axis_index("dp") // 2 % 2).astype(jnp.int32)
        one = jnp.where(lax.axis_index("tensor") % 2 == 0, low, high) if self.turned else low
        flat = jnp.where(one == 0, jnp.concatenate([keep, send]), jnp.concatenate([send, keep]))
        share = lax.psum_scatter(flat, "dp", scatter_dimension=0, tiled=True)
        whole = lax.all_gather(share, "dp", axis=0, tiled=True).reshape(2, *keep.shape)
        self.keep = jnp.where(one == 0, whole[0], whole[1])
        self.got = jnp.where(one == 0, whole[1], whole[0])
        if self.tail is not None:
            self.tail = lax.psum(self.tail, "dp")

    def cross(self, value, bits):
        dp, tp = self.dp, self.tp
        route = [(i * tp + t, (i ^ bits[t % 2]) * tp + t) for i in range(dp) for t in range(tp)]
        return lax.ppermute(value, ("dp", "tensor"), route)

    def quarter(self):
        if self.dp != 8:
            return
        rows, d = self.keep.shape
        tailed = self.tail is not None
        ins = (self.keep, self.got) + ((self.tail,) if tailed else ())
        outs = [arr((rows // 2 + (2 * TAIL if tailed else 0), d), bf16), arr((rows // 2, d), bf16)]
        outs += [arr(self.tail.shape, f32)] if tailed else []
        send, self.keep, *tail = self.call(
            functools.partial(fold_step, self.turned, tailed), ins, outs, name=self.name + "_half"
        )
        self.tail = tail[0] if tailed else None
        self.got = self.cross(send, self.steps[1])

    def add(self, name, sends, handed):
        tailed = self.tail is not None
        rows, d = self.keep.shape
        ins = (self.keep, self.got) + ((self.tail,) if tailed else ()) + handed
        outs = [arr((rows, d), bf16)]
        outs += [arr(self.tail.shape, f32)] if tailed else []
        outs += [arr((rows + 2 * TAIL, d), bf16)] if tailed and sends else []
        if handed:
            outs.append(arr((handed[0].shape[0] + 2 * TAIL * (len(handed) - 1), d), bf16))
        out = self.call(
            functools.partial(add_step, tailed, len(handed), sends), ins, outs, name=self.name + name
        )
        self.keep = out[0]
        if tailed:
            self.tail = out[1]
        return out[2] if tailed and sends else out[0], out[-1]

    def middle(self, *handed):
        if self.dp != 8:
            return handed[0] if handed else None
        send, given = self.add("_quarter", True, handed)
        self.got = self.cross(send, self.steps[2])
        return given

    def back_half(self):
        if self.dp != 8:
            return
        self.add("_sum", False, ())
        self.got = self.cross(self.keep, self.steps[1])

    def back_whole(self):
        if self.dp != 8:
            return
        rows, d = self.keep.shape
        out = self.call(functools.partial(join_kernel, self.turned), (self.keep, self.got), [arr((2, rows, d), bf16)], name=self.name + "_join")[0]
        self.keep = out.reshape(2 * rows, d)
        self.got = self.cross(self.keep, self.steps[0])


def collect(items, heads, info, counts, two, cots, exp, *refs):
    width = heads * HEAD
    chunks = items // 2
    attn, one, (out,) = refs[:chunks], refs[chunks : 2 * chunks], refs[2 * chunks :]
    out[...] = jnp.zeros_like(out)
    weights = [own_weight(info, items, k, counts) for k in range(chunks)]
    out[0:3, :] = sum(two[3 * k : 3 * k + 3, :] * weights[k] for k in range(chunks)) * 0.5
    each = [item_weight(info, items, i, counts) for i in range(items)]
    out[3:5, :] = sum(one[i // 2][2 * (i % 2) : 2 * (i % 2) + 2, :] * each[i] for i in range(items))
    out[8:10, :] = exp[0:2, :]
    out[10:12, :] = cots[0:2, :]
    out[12:13, 0 : 3 * width] = sum(attn[i // 2][i % 2 : i % 2 + 1, :] * each[i] for i in range(items))


def small_outputs(heads, counts, small, *outs):
    width = heads * HEAD
    d = small.shape[1]
    for i in range(5):
        outs[i][...] = small[i : i + 1, :].reshape(d)
    for i, weight in enumerate(row_weight(counts)):
        outs[5][i : i + 1, :] = small[8 + i : 9 + i, :] * weight
        outs[6][i : i + 1, :] = small[10 + i : 11 + i, :] * weight
    row = small[12:13, :]
    outs[7][0:1, :] = row[:, 0:width]
    outs[7][1:2, :] = row[:, 2 * width : 3 * width]


def run_small_outputs(call, heads, counts, small):
    d = small.shape[1]
    return call(
        functools.partial(small_outputs, heads),
        (counts, small),
        [arr((d,), f32)] * 5 + [arr((2, d), f32)] * 2 + [arr((2, heads * HEAD), f32)],
        name="small_outputs",
    )


def row_sum_kernel(small, got, out):
    out[0:8, :] = small[0:8, :] + got[0:8, :]
    out[8:, :] = small[8:, :]


def run_row_sum(call, small, got, name):
    return call(row_sum_kernel, (small, got), [arr(small.shape, f32)], name=name)[0]


def local(
    dp, tp,
    tokens, token_mask, expert_type, cotangent, ln1_gain, ln1_bias, w_qkv, qv_bias, w_out, out_bias,
    ln2_gain, ln2_bias, w_up, up_bias, w_down, down_bias,
):
    rows, d = tokens.shape
    items = rows // SEQ
    width = w_qkv.shape[2]
    heads = width // HEAD
    core_swap = lambda v: swap(v, "tensor", tp, 1)
    far_swap = lambda v: swap(v, "tensor", tp, 2)
    chunks = items // 2
    call = Order()
    w_t = w_qkv.transpose(1, 2, 0).reshape(3 * width, d)

    w_far = far_swap(w_out)
    c0, p, n, x, info, totals, vecs = run_front(
        call, items, heads, token_mask, expert_type, tokens, w_t, qv_bias,
        (ln1_gain, ln1_bias, out_bias, ln2_gain, ln2_bias),
    )
    ctx, proj, normed_one, kept, ctx_far, ctxs = [c0], [p], [n], [x], [far_swap(c0)], []
    for k in range(1, chunks):
        c0, p, n, x = run_attention_forward(call, k, heads, info, vecs, tokens, w_t, qv_bias)
        for group, value in zip((ctx, proj, normed_one, kept, ctx_far), (c0, p, n, x, far_swap(c0))):
            group.append(value)
    both = run_pack(call, ctx[0], ctx_far[0], "context_pack_0")
    ctxs.append((both, core_swap(both)))
    w_both = run_pack(call, w_out, w_far, "w_out_pack")
    w_got = core_swap(w_both)
    masked, small_c = run_mask_rows(call, items, info, cotangent)
    w_all = run_slots(call, w_both, w_got, "w_out_all")
    middle, normed_two, active, slopes = [], [], [], []
    for k in range(chunks):
        out = run_experts_up(call, k, items, heads, info, vecs, kept[k], ctxs[k], w_all, up_bias, w_up)
        for group, value in zip((middle, normed_two, active, slopes), out):
            group.append(value)
        if k + 1 < chunks:
            both = run_pack(call, ctx[k + 1], ctx_far[k + 1], "context_pack_%d" % (k + 1))
            ctxs.append((both, core_swap(both)))

    send, keep = run_expert_grads(call, items, info, active, [masked], "down_grads", (totals,))
    sum_down = Sum(call, dp, tp, "down", True, keep, totals)
    sum_down.start(send)
    part_own, part_other, down_own, down_other, small_e, *ghid = run_experts_back(
        call, items, info, masked, w_up, w_down, active, slopes
    )
    part_got = core_swap(part_other)
    down_got = core_swap(down_other)
    part = run_add(call, part_own, part_got, "part")
    part_far = far_swap(part)
    down = run_add(call, down_own, down_got, "expert_rows")
    down_far = far_swap(down)
    up_send, up_keep = run_expert_grads(call, items, info, normed_two, ghid, "up_grads")
    sum_up = Sum(call, dp, tp, "up", True, up_keep)
    sum_down.quarter()
    *branch_own, grad_mid, small_n = run_norm_two_back(call, vecs, masked, part, part_far, middle)
    branch_other = [core_swap(b) for b in branch_own]
    up_send = sum_down.middle(up_send)
    sum_up.start(up_send)
    gproj, small_a, small_o, one_own, one_got = [], [], [], [], []
    for k in range(chunks):
        g, sa, so, po, pt = run_attention_backward(
            call, k, heads, info, branch_own[k], branch_other[k], w_out, proj[k], w_t, kept[k]
        )
        for group, value in zip((gproj, small_a, small_o, one_own, one_got), (g, sa, so, po, core_swap(pt))):
            group.append(value)
    sum_up.quarter()
    sum_down.back_half()
    totals = sum_down.tail
    small = call(
        functools.partial(collect, items, heads),
        (info, totals, small_n, small_c, small_e, *small_a, *small_o),
        [arr((TAIL, d), f32)],
        name="collect",
    )[0]
    attn_send, keep = run_attention_grads(
        call, items, heads, info, totals, branch_own, branch_other, gproj, normed_one, ctx
    )
    one = run_pair(call, one_own, one_got, "one")
    one_far = far_swap(one)
    sum_attn = Sum(call, dp, tp, "attn", True, keep, small)
    attn_send = sum_up.middle(attn_send, small)
    sum_attn.start(attn_send)
    sum_down.back_whole()
    sum_attn.quarter()
    grad_own = run_norm_one_back(call, items, info, totals, vecs, grad_mid, one, one_far, kept)
    grad_other = core_swap(grad_own)
    sum_up.back_half()
    sum_attn.middle()
    out_own = run_output_rows(call, items, info, down_bias, down, down_far, middle)
    out_other = core_swap(out_own)
    grad_tokens = run_assemble(call, items, grad_own, grad_other, "grad_tokens")
    sum_up.back_whole()
    output = run_assemble(call, items, out_own, out_other, "output")
    sum_attn.back_half()
    small = sum_attn.tail
    small = run_row_sum(call, small, core_swap(small), "norm_rows_core")
    small_far = far_swap(small)
    sum_attn.back_whole()
    small = run_row_sum(call, small, small_far, "norm_rows_far")
    smalls = run_small_outputs(call, heads, totals, small)
    grad_down = run_whole(call, totals, sum_down.keep, sum_down.got, "down_whole", 20)
    grad_up = run_whole(call, totals, sum_up.keep, sum_up.got, "up_whole", 60)
    grad_qkv, grad_out = run_attention_whole(call, 3 * width, sum_attn.keep, sum_attn.got, "attn_whole")
    return (
        output,
        grad_tokens,
        smalls[3],
        smalls[4],
        grad_qkv.reshape(3, width, d).transpose(2, 0, 1),
        smalls[7],
        grad_out,
        smalls[2],
        smalls[0],
        smalls[1],
        grad_up.reshape(w_up.shape),
        smalls[5],
        grad_down.reshape(w_down.shape),
        smalls[6],
        totals[:2, 0].astype(jnp.int32),
    )


def solution(mesh):
    in_specs = (
        P("dp", None),
        P("dp"),
        P("dp"),
        P("dp", None),
        P(),
        P(),
        P(None, None, "tensor"),
        P(None, "tensor"),
        P("tensor", None),
        P(),
        P(),
        P(),
        P(None, None, "tensor"),
        P(None, "tensor"),
        P(None, "tensor", None),
        P(),
    )
    out_specs = (
        P("dp", None),
        P("dp", None),
        P(),
        P(),
        P(None, None, "tensor"),
        P(None, "tensor"),
        P("tensor", None),
        P(),
        P(),
        P(),
        P(None, None, "tensor"),
        P(None, "tensor"),
        P(None, "tensor", None),
        P(),
        P(),
    )
    return jax.shard_map(
        functools.partial(local, mesh.shape["dp"], mesh.shape["tensor"]),
        mesh=mesh,
        in_specs=in_specs,
        out_specs=out_specs,
        check_vma=False,
    )
```

```python
import functools

import jax
import jax.numpy as jnp
from jax import lax
from jax.experimental import pallas as pl
from jax.experimental.pallas import tpu as pltpu
from jax.sharding import PartitionSpec as P

HEAD = 64
PATCHES = 197
CAP = 40
SEQ = PATCHES + CAP
PAD = 240
ATT = 256
STAGE = 2 * SEQ + 32
TAIL = 16

epsilon = 1e-05
f32 = jnp.float32
bf16 = jnp.bfloat16

NT = (((1,), (1,)), ((), ()))
NN = (((1,), (0,)), ((), ()))
TN = (((0,), (0,)), ((), ()))

VMEM = pltpu.VMEM
SMEM = pltpu.SMEM
DMA = pltpu.SemaphoreType.DMA


def dot(a, b, dims=NN):
    return lax.dot_general(a, b, dims, preferred_element_type=f32)


def iota(shape, dim):
    return lax.broadcasted_iota(jnp.int32, shape, dim)


def unit_rows(x):
    mean = jnp.mean(x, -1, keepdims=True)
    centered = x - mean
    scale = lax.rsqrt(jnp.mean(centered * centered, -1, keepdims=True) + epsilon)
    return centered * scale, scale


def norm_back(grad, unit, scale, gain):
    t = grad * gain
    return scale * (
        t - jnp.mean(t, -1, keepdims=True) - unit * jnp.mean(t * unit, -1, keepdims=True)
    )


def vspec():
    return pl.BlockSpec(memory_space=VMEM)


def hspec():
    return pl.BlockSpec(memory_space=pltpu.HBM)


def aspec():
    return pl.BlockSpec(memory_space=pl.ANY)


class Order:
    def __init__(self):
        self.last = None

    def __call__(self, kernel, ins, outs, scratch=(), limit=16, specs=None, out_specs=None, name=None):
        taken = len(ins)
        behind = () if self.last is None or any(a is self.last for a in ins) else (self.last,)

        def body(*refs):
            kernel(*refs[:taken], *refs[taken + len(behind) :])

        results = pl.pallas_call(
            body,
            out_shape=list(outs),
            in_specs=list(specs or [vspec() for _ in ins]) + [aspec() for _ in behind],
            out_specs=list(out_specs or [vspec() for _ in outs]),
            scratch_shapes=list(scratch),
            compiler_params=pltpu.CompilerParams(vmem_limit_bytes=limit * 1024 * 1024),
            cost_estimate=pl.CostEstimate(flops=1, bytes_accessed=1, transcendentals=0),
            name=name,
        )(*ins, *behind)
        self.last = results[0]
        return results


def arr(shape, dtype):
    return jax.ShapeDtypeStruct(shape, dtype)


def position():
    return lax.axis_index("tensor")


def is_first():
    return lax.rem(position(), 2) == 0


def places(turned):
    place = lax.axis_index("dp")
    low = lax.rem(place, 2)
    high = lax.rem(lax.div(place, 2), 2)
    if not turned:
        return low, high
    first = is_first()
    return jnp.where(first, low, high), jnp.where(first, high, low)


def stage_rows(rows, buf, chunk):
    low = 2 * chunk * SEQ
    high = low + 2 * SEQ
    base = low // 16 * 16
    top = min(rows.shape[0], -(-high // 16) * 16)
    buf[0 : top - base] = rows[base:top].astype(f32)
    return [low - base, low - base + SEQ]


def item_rows(buf, offset, count, live=SEQ):
    rows = buf[pl.ds(offset, count), :]
    return jnp.where(iota(rows.shape, 0) < live, rows, 0.0)


def live_of(info, item):
    return info[item : item + 1, 0:1].astype(jnp.int32)


def expert_vector(info, items, item):
    return info[items + item : items + item + 1, 0:1]


def expert_of(info, items, item):
    return jnp.max(info[items + item : items + item + 1, :]).astype(jnp.int32)


def row_weight(counts):
    both = counts[0:1, 0:1] + counts[1:2, 0:1]
    return both / (2.0 * counts[0:1, 0:1]), both / (2.0 * counts[1:2, 0:1])


def attention_items(chunk, heads, info, rows, w_t, qv_bias, gain, bias, ctx, proj, normed, kept, buf):
    width = heads * HEAD
    offsets = stage_rows(rows, buf, chunk)
    b_three = jnp.concatenate([qv_bias[0:1, :], jnp.zeros((1, width), f32), qv_bias[1:2, :]], axis=1)
    for j in range(2):
        live = live_of(info, 2 * chunk + j)
        x = item_rows(buf, offsets[j], ATT)
        kept[j] = x[:PAD].astype(bf16)
        unit, _ = unit_rows(x)
        n_row = (unit * gain + bias).astype(bf16)
        normed[j] = n_row[:PAD]
        p_row = (dot(n_row, w_t[...], NT) + b_three).astype(bf16)
        proj[j] = p_row[:PAD]
        key_live = iota((ATT, ATT), 1) < live
        for h in range(heads):
            q = p_row[:, h * HEAD : (h + 1) * HEAD]
            k = p_row[:, width + h * HEAD : width + (h + 1) * HEAD]
            v = p_row[:, 2 * width + h * HEAD : 2 * width + (h + 1) * HEAD]
            s = jnp.where(key_live, dot(q, k, NT) * 0.125, -1e30)
            e = jnp.exp(s - jnp.max(s, -1, keepdims=True))
            att = (e * (1.0 / jnp.sum(e, -1, keepdims=True))).astype(bf16)
            c = dot(att, v).astype(bf16)
            at = j * width + h * HEAD
            ctx[:, at : at + HEAD] = c[:PAD]


def front(
    items, heads, mask_h, kind_h, tokens_h, w_h, qv_h, *refs
):
    vectors_h, refs = refs[:5], refs[5:]
    ctx, proj, normed, kept, info, counts, vecs = refs[:7]
    mask, kind, tokens, w_t, qv_bias, lines, buf, sems = refs[7:]
    pairs = [(mask_h, mask), (kind_h, kind), (tokens_h, tokens), (w_h, w_t), (qv_h, qv_bias)]
    pairs += [(v, lines.at[i]) for i, v in enumerate(vectors_h)]
    copies = [pltpu.make_async_copy(a, b, sems.at[i]) for i, (a, b) in enumerate(pairs)]
    for c in copies:
        c.start()
    copies[0].wait()
    copies[1].wait()
    total = 0
    second = 0
    row = iota(info.shape, 0)
    value = jnp.zeros(info.shape, f32)
    for i in range(items):
        n = PATCHES
        for slot in range(CAP):
            n = n + mask[i * SEQ + PATCHES + slot]
        e = kind[i * SEQ]
        total = total + n
        second = second + n * e
        value = jnp.where(row == i, n.astype(f32), value)
        value = jnp.where(row == items + i, e.astype(f32), value)
    info[...] = value
    row = iota(counts.shape, 0)
    counts[...] = jnp.where(
        row == 0, (total - second).astype(f32), jnp.where(row == 1, second.astype(f32), 0.0)
    )
    for c in copies[2:]:
        c.wait()
    for i in range(5):
        vecs[i : i + 1, :] = lines[i : i + 1, :]
    attention_items(
        0, heads, info, tokens[...], w_t, qv_bias, lines[0:1, :], lines[1:2, :], ctx, proj, normed, kept, buf
    )


def run_front(call, items, heads, mask, kind, tokens, w_t, qv_bias, vectors):
    width = heads * HEAD
    rows, d = tokens.shape
    ins = (mask, kind, tokens, w_t, qv_bias, *vectors)
    return call(
        functools.partial(front, items, heads),
        ins,
        [
            arr((PAD, 2 * width), bf16),
            arr((2, PAD, 3 * width), bf16),
            arr((2, PAD, d), bf16),
            arr((2, PAD, d), bf16),
            arr((2 * items, 128), f32),
            arr((TAIL, d), f32),
            arr((8, d), f32),
        ],
        [
            SMEM(mask.shape, jnp.int32),
            SMEM(kind.shape, jnp.int32),
            VMEM(tokens.shape, bf16),
            VMEM(w_t.shape, bf16),
            VMEM(qv_bias.shape, f32),
            VMEM((8, d), f32),
            VMEM((STAGE, d), f32),
            DMA((len(ins),)),
        ],
        specs=[hspec() for _ in ins],
        limit=60,
        name="front",
    )


def attention_forward(chunk, heads, *refs):
    hbm, outs, local, sems = refs[:5], refs[5:9], refs[9:14], refs[15]
    copies = [pltpu.make_async_copy(a, b, sems.at[i]) for i, (a, b) in enumerate(zip(hbm, local))]
    for c in copies:
        c.start()
    for c in copies:
        c.wait()
    info, vecs, tokens, w_t, qv_bias = local
    attention_items(
        chunk, heads, info, tokens[...], w_t, qv_bias, vecs[0:1, :], vecs[1:2, :], *outs, refs[14]
    )


def run_attention_forward(call, chunk, heads, info, vecs, tokens, w_t, qv_bias):
    width = heads * HEAD
    d = tokens.shape[1]
    ins = (info, vecs, tokens, w_t, qv_bias)
    return call(
        functools.partial(attention_forward, chunk, heads),
        ins,
        [arr((PAD, 2 * width), bf16), arr((2, PAD, 3 * width), bf16), arr((2, PAD, d), bf16), arr((2, PAD, d), bf16)],
        [VMEM(a.shape, a.dtype) for a in ins] + [VMEM((STAGE, d), f32), DMA((len(ins),))],
        specs=[hspec() for _ in ins],
        limit=60,
        name="attention_forward_%d" % chunk,
    )


def mask_rows(items, info, cot, masked, small, buf):
    d = cot.shape[1]
    buf[0 : items * SEQ] = cot[...].astype(f32)
    zero = jnp.zeros((1, d), f32)
    sums = [zero, zero]
    for i in range(items):
        rows = item_rows(buf, i * SEQ, PAD, live_of(info, i))
        masked[i] = rows.astype(bf16)
        line = jnp.sum(rows, 0, keepdims=True)
        e = expert_vector(info, items, i)
        for x in range(2):
            sums[x] = sums[x] + jnp.where(e == x, line, 0.0)
    small[...] = jnp.zeros_like(small)
    small[0:1, :] = sums[0]
    small[1:2, :] = sums[1]


def run_mask_rows(call, items, info, cot):
    d = cot.shape[1]
    return call(
        functools.partial(mask_rows, items),
        (info, cot),
        [arr((items, PAD, d), bf16), arr((8, d), f32)],
        [VMEM((items * SEQ + 16, d), f32)],
        name="mask_rows",
    )


def gather_slots():
    t = position()
    core = lax.rem(t, 2)
    return (t, t + 1 - 2 * core, lax.rem(t + 2, 4), lax.rem(t + 3 - 2 * core, 4))


def pack_kernel(own, far, out):
    out[0] = own[...]
    out[1] = far[...]


def run_pack(call, own, far, name):
    return call(pack_kernel, (own, far), [arr((2, *own.shape), own.dtype)], name=name)[0]


def put_slots(out, both, got):
    t, near, far, across = gather_slots()
    out[t] = both[0]
    out[far] = both[1]
    out[near] = got[0]
    out[across] = got[1]


def slot_kernel(both, got, out):
    put_slots(out, both, got)


def run_slots(call, both, got, name):
    return call(slot_kernel, (both, got), [arr((4, *both.shape[1:]), both.dtype)], name=name)[0]


def gelu_parts(h):
    cdf = 0.5 * (1.0 + lax.erf(h * 0.7071067811865476))
    density = jnp.exp(-0.5 * h * h) * 0.3989422804014327
    return h * cdf, cdf + h * density


def experts_up(chunk, items, heads, info, vecs, kept, both, got, w_out, up_bias, w_up, *refs):
    width = heads * HEAD
    d = kept.shape[2]
    middle, normed, active, slopes, ctx = refs
    first = is_first()
    put_slots(ctx, both, got)
    mids, n_rows = [], []
    for j in range(2):
        total = jnp.zeros((PAD, d), f32)
        for s in range(4):
            total = total + dot(ctx[s][:, j * width : (j + 1) * width], w_out[s])
        mid = kept[j].astype(f32) + total + vecs[2:3, :]
        mids.append(mid)
        unit, _ = unit_rows(mid)
        n_row = (unit * vecs[3:4, :] + vecs[4:5, :]).astype(bf16)
        normed[j] = n_row
        n_rows.append(n_row)
    middle[...] = jnp.where(first, mids[0], mids[1])
    for j in range(2):
        e = expert_of(info, items, 2 * chunk + j)
        h = dot(n_rows[j], w_up[e]) + up_bias[pl.ds(e, 1), :]
        value, slope = gelu_parts(h)
        active[j] = value.astype(bf16)
        slopes[j] = slope


def run_experts_up(call, chunk, items, heads, info, vecs, kept, ctxs, w_out, up_bias, w_up):
    width = heads * HEAD
    d = kept.shape[2]
    ff = w_up.shape[2]
    return call(
        functools.partial(experts_up, chunk, items, heads),
        (info, vecs, kept, *ctxs, w_out, up_bias, w_up),
        [
            arr((PAD, d), f32),
            arr((2, PAD, d), bf16),
            arr((2, PAD, ff), bf16),
            arr((2, PAD, ff), f32),
        ],
        [VMEM((4, PAD, 2 * width), bf16)],
        name="experts_up_%d" % chunk,
    )


def experts_back(items, info, masked, w_up, w_down, *refs):
    chunks = items // 2
    active, slopes, refs = refs[:chunks], refs[chunks : 2 * chunks], refs[2 * chunks :]
    sides, small, ghid = refs[:4], refs[4], refs[5:]
    first = is_first()
    zero = jnp.zeros((1, w_up.shape[2]), f32)
    sums = [zero, zero]
    for k in range(chunks):
        parts, downs = [], []
        for j in range(2):
            e = expert_of(info, items, 2 * k + j)
            wu = w_up[e]
            wd = w_down[e]
            gh = (dot(masked[2 * k + j], wd, NT) * slopes[k][j]).astype(bf16)
            ghid[k][j] = gh
            parts.append(dot(gh, wu, NT))
            downs.append(dot(active[k][j], wd))
            line = jnp.sum(gh.astype(f32), 0, keepdims=True)
            flag = expert_vector(info, items, 2 * k + j)
            for x in range(2):
                sums[x] = sums[x] + jnp.where(flag == x, line, 0.0)
        values = (
            jnp.where(first, parts[0], parts[1]),
            jnp.where(first, parts[1], parts[0]),
            jnp.where(first, downs[0], downs[1]),
            jnp.where(first, downs[1], downs[0]),
        )
        for side, value in zip(sides, values):
            side[k] = value.astype(bf16)
    small[...] = jnp.zeros_like(small)
    small[0:1, :] = sums[0]
    small[1:2, :] = sums[1]


def run_experts_back(call, items, info, masked, w_up, w_down, active, slopes):
    d = masked.shape[2]
    ff = w_up.shape[2]
    chunks = items // 2
    return call(
        functools.partial(experts_back, items),
        (info, masked, w_up, w_down, *active, *slopes),
        [arr((chunks, PAD, d), bf16)] * 4 + [arr((8, ff), f32)] + [arr((2, PAD, ff), bf16)] * chunks,
        limit=20,
        name="experts_back",
    )


def expert_grads(items, merged, tailed, info, *refs):
    chunks = items // 2
    tail, refs = (refs[0], refs[1:]) if tailed else (None, refs)
    lefts, refs = refs[:chunks], refs[chunks:]
    rights = refs[: 1 if merged else chunks]
    send, keep, total = refs[len(rights) :]
    for i in range(items):
        e = expert_of(info, items, i)
        right = rights[0][i] if merged else rights[i // 2][i % 2]
        term = dot(lefts[i // 2][i % 2], right, TN)
        if i == 0:
            total[e] = term
            total[1 - e] = jnp.zeros_like(term)
        else:
            total[e] += term
    one, _ = places(True)
    count = keep.shape[0]
    keep[...] = total[one].astype(bf16)
    send[0:count] = total[1 - one].astype(bf16)
    if tailed:
        put_tail(send, count, tail[...])


def run_expert_grads(call, items, info, lefts, rights, name, tail=()):
    merged = len(rights) == 1
    shape = (lefts[0].shape[2], rights[0].shape[2])
    return call(
        functools.partial(expert_grads, items, merged, len(tail) > 0),
        (info, *tail, *lefts, *rights),
        [arr((shape[0] + 2 * TAIL * len(tail), shape[1]), bf16), arr(shape, bf16)],
        [VMEM((2, *shape), f32)],
        name=name,
    )


def own_expert(info, items, chunk):
    return jnp.where(is_first(), expert_vector(info, items, 2 * chunk), expert_vector(info, items, 2 * chunk + 1))


def item_weight(info, items, item, counts):
    first, second = row_weight(counts)
    return jnp.where(expert_vector(info, items, item) == 0, first, second)


def own_weight(info, items, chunk, counts):
    first, second = row_weight(counts)
    return jnp.where(own_expert(info, items, chunk) == 0, first, second)


def norm_two_back(chunks, vecs, masked, pair, far, *refs):
    middles, branch, (grad_mid, small) = refs[:chunks], refs[chunks : 2 * chunks], refs[2 * chunks :]
    small[...] = jnp.zeros_like(small)
    for k in range(chunks):
        own_cot = jnp.where(is_first(), masked[2 * k], masked[2 * k + 1]).astype(f32)
        unit, scale = unit_rows(middles[k][...])
        grad = pair[k].astype(f32) + far[k].astype(f32)
        out = own_cot + norm_back(grad, unit, scale, vecs[3:4, :])
        grad_mid[k] = out
        branch[k][...] = out.astype(bf16)
        for i, value in enumerate((grad * unit, grad, out)):
            small[3 * k + i : 3 * k + i + 1, :] = jnp.sum(value, 0, keepdims=True)


def run_norm_two_back(call, vecs, masked, pair, far, middles):
    chunks = len(middles)
    return call(
        functools.partial(norm_two_back, chunks),
        (vecs, masked, pair, far, *middles),
        [arr(pair.shape[1:], bf16)] * chunks
        + [arr(pair.shape, f32), arr((-(-3 * chunks // 8) * 8, pair.shape[2]), f32)],
        name="norm_two_back",
    )


def attention_backward(
    chunk, heads, info, own, other, w_out, proj, w_t, kept,
    gproj, small, small_one, part_own, part_other,
):
    width = heads * HEAD
    first = is_first()
    parts = []
    small[...] = jnp.zeros_like(small)
    small_one[...] = jnp.zeros_like(small_one)
    for j in range(2):
        live = live_of(info, 2 * chunk + j)
        a, b = (own, other) if j == 0 else (other, own)
        branch = jnp.where(first, a[...], b[...])
        gctx = dot(branch, w_out[...], NT).astype(bf16)
        p_row = proj[j]
        key_live = iota((PAD, PAD), 1) < live
        gq, gk, gv = [], [], []
        for h in range(heads):
            q = p_row[:, h * HEAD : (h + 1) * HEAD]
            k = p_row[:, width + h * HEAD : width + (h + 1) * HEAD]
            v = p_row[:, 2 * width + h * HEAD : 2 * width + (h + 1) * HEAD]
            gc = gctx[:, h * HEAD : (h + 1) * HEAD]
            s = jnp.where(key_live, dot(q, k, NT) * 0.125, -1e30)
            e = jnp.exp(s - jnp.max(s, -1, keepdims=True))
            att = e * (1.0 / jnp.sum(e, -1, keepdims=True))
            ga = dot(gc, v, NT)
            gs = (att * (ga - jnp.sum(ga * att, -1, keepdims=True))).astype(bf16)
            gv.append(dot(att.astype(bf16), gc, TN))
            gq.append(dot(gs, k) * 0.125)
            gk.append(dot(gs, q, TN) * 0.125)
        gp = jnp.concatenate(gq + gk + gv, axis=1).astype(bf16)
        gproj[j] = gp
        small[j : j + 1, :] = jnp.sum(gp.astype(f32), 0, keepdims=True)
        part = dot(gp, w_t[...])
        parts.append(part)
        unit, _ = unit_rows(kept[j].astype(f32))
        small_one[2 * j : 2 * j + 1, :] = jnp.sum(part * unit, 0, keepdims=True)
        small_one[2 * j + 1 : 2 * j + 2, :] = jnp.sum(part, 0, keepdims=True)
    part_own[...] = jnp.where(first, parts[0], parts[1]).astype(bf16)
    part_other[...] = jnp.where(first, parts[1], parts[0]).astype(bf16)


def run_attention_backward(call, chunk, heads, info, own, other, w_out, proj, w_t, kept):
    width = heads * HEAD
    d = own.shape[1]
    side = arr((PAD, d), bf16)
    return call(
        functools.partial(attention_backward, chunk, heads),
        (info, own, other, w_out, proj, w_t, kept),
        [arr((2, PAD, 3 * width), bf16), arr((8, 3 * width), f32), arr((8, d), f32), side, side],
        name="attention_backward_%d" % chunk,
    )


def attention_grads(items, heads, info, counts, tail, *refs):
    width = heads * HEAD
    chunks = items // 2
    own, other, gproj, normed, ctx = (refs[i * chunks : (i + 1) * chunks] for i in range(5))
    send, keep, both = refs[5 * chunks :]
    first = is_first()
    rows = 3 * width
    total = jnp.zeros((rows, keep.shape[1]), f32)
    total_out = jnp.zeros((width, keep.shape[1]), f32)
    for k in range(chunks):
        for j in range(2):
            weight = item_weight(info, items, 2 * k + j, counts)
            total = total + dot((gproj[k][j].astype(f32) * weight).astype(bf16), normed[k][j], TN)
            a, b = (own, other) if j == 0 else (other, own)
            branch = jnp.where(first, a[k][...], b[k][...]).astype(f32)
            branch = (branch * weight).astype(bf16)
            total_out = total_out + dot(ctx[k][:, j * width : (j + 1) * width], branch, TN)
    half = 2 * width
    both[0] = total[:half].astype(bf16)
    both[1, 0 : rows - half] = total[half:].astype(bf16)
    both[1, rows - half :] = total_out.astype(bf16)
    one, _ = places(True)
    keep[...] = both[one]
    send[0:half] = both[1 - one]
    put_tail(send, half, tail[...])


def run_attention_grads(call, items, heads, info, counts, tail, own, other, gproj, normed, ctx):
    width = heads * HEAD
    d = own[0].shape[1]
    return call(
        functools.partial(attention_grads, items, heads),
        (info, counts, tail, *own, *other, *gproj, *normed, *ctx),
        [arr((2 * width + 2 * TAIL, d), bf16), arr((2 * width, d), bf16)],
        [VMEM((2, 2 * width, d), bf16)],
        name="attention_grads",
    )


def norm_one_back(items, info, counts, vecs, grad_mid, pair, far, *refs):
    chunks = items // 2
    kept, grad_own = refs[:chunks], refs[chunks]
    for k in range(chunks):
        x = jnp.where(is_first(), kept[k][0], kept[k][1]).astype(f32)
        unit, scale = unit_rows(x)
        grad = pair[k].astype(f32) + far[k].astype(f32)
        total = grad_mid[k] + norm_back(grad, unit, scale, vecs[0:1, :])
        grad_own[k] = (total * own_weight(info, items, k, counts)).astype(bf16)


def run_norm_one_back(call, items, info, counts, vecs, grad_mid, pair, far, kept):
    return call(
        functools.partial(norm_one_back, items),
        (info, counts, vecs, grad_mid, pair, far, *kept),
        [arr(pair.shape, bf16)],
        name="norm_one_back",
    )[0]


def output_rows(items, info, down_bias, pair, far, *refs):
    chunks = items // 2
    middles, out = refs[:chunks], refs[chunks]
    for k in range(chunks):
        bias = jnp.where(own_expert(info, items, k) == 0, down_bias[0:1, :], down_bias[1:2, :])
        out[k] = (middles[k][...] + (pair[k].astype(f32) + far[k].astype(f32)) + bias).astype(bf16)


def run_output_rows(call, items, info, down_bias, pair, far, middles):
    return call(
        functools.partial(output_rows, items),
        (info, down_bias, pair, far, *middles),
        [arr(pair.shape, bf16)],
        name="output_rows",
    )[0]


def assemble(items, own, other, out, buf, low, sem):
    first = is_first()
    for k in range(items // 2):
        for j in range(2):
            a, b = (own, other) if j == 0 else (other, own)
            buf[pl.ds((2 * k + j) * SEQ, PAD), :] = jnp.where(first, a[k], b[k]).astype(f32)
    low[...] = buf[0 : items * SEQ, :].astype(bf16)
    copy = pltpu.make_async_copy(low, out, sem)
    copy.start()
    copy.wait()


def run_assemble(call, items, own, other, name):
    d = own.shape[2]
    return call(
        functools.partial(assemble, items),
        (own, other),
        [arr((items * SEQ, d), bf16)],
        [VMEM((items * SEQ + 16, d), f32), VMEM((items * SEQ, d), bf16), DMA],
        out_specs=[hspec()],
        name=name,
    )[0]


def swap(value, axis, size, bit):
    return lax.ppermute(value, axis, [(i, i ^ bit) for i in range(size)])


def add_kernel(a, b, out):
    out[...] = (a[...].astype(f32) + b[...].astype(f32)).astype(out.dtype)


def run_add(call, a, b, name):
    return call(add_kernel, (a, b), [arr(a.shape, a.dtype)], name=name)[0]


def pair_kernel(chunks, *refs):
    own, got, out = refs[:chunks], refs[chunks : 2 * chunks], refs[2 * chunks]
    for k in range(chunks):
        out[k] = (own[k][...].astype(f32) + got[k][...].astype(f32)).astype(bf16)


def run_pair(call, own, got, name):
    return call(
        functools.partial(pair_kernel, len(own)), (*own, *got), [arr((len(own), *own[0].shape), bf16)], name=name
    )[0]


def split_rows(rows):
    high = rows.astype(bf16)
    return high, (rows - high.astype(f32)).astype(bf16)


def add_tail(held, got, at):
    return held[...] + got[at : at + TAIL].astype(f32) + got[at + TAIL : at + 2 * TAIL].astype(f32)


def put_tail(out, at, rows):
    out[at : at + TAIL], out[at + TAIL : at + 2 * TAIL] = split_rows(rows)


def attach_kernel(rows, tail, out):
    count = rows.shape[0]
    out[0:count] = rows[...]
    put_tail(out, count, tail[...])


def half_of(ref, index, count):
    return ref[pl.ds(pl.multiple_of(index * count, count), count), :]


def fold_step(turned, tailed, handed, keep, got, *refs):
    refs = list(refs)
    held = refs.pop(0) if tailed else None
    given = [refs.pop(0) for _ in range(handed)]
    send_next, keep_next = refs[:2]
    count = keep_next.shape[0]
    _, two = places(turned)
    for out, index in ((keep_next, two), (send_next, 1 - two)):
        total = half_of(keep, index, count).astype(f32) + half_of(got, index, count).astype(f32)
        out[0:count] = total.astype(bf16)
    if tailed:
        tail = add_tail(held, got, 2 * count)
        refs[2][...] = tail
        put_tail(send_next, count, tail)
    for a in given:
        piece = refs[-1].shape[0]
        refs[-2][...] = a[0:piece]
        refs[-1][...] = a[piece : 2 * piece]


def fold_two_step(turned, keep, got_low, got_high, send_next, keep_next):
    count = keep_next.shape[0]
    _, two = places(turned)
    for out, index in ((keep_next, two), (send_next, 1 - two)):
        got = jnp.where(index == 0, got_low[...], got_high[...]).astype(f32)
        out[...] = (half_of(keep, index, count).astype(f32) + got).astype(bf16)


def add_step(tailed, handed, sends, keep, got, *refs):
    refs = list(refs)
    held = refs.pop(0) if tailed else None
    given = [refs.pop(0) for _ in range(handed)]
    out = refs.pop(0)
    count = out.shape[0]
    total = (keep[...].astype(f32) + got[0:count].astype(f32)).astype(bf16)
    out[...] = total
    if tailed:
        tail = add_tail(held, got, count)
        refs.pop(0)[...] = tail
        if sends:
            send = refs.pop(0)
            send[0:count] = total
            put_tail(send, count, tail)
    if handed == 1:
        refs[0][...] = given[0][...]
    if handed == 2:
        attach_kernel(given[0], given[1], refs[0])


def join_kernel(turned, own, other, out):
    _, bit = places(turned)
    out[bit] = own[...]
    out[1 - bit] = other[...]


PIECES = 4


def whole_kernel(scaled, *refs):
    counts = refs[0] if scaled else None
    own, other, out, buf, sems = refs[1:] if scaled else refs
    bit, _ = places(True)
    rows = own.shape[0] // PIECES
    copies = []
    for side, ref in enumerate((own, other)):
        half = bit if side == 0 else 1 - bit
        weight = 1.0
        if scaled:
            first, second = row_weight(counts)
            weight = jnp.where(half == 0, first, second)
        for i in range(PIECES):
            at = pl.ds(i * rows, rows)
            buf[side, at] = ref[at].astype(f32) * weight
            copy = pltpu.make_async_copy(buf.at[side, at], out.at[half, at], sems.at[side, i])
            copy.start()
            copies.append(copy)
    for copy in copies:
        copy.wait()


def run_whole(call, counts, own, other, name, limit):
    scaled = counts is not None
    shape = (2, *own.shape)
    return call(
        functools.partial(whole_kernel, scaled),
        ((counts,) if scaled else ()) + (own, other),
        [arr(shape, f32)],
        [VMEM(shape, f32), DMA((2, PIECES))],
        out_specs=[hspec()],
        limit=limit,
        name=name,
    )[0]


def attention_whole_kernel(rows, own, other, grad_qkv, grad_out, low, buf, sems):
    bit, _ = places(True)
    half = own.shape[0]
    low[bit] = own[...]
    low[1 - bit] = other[...]
    copies = []
    spans = [(grad_qkv, 0, 0, half), (grad_qkv, 1, half, rows - half), (grad_out, 1, 0, 2 * half - rows)]
    start = [0, 0, rows - half]
    for i, (out, side, to, count) in enumerate(spans):
        at = pl.ds(start[i], count)
        buf[side, at] = low[side, at].astype(f32)
        copy = pltpu.make_async_copy(buf.at[side, at], out.at[pl.ds(to, count)], sems.at[i])
        copy.start()
        copies.append(copy)
    for copy in copies:
        copy.wait()


def run_attention_whole(call, rows, own, other, name):
    half, d = own.shape
    return call(
        functools.partial(attention_whole_kernel, rows),
        (own, other),
        [arr((rows, d), f32), arr((2 * half - rows, d), f32)],
        [VMEM((2, half, d), bf16), VMEM((2, half, d), f32), DMA((3,))],
        out_specs=[hspec(), hspec()],
        limit=60,
        name=name,
    )


class Sum:
    def __init__(self, call, dp, tp, name, turned, keep, tail=None):
        self.call, self.dp, self.tp, self.name, self.keep, self.tail = call, dp, tp, name, keep, tail
        self.turned = turned
        self.steps = ((1, 2), (2, 1), (4, 4)) if turned else ((1, 1), (2, 2), (4, 4))

    def start(self, send):
        if self.dp == 8 and isinstance(send, list):
            self.got = tuple(self.cross(piece, self.steps[0]) for piece in send)
            return
        send = jnp.concatenate(send) if isinstance(send, list) else send
        if self.dp == 8:
            self.got = self.cross(send, self.steps[0])
            return
        keep = self.keep
        send = send[: keep.shape[0]]
        low = (lax.axis_index("dp") % 2).astype(jnp.int32)
        high = (lax.axis_index("dp") // 2 % 2).astype(jnp.int32)
        one = jnp.where(lax.axis_index("tensor") % 2 == 0, low, high) if self.turned else low
        flat = jnp.where(one == 0, jnp.concatenate([keep, send]), jnp.concatenate([send, keep]))
        share = lax.psum_scatter(flat, "dp", scatter_dimension=0, tiled=True)
        whole = lax.all_gather(share, "dp", axis=0, tiled=True).reshape(2, *keep.shape)
        self.keep = jnp.where(one == 0, whole[0], whole[1])
        self.got = jnp.where(one == 0, whole[1], whole[0])
        if self.tail is not None:
            self.tail = lax.psum(self.tail, "dp")

    def cross(self, value, bits):
        dp, tp = self.dp, self.tp
        route = [(i * tp + t, (i ^ bits[t % 2]) * tp + t) for i in range(dp) for t in range(tp)]
        return lax.ppermute(value, ("dp", "tensor"), route)

    def quarter(self, *handed):
        if self.dp != 8:
            return jnp.split(handed[0], 2) if handed else None
        rows, d = self.keep.shape
        tailed = self.tail is not None
        ins = (self.keep, self.got) + ((self.tail,) if tailed else ()) + handed
        outs = [arr((rows // 2 + (2 * TAIL if tailed else 0), d), bf16), arr((rows // 2, d), bf16)]
        outs += [arr(self.tail.shape, f32)] if tailed else []
        outs += [arr((a.shape[0] // 2, a.shape[1]), a.dtype) for a in handed for _ in range(2)]
        if isinstance(self.got, tuple):
            send, self.keep = self.call(
                functools.partial(fold_two_step, self.turned), (self.keep, *self.got), outs, name=self.name + "_half"
            )
            self.got = self.cross(send, self.steps[1])
            return None
        send, self.keep, *rest = self.call(
            functools.partial(fold_step, self.turned, tailed, len(handed)), ins, outs, name=self.name + "_half"
        )
        self.tail = rest[0] if tailed else None
        self.got = self.cross(send, self.steps[1])
        return rest[-2:] if handed else None

    def add(self, name, sends, handed):
        tailed = self.tail is not None
        rows, d = self.keep.shape
        ins = (self.keep, self.got) + ((self.tail,) if tailed else ()) + handed
        outs = [arr((rows, d), bf16)]
        outs += [arr(self.tail.shape, f32)] if tailed else []
        outs += [arr((rows + 2 * TAIL, d), bf16)] if tailed and sends else []
        if handed:
            outs.append(arr((handed[0].shape[0] + 2 * TAIL * (len(handed) - 1), d), bf16))
        out = self.call(
            functools.partial(add_step, tailed, len(handed), sends), ins, outs, name=self.name + name
        )
        self.keep = out[0]
        if tailed:
            self.tail = out[1]
        return out[2] if tailed and sends else out[0], out[-1]

    def middle(self, *handed):
        if self.dp != 8:
            return handed[0] if handed else None
        send, given = self.add("_quarter", True, handed)
        self.got = self.cross(send, self.steps[2])
        return given

    def back_half(self):
        if self.dp != 8:
            return
        self.add("_sum", False, ())
        self.got = self.cross(self.keep, self.steps[1])

    def back_whole(self):
        if self.dp != 8:
            return
        rows, d = self.keep.shape
        out = self.call(functools.partial(join_kernel, self.turned), (self.keep, self.got), [arr((2, rows, d), bf16)], name=self.name + "_join")[0]
        self.keep = out.reshape(2 * rows, d)
        self.got = self.cross(self.keep, self.steps[0])


def collect(items, heads, info, counts, two, cots, exp, *refs):
    width = heads * HEAD
    chunks = items // 2
    attn, one, (out,) = refs[:chunks], refs[chunks : 2 * chunks], refs[2 * chunks :]
    out[...] = jnp.zeros_like(out)
    weights = [own_weight(info, items, k, counts) for k in range(chunks)]
    out[0:3, :] = sum(two[3 * k : 3 * k + 3, :] * weights[k] for k in range(chunks)) * 0.5
    each = [item_weight(info, items, i, counts) for i in range(items)]
    out[3:5, :] = sum(one[i // 2][2 * (i % 2) : 2 * (i % 2) + 2, :] * each[i] for i in range(items))
    out[8:10, :] = exp[0:2, :]
    out[10:12, :] = cots[0:2, :]
    out[12:13, 0 : 3 * width] = sum(attn[i // 2][i % 2 : i % 2 + 1, :] * each[i] for i in range(items))


def small_outputs(heads, counts, small, *outs):
    width = heads * HEAD
    d = small.shape[1]
    for i in range(5):
        outs[i][...] = small[i : i + 1, :].reshape(d)
    for i, weight in enumerate(row_weight(counts)):
        outs[5][i : i + 1, :] = small[8 + i : 9 + i, :] * weight
        outs[6][i : i + 1, :] = small[10 + i : 11 + i, :] * weight
    row = small[12:13, :]
    outs[7][0:1, :] = row[:, 0:width]
    outs[7][1:2, :] = row[:, 2 * width : 3 * width]


def run_small_outputs(call, heads, counts, small):
    d = small.shape[1]
    return call(
        functools.partial(small_outputs, heads),
        (counts, small),
        [arr((d,), f32)] * 5 + [arr((2, d), f32)] * 2 + [arr((2, heads * HEAD), f32)],
        name="small_outputs",
    )


def row_sum_kernel(small, got, out):
    out[0:8, :] = small[0:8, :] + got[0:8, :]
    out[8:, :] = small[8:, :]


def run_row_sum(call, small, got, name):
    return call(row_sum_kernel, (small, got), [arr(small.shape, f32)], name=name)[0]


def local(
    dp, tp,
    tokens, token_mask, expert_type, cotangent, ln1_gain, ln1_bias, w_qkv, qv_bias, w_out, out_bias,
    ln2_gain, ln2_bias, w_up, up_bias, w_down, down_bias,
):
    rows, d = tokens.shape
    items = rows // SEQ
    width = w_qkv.shape[2]
    heads = width // HEAD
    core_swap = lambda v: swap(v, "tensor", tp, 1)
    far_swap = lambda v: swap(v, "tensor", tp, 2)
    chunks = items // 2
    call = Order()
    w_t = w_qkv.transpose(1, 2, 0).reshape(3 * width, d)

    w_far = far_swap(w_out)
    c0, p, n, x, info, totals, vecs = run_front(
        call, items, heads, token_mask, expert_type, tokens, w_t, qv_bias,
        (ln1_gain, ln1_bias, out_bias, ln2_gain, ln2_bias),
    )
    ctx, proj, normed_one, kept, ctx_far, ctxs = [c0], [p], [n], [x], [far_swap(c0)], []
    for k in range(1, chunks):
        c0, p, n, x = run_attention_forward(call, k, heads, info, vecs, tokens, w_t, qv_bias)
        for group, value in zip((ctx, proj, normed_one, kept, ctx_far), (c0, p, n, x, far_swap(c0))):
            group.append(value)
    both = run_pack(call, ctx[0], ctx_far[0], "context_pack_0")
    ctxs.append((both, core_swap(both)))
    w_both = run_pack(call, w_out, w_far, "w_out_pack")
    w_got = core_swap(w_both)
    masked, small_c = run_mask_rows(call, items, info, cotangent)
    w_all = run_slots(call, w_both, w_got, "w_out_all")
    middle, normed_two, active, slopes = [], [], [], []
    for k in range(chunks):
        out = run_experts_up(call, k, items, heads, info, vecs, kept[k], ctxs[k], w_all, up_bias, w_up)
        for group, value in zip((middle, normed_two, active, slopes), out):
            group.append(value)
        if k + 1 < chunks:
            both = run_pack(call, ctx[k + 1], ctx_far[k + 1], "context_pack_%d" % (k + 1))
            ctxs.append((both, core_swap(both)))

    send, keep = run_expert_grads(call, items, info, active, [masked], "down_grads", (totals,))
    sum_down = Sum(call, dp, tp, "down", True, keep, totals)
    sum_down.start(send)
    part_own, part_other, down_own, down_other, small_e, *ghid = run_experts_back(
        call, items, info, masked, w_up, w_down, active, slopes
    )
    part_got = core_swap(part_other)
    down_got = core_swap(down_other)
    part = run_add(call, part_own, part_got, "part")
    part_far = far_swap(part)
    down = run_add(call, down_own, down_got, "expert_rows")
    down_far = far_swap(down)
    up_send, up_keep = run_expert_grads(call, items, info, normed_two, ghid, "up_grads")
    sum_up = Sum(call, dp, tp, "up", True, up_keep)
    up_send = sum_down.quarter(up_send)
    sum_up.start(up_send)
    *branch_own, grad_mid, small_n = run_norm_two_back(call, vecs, masked, part, part_far, middle)
    branch_other = [core_swap(b) for b in branch_own]
    sum_down.middle()
    gproj, small_a, small_o, one_own, one_got = [], [], [], [], []
    for k in range(chunks):
        g, sa, so, po, pt = run_attention_backward(
            call, k, heads, info, branch_own[k], branch_other[k], w_out, proj[k], w_t, kept[k]
        )
        for group, value in zip((gproj, small_a, small_o, one_own, one_got), (g, sa, so, po, core_swap(pt))):
            group.append(value)
        if k == 0 and False:
            sum_up.quarter()
    if True:
        sum_up.quarter()
    if False:
        sum_up.middle()
    sum_down.back_half()
    totals = sum_down.tail
    small = call(
        functools.partial(collect, items, heads),
        (info, totals, small_n, small_c, small_e, *small_a, *small_o),
        [arr((TAIL, d), f32)],
        name="collect",
    )[0]
    attn_send, keep = run_attention_grads(
        call, items, heads, info, totals, small, branch_own, branch_other, gproj, normed_one, ctx
    )
    sum_attn = Sum(call, dp, tp, "attn", True, keep, small)
    sum_attn.start(attn_send)
    one = run_pair(call, one_own, one_got, "one")
    one_far = far_swap(one)
    if True:
        sum_up.middle()
    sum_down.back_whole()
    sum_attn.quarter()
    grad_own = run_norm_one_back(call, items, info, totals, vecs, grad_mid, one, one_far, kept)
    grad_other = core_swap(grad_own)
    sum_up.back_half()
    sum_attn.middle()
    out_own = run_output_rows(call, items, info, down_bias, down, down_far, middle)
    out_other = core_swap(out_own)
    grad_tokens = run_assemble(call, items, grad_own, grad_other, "grad_tokens")
    sum_up.back_whole()
    output = run_assemble(call, items, out_own, out_other, "output")
    sum_attn.back_half()
    small = sum_attn.tail
    small = run_row_sum(call, small, core_swap(small), "norm_rows_core")
    small_far = far_swap(small)
    sum_attn.back_whole()
    small = run_row_sum(call, small, small_far, "norm_rows_far")
    smalls = run_small_outputs(call, heads, totals, small)
    grad_down = run_whole(call, totals, sum_down.keep, sum_down.got, "down_whole", 20)
    grad_up = run_whole(call, totals, sum_up.keep, sum_up.got, "up_whole", 60)
    grad_qkv, grad_out = run_attention_whole(call, 3 * width, sum_attn.keep, sum_attn.got, "attn_whole")
    return (
        output,
        grad_tokens,
        smalls[3],
        smalls[4],
        grad_qkv.reshape(3, width, d).transpose(2, 0, 1),
        smalls[7],
        grad_out,
        smalls[2],
        smalls[0],
        smalls[1],
        grad_up.reshape(w_up.shape),
        smalls[5],
        grad_down.reshape(w_down.shape),
        smalls[6],
        totals[:2, 0].astype(jnp.int32),
    )


def solution(mesh):
    in_specs = (
        P("dp", None),
        P("dp"),
        P("dp"),
        P("dp", None),
        P(),
        P(),
        P(None, None, "tensor"),
        P(None, "tensor"),
        P("tensor", None),
        P(),
        P(),
        P(),
        P(None, None, "tensor"),
        P(None, "tensor"),
        P(None, "tensor", None),
        P(),
    )
    out_specs = (
        P("dp", None),
        P("dp", None),
        P(),
        P(),
        P(None, None, "tensor"),
        P(None, "tensor"),
        P("tensor", None),
        P(),
        P(),
        P(),
        P(None, None, "tensor"),
        P(None, "tensor"),
        P(None, "tensor", None),
        P(),
        P(),
    )
    return jax.shard_map(
        functools.partial(local, mesh.shape["dp"], mesh.shape["tensor"]),
        mesh=mesh,
        in_specs=in_specs,
        out_specs=out_specs,
        check_vma=False,
    )
```
